32 devices in a mesh: dp: 8 (over z, y), seq: 4 (over x, core).
Axes of the slice: x: 2, y: 2, z: 4, core: 2. Of those that a mesh axis runs over, the one named last changes fastest.
Arguments:
- tokens: bfloat16 [8, 512, 1536], P('dp', 'seq'), may hold values from -6 to 6
- cotangent: bfloat16 [8, 512, 1536], P('dp', 'seq'), may hold values from -6 to 6
- timesteps: int32 [8], replicated, may hold values from 0 to 999
- grid_widths: int32 [8], P('dp'), may hold values from 16 to 64, as said below
- scan_path: int32 [8, 512], P('dp', 'seq'), may hold values from 0 to 511, as said below
- ada_weight: bfloat16 [1536, 4608], P(None, 'dp'), may hold values from -0.15625 to 0.15625
- ada_bias: float32 [4608], P('dp'), may hold values from -3 to 3
- edge: float32 [1536], replicated, may hold values from -5 to 5
- in_weight: bfloat16 [1536, 6144], replicated, may hold values from -0.15625 to 0.15625
- conv_weight: float32 [2, 4, 3072], replicated, may hold values from -3 to 3
- conv_bias: float32 [2, 3072], replicated, may hold values from -3 to 3
- xproj_weight: bfloat16 [2, 3072, 128], replicated, may hold values from -0.109375 to 0.109375
- dt_weight: bfloat16 [2, 96, 3072], replicated, may hold values from -0.625 to 0.625
- dt_bias: float32 [2, 3072], replicated, may hold values from -12 to -2
- a_log: float32 [2, 3072, 16], replicated, may hold values from 0 to 2.77
- skip: float32 [2, 3072], replicated, may hold values from 0.5 to 1.5
- out_weight: bfloat16 [3072, 1536], replicated, may hold values from -0.109375 to 0.109375
Outputs:
- result: bfloat16 [8, 512, 1536], P('dp', 'seq')
- grad_tokens: bfloat16 [8, 512, 1536], P('dp', 'seq')
- grad_ada_weight: float32 [1536, 4608], P(None, 'dp')
- grad_ada_bias: float32 [4608], P('dp')
- grad_edge: float32 [1536], replicated
- grad_in_weight: float32 [1536, 6144], P(('dp', 'seq'))
- grad_conv_weight: float32 [2, 4, 3072], replicated
- grad_conv_bias: float32 [2, 3072], replicated
- grad_xproj_weight: float32 [2, 3072, 128], replicated
- grad_dt_weight: float32 [2, 96, 3072], replicated
- grad_dt_bias: float32 [2, 3072], replicated
- grad_a_log: float32 [2, 3072, 16], replicated
- grad_skip: float32 [2, 3072], replicated
- grad_out_weight: float32 [3072, 1536], P(('dp', 'seq'))
The draws below stay inside these ranges and needn't reach their ends.
Inputs may be any that keep to these rules, and one draw needn't show every extreme that they name: `grid_widths`: each is one of 16, 32 and 64; each of the three occurs. `scan_path`: for each image a permutation of its 512 raster indices that visits the grid's rows in order, each row left to right or right to left.
All inputs are finite; a program needn't handle non-finite values.
Results may differ from the reference program's by a relative error of at most 0.012.
The reference program's roundings to bfloat16 on the way count: a program that leaves them out, or rounds other values in their place, can miss the bound.
Values may be sent and summed in bfloat16 or wider, within the bound.
A program may use at most 256 MiB of HBM per device.

```python
import math
from functools import partial
import jax
import jax.numpy as jnp
from jax import lax

D = 1536
INNER = 3072
STATE = 16
DT_RANK = 96
CONV = 4
LENGTH = 512
GRID = 32
BLOCK = 16
IMAGES = 8


def grid_shape(key):
    options = jnp.array([GRID // 2, GRID, GRID * 2], dtype=jnp.int32)
    return options[jax.random.permutation(key, IMAGES) % 3]


def draw_grid_widths(key, part):
    widths = grid_shape(key)
    return widths


def draw_scan_path(key, part):
    widths = grid_shape(key)
    key = jax.random.fold_in(key, 2)
    flips = jax.random.randint(key, (IMAGES, LENGTH), 0, 2)
    position = jnp.arange(LENGTH, dtype=jnp.int32)[None, :]
    row_ids = position // widths[:, None]
    column = position % widths[:, None]
    backward = jnp.take_along_axis(flips, row_ids, axis=1)
    return (row_ids * widths[:, None] + jnp.where(backward == 1, widths[:, None] - 1 - column, column)).astype(jnp.int32)


def draw_dt_bias(key, part):
    key = jax.random.fold_in(key, 3)
    lower = 0.0001
    upper = 0.1
    steps = jnp.exp(jax.random.uniform(key, (2, INNER), jnp.float32, math.log(lower), math.log(upper)))
    return steps + jnp.log(-jnp.expm1(-steps))


def place_ends(values, stream_key, smallest, largest):
    index_at = [jax.random.randint(jax.random.fold_in(stream_key, axis), (), 0, length) for axis, length in enumerate(values.shape)]
    longest = values.shape.index(max(values.shape))
    neighbour = index_at[:longest] + [(index_at[longest] + 1) % values.shape[longest]] + index_at[longest + 1:]
    return values.at[tuple(index_at)].set(smallest).at[tuple(neighbour)].set(largest)


def spiked(result, stream_key, source, target, blocks, factor):
    def block_of(dim):
        return (jnp.arange(result.shape[dim]) // (result.shape[dim] // blocks)).reshape((-1,) + (1,) * (result.ndim - 1 - dim))

    one_side = jax.random.permutation(stream_key, blocks)[block_of(target)]
    far = (block_of(target) + blocks // 2) % blocks
    return jnp.where((block_of(source) == one_side) | (block_of(source) == far), factor * result, result)


def block_scale(key, shape, split, low, largest):
    gain = 1.0
    for dim, parts in split:
        heights = jax.random.uniform(jax.random.fold_in(jax.random.fold_in(key, 6), dim), (parts,), jnp.float32, low / len(split), largest / len(split))
        gain = gain * jnp.repeat(jnp.exp(heights), shape[dim] // parts).reshape((-1,) + (1,) * (len(shape) - 1 - dim))
    return gain


def bell_draw(key, extent, deviation, most, cuts=(), kind=jnp.bfloat16):
    loudness = block_scale(key, extent, cuts, -0.22, 0.18) if cuts else 1.0
    drawn = jax.random.normal(key, extent, jnp.float32) * deviation * loudness
    return jnp.minimum(jnp.maximum(drawn, -most), most).astype(kind)


def gaussian_with(stream_key, extent, deviation, bound, shards, heavy, kind=jnp.bfloat16):
    values = deviation * jax.random.normal(stream_key, extent, jnp.float32)
    if shards:
        values = values * block_scale(stream_key, extent, shards, -0.22, 0.18)
    return jnp.clip(spiked(values, jax.random.fold_in(stream_key, 3), *heavy), -bound, bound).astype(kind)


def setup_inputs(seed: int = 0) -> dict:
    keys = jax.random.split(jax.random.key(seed), 18)
    tokens = bell_draw(keys[0], (IMAGES, LENGTH, D), 1.0, 6.0, ((0, 8), (1, 4)))
    cotangent = gaussian_with(keys[1], (IMAGES, LENGTH, D), 1.0, 6.0, ((0, 8), (1, 4)), (0, 2, 8, 2.0))
    timesteps = place_ends(jax.random.randint(keys[2], (IMAGES,), 0, 1000), jax.random.fold_in(keys[2], 1), 0, 999).astype(jnp.int32)
    grid_widths = draw_grid_widths(jax.random.fold_in(keys[17], 71), 0)
    scan_path = draw_scan_path(jax.random.fold_in(keys[17], 71), 0)
    ada_weight = bell_draw(keys[5], (D, 3 * D), D ** -0.5, 0.15625, ((1, 8),))
    ada_bias = bell_draw(keys[6], (3 * D,), 0.5, 3.0, ((0, 8),), jnp.float32)
    edge = bell_draw(keys[7], (D,), 1.0, 5.0, (), jnp.float32)
    in_weight = bell_draw(keys[8], (D, 2 * INNER), D ** -0.5, 0.15625)
    conv_weight = bell_draw(keys[9], (2, CONV, INNER), CONV ** -0.5, 3.0, (), jnp.float32)
    conv_bias = bell_draw(keys[10], (2, INNER), 0.5, 3.0, (), jnp.float32)
    xproj_weight = bell_draw(keys[11], (2, INNER, DT_RANK + 2 * STATE), INNER ** -0.5, 0.109375)
    dt_weight = bell_draw(keys[12], (2, DT_RANK, INNER), DT_RANK ** -0.5, 0.625)
    dt_bias = draw_dt_bias(jax.random.fold_in(keys[17], 71), 0)
    a_log = jnp.clip(jax.random.uniform(keys[14], (2, INNER, STATE), jnp.float32, 0.0, 2.77), 0.0, 2.77)
    skip = jnp.clip(1.0 + 0.1 * jax.random.normal(keys[15], (2, INNER), jnp.float32), 0.5, 1.5)
    out_weight = bell_draw(keys[16], (INNER, D), INNER ** -0.5, 0.109375)
    return {"tokens": tokens, "cotangent": cotangent, "timesteps": timesteps, "grid_widths": grid_widths, "scan_path": scan_path, "ada_weight": ada_weight, "ada_bias": ada_bias, "edge": edge, "in_weight": in_weight, "conv_weight": conv_weight, "conv_bias": conv_bias, "xproj_weight": xproj_weight, "dt_weight": dt_weight, "dt_bias": dt_bias, "a_log": a_log, "skip": skip, "out_weight": out_weight}


@jax.custom_vjp
def low(v):
    return lax.optimization_barrier(v.astype(jnp.bfloat16)).astype(jnp.float32)

@jax.custom_vjp
def low_back(v):
    return v

def low_keep(v):
    return (low(v), None)

def low_pass(kept, grad):
    return (grad,)

def back_keep(v):
    return (v, None)

def back_low(kept, grad):
    return (low(grad),)
low.defvjp(low_keep, low_pass)
low_back.defvjp(back_keep, back_low)
highest = lax.Precision.HIGHEST
epsilon = 1e-06

def time_embedding(step_ids, model_width):
    halfway = model_width // 2
    frequency = jnp.exp(-math.log(10000.0) * jnp.arange(halfway, dtype=jnp.float32) / halfway)
    angles = step_ids.astype(jnp.float32)[:, None] * frequency[None, :]
    return jnp.concatenate([jnp.cos(angles), jnp.sin(angles)], axis=1)

def token_step(decay, state, pieces):
    inputs_u, deltas, inflow, readout = pieces
    state = jnp.exp(deltas[:, :, None] * decay) * state + (deltas * inputs_u)[:, :, None] * inflow[:, None, :]
    return (state, lax.optimization_barrier(jnp.sum(state * readout[:, None, :], axis=2)))

def selective(inputs_u, deltas, inflow, readout, decay):
    groups = inputs_u.shape[0]
    length = inputs_u.shape[1]
    channels = inputs_u.shape[2]
    blocks = length // BLOCK

    def to_blocks(item):
        moved = jnp.swapaxes(item, 0, 1)
        return moved.reshape((blocks, BLOCK) + moved.shape[1:])

    @jax.checkpoint
    def block_step(state, pieces):
        return lax.scan(partial(token_step, decay), state, pieces)
    initial = jnp.zeros((groups, channels, decay.shape[1]), jnp.float32)
    final, outputs = lax.scan(block_step, initial, tuple((to_blocks(item) for item in (inputs_u, deltas, inflow, readout))))
    return jnp.swapaxes(outputs.reshape((length, groups, channels)), 0, 1)

def block_forward(tokens, cond, widths, path, params):
    ada_weight, ada_bias, edge, in_weight, conv_weight, conv_bias, xproj_weight, dt_weight, dt_bias, a_log, skip, out_weight = params
    modulation = jnp.dot(cond, ada_weight, precision=highest) + ada_bias
    shift_term = modulation[:, :D][:, None, :]
    scale_term = modulation[:, D:2 * D][:, None, :]
    gate_term = modulation[:, 2 * D:][:, None, :]
    centred = tokens - lax.optimization_barrier(jnp.mean(tokens, axis=2, keepdims=True))
    normed = centred * lax.rsqrt(lax.optimization_barrier(jnp.mean(centred * centred, axis=2, keepdims=True)) + epsilon)
    flags = (jnp.remainder(path, widths[:, None]) == widths[:, None] - 1).astype(jnp.float32)
    hidden = low(normed * (1.0 + scale_term) + shift_term + flags[:, :, None] * edge)
    mixed = low_back(jnp.einsum('gld,de->gle', hidden, in_weight, precision=highest))
    inner_x = low(mixed[:, :, :INNER])
    gate_z = mixed[:, :, INNER:]
    rim_width = CONV - 1
    padded = jnp.pad(inner_x, ((0, 0), (rim_width, rim_width), (0, 0)))
    combined = jnp.zeros_like(gate_z)
    for direction in range(2):
        if direction == 0:
            conv_sum = conv_bias[0] + sum((conv_weight[0, tap_index] * padded[:, tap_index:tap_index + LENGTH] for tap_index in range(CONV)))
        else:
            conv_sum = conv_bias[1] + sum((conv_weight[1, tap_index] * padded[:, 2 * rim_width - tap_index:2 * rim_width - tap_index + LENGTH] for tap_index in range(CONV)))
        activated = low(jax.nn.silu(conv_sum))
        if direction == 1:
            activated = jnp.flip(activated, axis=1)
        projected = low_back(jnp.einsum('gle,ek->glk', activated, xproj_weight[direction], precision=highest))
        dt_low = low(projected[:, :, :DT_RANK])
        inflow = projected[:, :, DT_RANK:DT_RANK + STATE]
        readout = projected[:, :, DT_RANK + STATE:]
        pre_act = low_back(jnp.einsum('glr,re->gle', dt_low, dt_weight[direction], precision=highest) + dt_bias[direction])
        deltas = jax.nn.softplus(pre_act)
        outputs = selective(activated, deltas, inflow, readout, -jnp.exp(a_log[direction])) + skip[direction] * activated
        if direction == 1:
            outputs = jnp.flip(outputs, axis=1)
        combined = combined + outputs
    gated = low(combined * jax.nn.silu(gate_z))
    branch = low_back(jnp.einsum('gle,ed->gld', gated, out_weight, precision=highest))
    return tokens + gate_term * branch

def reference(tokens, cotangent, timesteps, grid_widths, scan_path, ada_weight, ada_bias, edge, in_weight, conv_weight, conv_bias, xproj_weight, dt_weight, dt_bias, a_log, skip, out_weight):
    params = tuple((item.astype(jnp.float32) for item in (ada_weight, ada_bias, edge, in_weight, conv_weight, conv_bias, xproj_weight, dt_weight, dt_bias, a_log, skip, out_weight)))
    cond = low(jax.nn.silu(time_embedding(timesteps, D)))
    group_size = math.gcd(IMAGES, max(1, 4096 // LENGTH))
    group_count = IMAGES // group_size

    def grouped(item):
        return item.reshape((group_count, group_size) + item.shape[1:])

    def one_group(totals, pieces):
        block_tokens, block_cot, block_cond, block_widths, block_path = pieces

        def closure(inputs, weights):
            return block_forward(inputs, block_cond, block_widths, block_path, weights)
        output, pullback = jax.vjp(closure, block_tokens.astype(jnp.float32), params)
        grad_inputs, grad_weights = pullback(block_cot.astype(jnp.float32))
        totals = jax.tree.map(jnp.add, totals, grad_weights)
        return (totals, (output.astype(jnp.bfloat16), grad_inputs.astype(jnp.bfloat16)))
    zero_grads = jax.tree.map(jnp.zeros_like, params)
    grads, (outputs, grad_inputs) = lax.scan(one_group, zero_grads, tuple((grouped(item) for item in (tokens, cotangent, cond, grid_widths, scan_path))))
    outputs = outputs.reshape(tokens.shape)
    grad_inputs = grad_inputs.reshape(tokens.shape)
    return (outputs, grad_inputs, grads[0], grads[1], grads[2], grads[3], grads[4], grads[5], grads[6], grads[7], grads[8], grads[9], grads[10], grads[11])
```

```python
import functools
import math

import jax, jax.numpy as jnp
from jax import lax
from jax.sharding import PartitionSpec as P
from jax.experimental import pallas as pl
from jax.experimental.pallas import tpu as pltpu

STATE=16
LOG2E=1.4426950408889634
F32=jnp.float32
BF=jnp.bfloat16
epsilon = 1e-06
highest = lax.Precision.HIGHEST

def iota(shape, dim):
    return lax.broadcasted_iota(jnp.int32, shape, dim)

def dot(a,b):
    return lax.dot_general(a,b,(((1,),(0,)),((),())),preferred_element_type=F32)
def dot_nt(a,b):
    return lax.dot_general(a,b,(((1,),(1,)),((),())),preferred_element_type=F32)
def dot_tn(a,b):
    return lax.dot_general(a,b,(((0,),(0,)),((),())),preferred_element_type=F32)

def softplus(x):
    return jnp.maximum(x,0.0)+jnp.log1p(jnp.exp(-jnp.abs(x)))

def spread(proj, first, out_ref):
    tb = proj.shape[0]
    rows = tb*STATE
    rep = (iota((rows,tb),0)//STATE == iota((rows,tb),1)).astype(F32).astype(BF)
    hi = proj.astype(BF)
    lo = (proj-hi.astype(F32)).astype(BF)
    mask = (iota((rows,128),1)-first == lax.rem(iota((rows,128),0),STATE)).astype(F32)
    a = (dot(rep,hi)*mask).astype(BF)
    b = (dot(rep,lo)*mask).astype(BF)
    ones = jnp.ones((128,128),F32).astype(BF)
    out_ref[...] = dot(a,ones)+dot(b,ones)

def diag_of(proj_rows, first):
    u = proj_rows.shape[0]
    k = u*STATE
    e = (iota((128,k),0)-first == lax.rem(iota((128,k),1),STATE)).astype(F32).astype(BF)
    m = (iota((u,k),1)//STATE == iota((u,k),0)).astype(F32)
    return (dot(proj_rows.astype(BF), e)*m).astype(BF)

def fwd_kernel(rev, tb, U, proj_ref, act_ref, dtw_ref, dtb_ref, a2_ref, hall_ref, y_ref, h_sc, bb, dl, du, dlu, duu):
    C = act_ref.shape[1]
    @pl.when(pl.program_id(0)==0)
    def _():
        h_sc[...] = jnp.zeros_like(h_sc)
    proj = proj_ref[...]
    spread(proj, 96, bb)
    pre = dot(proj.astype(BF), dtw_ref[...]) + dtb_ref[...]
    delta = softplus(pre)
    dl[...] = delta
    du[...] = delta*act_ref[...].astype(F32)
    def group(k, _):
        g = (tb//U-1-k) if rev else k
        t0 = pl.multiple_of(g*U, U)
        dlu[...] = dl[pl.ds(t0,U),:]
        duu[...] = du[pl.ds(t0,U),:]
        hs = [[h_sc[pl.ds(8*s,8), pl.ds(128*c,128)] for s in range(2)] for c in range(C//128)]
        for i in range(U):
            loc = (U-1-i) if rev else i
            tt = t0 + loc
            r = pl.multiple_of(tt*STATE, STATE)
            b = [bb[pl.ds(r+8*s, 8), :] for s in range(2)]
            for c in range(C//128):
                col = pl.ds(128*c,128)
                d = dlu[pl.ds(loc,1), col]
                x = duu[pl.ds(loc,1), col]
                for s in range(2):
                    a = jnp.exp2(d*a2_ref[pl.ds(8*s,8), col])
                    hs[c][s] = a*hs[c][s] + x*b[s]
                hall_ref[pl.ds(r,STATE), col] = jnp.concatenate(hs[c],0).astype(BF)
        for c in range(C//128):
            for s in range(2):
                h_sc[pl.ds(8*s,8), pl.ds(128*c,128)] = hs[c][s]
        cd = diag_of(proj_ref[pl.ds(t0,U),:], 112)
        y_ref[pl.ds(t0,U),:] = dot(cd, hall_ref[pl.ds(pl.multiple_of(t0*STATE,U*STATE),U*STATE),:])
        return 0
    lax.fori_loop(0, tb//U, group, 0)

def scan_fwd(proj, act, dtw, dtb, a2, rev, tb=64, U=16):
    T, C = act.shape
    nb = T//tb
    blk = (lambda j: (nb-1-j,0)) if rev else (lambda j:(j,0))
    whole = lambda j:(0,0)
    return pl.pallas_call(
        functools.partial(fwd_kernel, rev, tb, U),
        grid=(nb,),
        in_specs=[pl.BlockSpec((tb,128),blk), pl.BlockSpec((tb,C),blk), pl.BlockSpec((128,C),whole), pl.BlockSpec((1,C),whole), pl.BlockSpec((STATE,C),whole)],
        out_specs=[pl.BlockSpec((tb*STATE,C),blk), pl.BlockSpec((tb,C),blk)],
        out_shape=[jax.ShapeDtypeStruct((T*STATE,C),BF), jax.ShapeDtypeStruct((T,C),F32)],
        scratch_shapes=[pltpu.VMEM((STATE,C),F32), pltpu.VMEM((tb*STATE,128),F32), pltpu.VMEM((tb,C),F32), pltpu.VMEM((tb,C),F32), pltpu.VMEM((U,C),F32), pltpu.VMEM((U,C),F32)],
        compiler_params=pltpu.CompilerParams(vmem_limit_bytes=48<<20),
        name="scan_fwd",
    )(proj, act, dtw, dtb, a2)

def fold(p):
    u,k = p.shape
    m = (iota((u,k),1)//STATE == iota((u,k),0)).astype(F32)
    p = p*m
    acc = p[:, :128]
    for j in range(1,k//128):
        acc = acc + p[:, 128*j:128*(j+1)]
    for sh in (64,32,16):
        acc = acc + pltpu.roll(acc, sh, 1)
    return acc

def bwd_kernel(rev, tb, U, proj_ref, act_ref, dy_ref, hall_ref, hprev_ref, dtw_ref, dtb_ref, a2_ref, an_ref, dpre_ref, dact_ref, dcoef_ref, dalog_ref, g_sc, cb, dl, gb, qb, dlu, dyu):
    C = act_ref.shape[1]
    n = pl.num_programs(0)
    j = pl.program_id(0)
    @pl.when(j==0)
    def _():
        g_sc[...] = jnp.zeros_like(g_sc)
        dalog_ref[...] = jnp.zeros_like(dalog_ref)
    proj = proj_ref[...]
    spread(proj, 112, cb)
    pre = dot(proj.astype(BF), dtw_ref[...]) + dtb_ref[...]
    dl[...] = softplus(pre)
    first = jnp.where(j==n-1, 0.0, 1.0)
    def group(k, _):
        g = k if rev else (tb//U-1-k)
        t0 = pl.multiple_of(g*U, U)
        dlu[...] = dl[pl.ds(t0,U),:]
        dyu[...] = dy_ref[pl.ds(t0,U),:]
        gs = [[g_sc[pl.ds(8*s,8), pl.ds(128*c,128)] for s in range(2)] for c in range(C//128)]
        for i in range(U):
            loc = i if rev else (U-1-i)
            tt = t0 + loc
            r = pl.multiple_of(tt*STATE, STATE)
            cc = [cb[pl.ds(r+8*s, 8), :] for s in range(2)]
            edge = (i==U-1)
            for c in range(C//128):
                col = pl.ds(128*c,128)
                d = dlu[pl.ds(loc,1), col]
                dy = dyu[pl.ds(loc,1), col]
                if not edge:
                    hp = hall_ref[pl.ds(pl.multiple_of((tt+1 if rev else tt-1)*STATE,STATE),STATE), col].astype(F32)
                else:
                    rr = (t0+U if rev else t0-1)
                    inside = (rr < tb) if rev else (rr >= 0)
                    rc = jnp.clip(rr,0,tb-1)
                    hin = hall_ref[pl.ds(pl.multiple_of(rc*STATE,STATE),STATE), col].astype(F32)
                    hout = hprev_ref[:, col].astype(F32)*first
                    hp = jnp.where(inside, hin, hout)
                gg=[]; qq=[]
                for s in range(2):
                    an = an_ref[pl.ds(8*s,8), col]
                    a = jnp.exp2(d*a2_ref[pl.ds(8*s,8), col])
                    gt = dy*cc[s] + gs[c][s]
                    car = a*gt
                    gs[c][s] = car
                    q = car*hp[8*s:8*s+8]
                    dalog_ref[pl.ds(8*s,8), col] += q*d
                    gg.append(gt); qq.append(q*an)
                gb[pl.ds(loc*STATE,STATE), col] = jnp.concatenate(gg,0).astype(BF)
                qb[pl.ds(loc*STATE,STATE), col] = jnp.concatenate(qq,0).astype(BF)
        for c in range(C//128):
            for s in range(2):
                g_sc[pl.ds(8*s,8), pl.ds(128*c,128)] = gs[c][s]
        rows = pl.ds(t0,U)
        bd = diag_of(proj_ref[rows,:], 96)
        ones = (iota((U,U*STATE),1)//STATE == iota((U,U*STATE),0)).astype(F32).astype(BF)
        gall = gb[...]
        S = dot(bd, gall)
        Q = dot(ones, qb[...])
        act = act_ref[rows,:].astype(F32)
        dd = dl[rows,:]
        dy = dy_ref[rows,:]
        sig = 1.0-jnp.exp(-dd)
        dpre_ref[rows,:] = ((Q + act*S)*sig).astype(BF)
        dact_ref[rows,:] = dd*S
        di = fold(dot_nt((dd*act).astype(BF), gall))
        hrows = hall_ref[pl.ds(pl.multiple_of(t0*STATE,U*STATE),U*STATE),:]
        dr = fold(dot_nt(dy.astype(BF), hrows))
        lane = iota((U,128),1)
        dcoef_ref[rows,:] = jnp.where(lane<96, 0.0, jnp.where(lane<112, di, dr))
        return 0
    lax.fori_loop(0, tb//U, group, 0)

def scan_bwd(proj, act, dy, hall, dtw, dtb, a2, an, rev, tb=64, U=16):
    T, C = act.shape
    nb = T//tb
    blk = (lambda j:(j,0)) if rev else (lambda j: (nb-1-j,0))
    hp = (lambda j: (jnp.minimum((j+1)*tb, T-1),0)) if rev else (lambda j: (jnp.maximum((nb-1-j)*tb-1,0),0))
    whole = lambda j:(0,0)
    return pl.pallas_call(
        functools.partial(bwd_kernel, rev, tb, U),
        grid=(nb,),
        in_specs=[pl.BlockSpec((tb,128),blk), pl.BlockSpec((tb,C),blk), pl.BlockSpec((tb,C),blk), pl.BlockSpec((tb*STATE,C),blk), pl.BlockSpec((STATE,C),hp), pl.BlockSpec((128,C),whole), pl.BlockSpec((1,C),whole), pl.BlockSpec((STATE,C),whole), pl.BlockSpec((STATE,C),whole)],
        out_specs=[pl.BlockSpec((tb,C),blk), pl.BlockSpec((tb,C),blk), pl.BlockSpec((tb,128),blk), pl.BlockSpec((STATE,C),whole)],
        out_shape=[jax.ShapeDtypeStruct((T,C),BF), jax.ShapeDtypeStruct((T,C),F32), jax.ShapeDtypeStruct((T,128),F32), jax.ShapeDtypeStruct((STATE,C),F32)],
        scratch_shapes=[pltpu.VMEM((STATE,C),F32), pltpu.VMEM((tb*STATE,128),F32), pltpu.VMEM((tb,C),F32), pltpu.VMEM((U*STATE,C),BF), pltpu.VMEM((U*STATE,C),BF), pltpu.VMEM((U,C),F32), pltpu.VMEM((U,C),F32)],
        compiler_params=pltpu.CompilerParams(vmem_limit_bytes=48<<20),
        name="scan_bwd",
    )(proj, act, dy, hall, hall, dtw, dtb, a2, an)


def time_embedding(step_ids, model_width):
    halfway = model_width // 2
    frequency = jnp.exp(-math.log(10000.0) * jnp.arange(halfway, dtype=jnp.float32) / halfway)
    angles = step_ids.astype(jnp.float32)[:, None] * frequency[None, :]
    return jnp.concatenate([jnp.cos(angles), jnp.sin(angles)], axis=1)


def silu_slope(values):
    sigma = jax.nn.sigmoid(values)
    return sigma * (1.0 + values * (1.0 - sigma))


def shards(
    tokens,
    cotangent,
    timesteps,
    grid_widths,
    scan_path,
    ada_weight,
    ada_bias,
    edge,
    in_weight,
    conv_weight,
    conv_bias,
    xproj_weight,
    dt_weight,
    dt_bias,
    a_log,
    skip,
    out_weight,
):
    seg_len, width = tokens.shape[1:]
    inner = in_weight.shape[1] // 2
    rank = dt_weight.shape[1]
    taps = conv_weight.shape[1]
    rim = taps - 1
    columns = ada_weight.shape[1]
    n_seq = lax.axis_size("seq")
    n_dp = lax.axis_size("dp")
    dp_index = lax.axis_index("dp")
    seq_index = lax.axis_index("seq")
    length = seg_len * n_seq
    chans = inner // n_seq

    def mine(weight, dim, first=0):
        return lax.dynamic_slice_in_dim(weight, first + seq_index * chans, chans, dim)

    embedded = jax.nn.silu(time_embedding(timesteps, width)).astype(BF)
    modulation_part = jnp.dot(embedded, ada_weight, preferred_element_type=F32) + ada_bias
    modulation_all = lax.all_gather(modulation_part, "dp", axis=1, tiled=True)
    modulation_own = lax.dynamic_slice_in_dim(modulation_all, dp_index, 1, 0)
    shift_term = modulation_own[:, :width]
    scale_term = modulation_own[:, width : 2 * width]
    gate_term = modulation_own[:, 2 * width :]

    both = lax.all_gather(jnp.concatenate([tokens, cotangent], 0), "seq", axis=1, tiled=True)
    path = lax.all_gather(scan_path[0], "seq", axis=0, tiled=True)

    def norm(values):
        values = values.astype(F32)
        centred = values - jnp.mean(values, axis=1, keepdims=True)
        inv_std = lax.rsqrt(jnp.mean(centred * centred, axis=1, keepdims=True) + epsilon)
        return centred * inv_std, inv_std

    def flags_of(item):
        return (jnp.remainder(item, grid_widths[0]) == grid_widths[0] - 1).astype(F32)[:, None]

    normed_all, _ = norm(both[0])
    hidden = (normed_all * (1.0 + scale_term) + shift_term + flags_of(path) * edge).astype(BF)
    grad_branch = (both[1].astype(F32) * gate_term).astype(BF)
    w_x, w_z = mine(in_weight, 1), mine(in_weight, 1, inner)
    w_out = mine(out_weight, 0)
    xin = jnp.dot(hidden, w_x, preferred_element_type=F32).astype(BF)
    gate_z = jnp.dot(hidden, w_z, preferred_element_type=F32)

    conv_w, conv_b = mine(conv_weight, 2), mine(conv_bias, 1)
    padded = jnp.pad(xin, ((rim, rim), (0, 0))).astype(F32)
    starts = [list(range(taps)), [2 * rim - tap for tap in range(taps)]]
    conv = [
        conv_b[d]
        + sum(conv_w[d, tap] * padded[starts[d][tap] : starts[d][tap] + length] for tap in range(taps))
        for d in range(2)
    ]
    act = [jax.nn.silu(item).astype(BF) for item in conv]
    xproj = mine(xproj_weight, 1)
    proj = lax.psum(
        jnp.stack([jnp.dot(act[d], xproj[d], preferred_element_type=F32) for d in range(2)]), "seq"
    )
    dtw = jnp.pad(mine(dt_weight, 2), ((0, 0), (0, 128 - rank), (0, 0)))
    dtb = mine(dt_bias, 1)
    decay = -jnp.exp(jnp.swapaxes(mine(a_log, 1), 1, 2))
    decay2 = decay * LOG2E
    skips = mine(skip, 1)

    silu_z = jax.nn.silu(gate_z)
    grad_gated = lax.dot_general(
        grad_branch, w_out, (((1,), (1,)), ((), ())), preferred_element_type=F32
    )
    dy = grad_gated * silu_z

    y_total = skips[0] * act[0].astype(F32) + skips[1] * act[1].astype(F32)
    states = []
    for d in range(2):
        held, y = scan_fwd(proj[d], act[d], dtw[d], dtb[d : d + 1], decay2[d], d == 1)
        states.append(held)
        y_total = y_total + y
    gated = (y_total * silu_z).astype(BF)
    grad_z = (grad_gated * y_total * silu_slope(gate_z)).astype(BF)
    branch = lax.psum_scatter(
        jnp.dot(gated, w_out, preferred_element_type=F32), "seq", scatter_dimension=0, tiled=True
    )
    tok_float = tokens[0].astype(F32)
    cot_float = cotangent[0].astype(F32)
    result = (tok_float + gate_term * branch).astype(BF)
    gate_grad = jnp.sum(cot_float * branch, axis=0)

    def summed_rows(left, right):
        whole = lax.dot_general(
            left, right, (((0,), (0,)), ((), ())), preferred_element_type=F32
        ).astype(BF)
        return lax.psum_scatter(whole, "dp", scatter_dimension=0, tiled=True)

    out_rows = summed_rows(gated, grad_branch)
    total = n_dp * n_seq
    out_grad = lax.ppermute(
        out_rows,
        ("dp", "seq"),
        [(d * n_seq + s, s * n_dp + d) for d in range(n_dp) for s in range(n_seq)],
    ).astype(F32)

    def in_rows(grad):
        rows = summed_rows(hidden, grad)
        rows = rows.reshape(n_seq, -1, chans)
        return lax.all_to_all(rows, "seq", 0, 0)

    in_z = in_rows(grad_z)

    partial = []
    kept = []
    for d in range(2):
        dpre, dact, dcoef, dalog = scan_bwd(
            proj[d], act[d], dy, states[d], dtw[d], dtb[d : d + 1], decay2[d], decay[d], d == 1
        )
        partial.append(
            lax.dot_general(dpre, dtw[d], (((1,), (1,)), ((), ())), preferred_element_type=F32)
            + dcoef
        )
        kept.append((dpre, dact, dalog * decay[d]))
    dproj = lax.psum(jnp.stack(partial), "seq").astype(BF)
    grad_conv, small, xproj_grads = [], [], []
    for d in range(2):
        dpre, dact, dalog = kept[d]
        act_f = act[d].astype(F32)
        dact = (
            lax.dot_general(dproj[d], xproj[d], (((1,), (1,)), ((), ())), preferred_element_type=F32)
            + dact
            + dy * skips[d]
        )
        dconv = dact * silu_slope(conv[d])
        grad_conv.append(dconv)
        xproj_grads.append(
            lax.dot_general(
                dproj[d], act[d], (((0,), (0,)), ((), ())), preferred_element_type=F32
            )
        )
        dtw_grad = lax.dot_general(
            proj[d].astype(BF), dpre, (((0,), (0,)), ((), ())), preferred_element_type=F32
        )[:rank]
        conv_rows = jnp.stack(
            [jnp.sum(dconv * padded[first : first + length], axis=0) for first in starts[d]]
        )
        vectors = jnp.stack(
            [
                jnp.sum(dconv, axis=0),
                jnp.sum(dpre.astype(F32), axis=0),
                jnp.sum(dy * act_f, axis=0),
            ]
        )
        small.append(jnp.concatenate([dtw_grad, dalog, conv_rows, vectors], axis=0))
    dxin = 0.0
    for d in range(2):
        for tap in range(taps):
            first = starts[d][tap]
            dxin = dxin + jnp.pad(
                conv_w[d, tap] * grad_conv[d], ((first, 2 * rim - first), (0, 0))
            )
    dxin = dxin[rim : rim + length].astype(BF)
    in_x = in_rows(dxin)
    in_grad = jnp.concatenate([in_x, in_z], axis=0)
    in_grad = jnp.swapaxes(in_grad, 0, 1).reshape(-1, 2 * inner).astype(F32)

    grad_hidden = lax.psum_scatter(
        lax.dot_general(dxin, w_x, (((1,), (1,)), ((), ())), preferred_element_type=F32)
        + lax.dot_general(grad_z, w_z, (((1,), (1,)), ((), ())), preferred_element_type=F32),
        "seq",
        scatter_dimension=0,
        tiled=True,
    )
    normed, inv_std = norm(tokens[0])
    edge_grad = jnp.sum(flags_of(scan_path[0]) * grad_hidden, axis=0)
    shift_grad = jnp.sum(grad_hidden, axis=0)
    scale_grad = jnp.sum(grad_hidden * normed, axis=0)
    grad_normed = grad_hidden * (1.0 + scale_term)
    grad_tok = cot_float + inv_std * (
        grad_normed
        - jnp.mean(grad_normed, axis=1, keepdims=True)
        - normed * jnp.mean(grad_normed * normed, axis=1, keepdims=True)
    )
    mod_row = jnp.concatenate([shift_grad, scale_grad, gate_grad])[None]
    mod_table = lax.dynamic_update_slice(
        jnp.zeros((timesteps.shape[0], mod_row.shape[1]), F32), mod_row, (dp_index, dp_index * 0)
    )
    mod_table, edge_grad = lax.psum((mod_table, edge_grad), ("dp", "seq"))
    mod_columns = lax.dynamic_slice_in_dim(mod_table, dp_index * columns, columns, 1)
    ada_b_grad = jnp.sum(mod_columns, axis=0)
    ada_w_grad = jnp.dot(embedded.astype(F32).T, mod_columns, precision=highest)

    rows = jnp.stack([jnp.concatenate([xproj_grads[d], small[d]], axis=0) for d in range(2)])
    rows = lax.psum(rows, "dp").astype(BF)
    rows = lax.all_gather(rows, "seq", axis=2, tiled=True).astype(F32)
    cuts = [128, 128 + rank, 128 + rank + STATE, 128 + rank + STATE + taps]
    xproj_grad = jnp.swapaxes(rows[:, : cuts[0]], 1, 2)
    dtw_grad = rows[:, cuts[0] : cuts[1]]
    alog_grad = jnp.swapaxes(rows[:, cuts[1] : cuts[2]], 1, 2)
    convw_grad = rows[:, cuts[2] : cuts[3]]
    last = cuts[3]
    return (
        result[None],
        grad_tok.astype(BF)[None],
        ada_w_grad,
        ada_b_grad,
        edge_grad,
        in_grad,
        convw_grad,
        rows[:, last],
        xproj_grad,
        dtw_grad,
        rows[:, last + 1],
        alog_grad,
        rows[:, last + 2],
        out_grad,
    )


def solution(mesh):
    in_specs = (
        P("dp", "seq", None),
        P("dp", "seq", None),
        P(),
        P("dp"),
        P("dp", "seq"),
        P(None, "dp"),
        P("dp"),
        P(),
        P(),
        P(),
        P(),
        P(),
        P(),
        P(),
        P(),
        P(),
        P(),
    )
    out_specs = (
        P("dp", "seq", None),
        P("dp", "seq", None),
        P(None, "dp"),
        P("dp"),
        P(),
        P(("dp", "seq"), None),
        P(),
        P(),
        P(),
        P(),
        P(),
        P(),
        P(),
        P(("dp", "seq"), None),
    )
    return jax.shard_map(shards, mesh=mesh, in_specs=in_specs, out_specs=out_specs, check_vma=False)
```

```python
import functools
import math

import jax, jax.numpy as jnp
from jax import lax
from jax.sharding import PartitionSpec as P
from jax.experimental import pallas as pl
from jax.experimental.pallas import tpu as pltpu

STATE=16
LOG2E=1.4426950408889634
F32=jnp.float32
BF=jnp.bfloat16
epsilon = 1e-06
highest = lax.Precision.HIGHEST

def iota(shape, dim):
    return lax.broadcasted_iota(jnp.int32, shape, dim)

def dot(a,b):
    return lax.dot_general(a,b,(((1,),(0,)),((),())),preferred_element_type=F32)
def dot_nt(a,b):
    return lax.dot_general(a,b,(((1,),(1,)),((),())),preferred_element_type=F32)
def dot_tn(a,b):
    return lax.dot_general(a,b,(((0,),(0,)),((),())),preferred_element_type=F32)

def softplus(x):
    return jnp.maximum(x,0.0)+jnp.log1p(jnp.exp(-jnp.abs(x)))

def spread(proj, first, out_ref):
    tb = proj.shape[0]
    rows = tb*STATE
    rep = (iota((rows,tb),0)//STATE == iota((rows,tb),1)).astype(F32).astype(BF)
    hi = proj.astype(BF)
    lo = (proj-hi.astype(F32)).astype(BF)
    mask = (iota((rows,128),1)-first == lax.rem(iota((rows,128),0),STATE)).astype(F32)
    a = (dot(rep,hi)*mask).astype(BF)
    b = (dot(rep,lo)*mask).astype(BF)
    ones = jnp.ones((128,128),F32).astype(BF)
    out_ref[...] = dot(a,ones)+dot(b,ones)

def diag_of(proj_rows, first):
    u = proj_rows.shape[0]
    k = u*STATE
    e = (iota((128,k),0)-first == lax.rem(iota((128,k),1),STATE)).astype(F32).astype(BF)
    m = (iota((u,k),1)//STATE == iota((u,k),0)).astype(F32)
    return (dot(proj_rows.astype(BF), e)*m).astype(BF)

def fwd_kernel(rev, tb, U, proj_ref, act_ref, dtw_ref, dtb_ref, a2_ref, hall_ref, y_ref, h_sc, bb, dl, du, dlu, duu):
    C = act_ref.shape[1]
    @pl.when(pl.program_id(0)==0)
    def _():
        h_sc[...] = jnp.zeros_like(h_sc)
    proj = proj_ref[...]
    spread(proj, 96, bb)
    pre = dot(proj.astype(BF), dtw_ref[...]) + dtb_ref[...]
    delta = softplus(pre)
    dl[...] = delta
    du[...] = delta*act_ref[...].astype(F32)
    def group(k, _):
        g = (tb//U-1-k) if rev else k
        t0 = pl.multiple_of(g*U, U)
        dlu[...] = dl[pl.ds(t0,U),:]
        duu[...] = du[pl.ds(t0,U),:]
        hs = [[h_sc[pl.ds(8*s,8), pl.ds(128*c,128)] for s in range(2)] for c in range(C//128)]
        for i in range(U):
            loc = (U-1-i) if rev else i
            tt = t0 + loc
            r = pl.multiple_of(tt*STATE, STATE)
            b = [bb[pl.ds(r+8*s, 8), :] for s in range(2)]
            for c in range(C//128):
                col = pl.ds(128*c,128)
                d = dlu[pl.ds(loc,1), col]
                x = duu[pl.ds(loc,1), col]
                for s in range(2):
                    a = jnp.exp2(d*a2_ref[pl.ds(8*s,8), col])
                    hs[c][s] = a*hs[c][s] + x*b[s]
                hall_ref[pl.ds(r,STATE), col] = jnp.concatenate(hs[c],0).astype(BF)
        for c in range(C//128):
            for s in range(2):
                h_sc[pl.ds(8*s,8), pl.ds(128*c,128)] = hs[c][s]
        cd = diag_of(proj_ref[pl.ds(t0,U),:], 112)
        y_ref[pl.ds(t0,U),:] = dot(cd, hall_ref[pl.ds(pl.multiple_of(t0*STATE,U*STATE),U*STATE),:])
        return 0
    lax.fori_loop(0, tb//U, group, 0)

def scan_fwd(proj, act, dtw, dtb, a2, rev, tb=64, U=16):
    T, C = act.shape
    nb = T//tb
    blk = (lambda j: (nb-1-j,0)) if rev else (lambda j:(j,0))
    whole = lambda j:(0,0)
    return pl.pallas_call(
        functools.partial(fwd_kernel, rev, tb, U),
        grid=(nb,),
        in_specs=[pl.BlockSpec((tb,128),blk), pl.BlockSpec((tb,C),blk), pl.BlockSpec((128,C),whole), pl.BlockSpec((1,C),whole), pl.BlockSpec((STATE,C),whole)],
        out_specs=[pl.BlockSpec((tb*STATE,C),blk), pl.BlockSpec((tb,C),blk)],
        out_shape=[jax.ShapeDtypeStruct((T*STATE,C),BF), jax.ShapeDtypeStruct((T,C),F32)],
        scratch_shapes=[pltpu.VMEM((STATE,C),F32), pltpu.VMEM((tb*STATE,128),F32), pltpu.VMEM((tb,C),F32), pltpu.VMEM((tb,C),F32), pltpu.VMEM((U,C),F32), pltpu.VMEM((U,C),F32)],
        compiler_params=pltpu.CompilerParams(vmem_limit_bytes=48<<20),
        cost_estimate=pl.CostEstimate(flops=int(T*STATE*C*30), bytes_accessed=60000000, transcendentals=T*STATE*C),
        name="scan_fwd",
    )(proj, act, dtw, dtb, a2)

def fold(p):
    u,k = p.shape
    m = (iota((u,k),1)//STATE == iota((u,k),0)).astype(F32)
    p = p*m
    acc = p[:, :128]
    for j in range(1,k//128):
        acc = acc + p[:, 128*j:128*(j+1)]
    for sh in (64,32,16):
        acc = acc + pltpu.roll(acc, sh, 1)
    return acc

def bwd_kernel(rev, tb, U, proj_ref, act_ref, dy_ref, hall_ref, hprev_ref, dtw_ref, dtb_ref, a2_ref, an_ref, dpre_ref, dact_ref, dcoef_ref, dalog_ref, g_sc, cb, dl, gb, qb, dlu, dyu):
    C = act_ref.shape[1]
    n = pl.num_programs(0)
    j = pl.program_id(0)
    @pl.when(j==0)
    def _():
        g_sc[...] = jnp.zeros_like(g_sc)
        dalog_ref[...] = jnp.zeros_like(dalog_ref)
    proj = proj_ref[...]
    spread(proj, 112, cb)
    pre = dot(proj.astype(BF), dtw_ref[...]) + dtb_ref[...]
    dl[...] = softplus(pre)
    first = jnp.where(j==n-1, 0.0, 1.0)
    def group(k, _):
        g = k if rev else (tb//U-1-k)
        t0 = pl.multiple_of(g*U, U)
        dlu[...] = dl[pl.ds(t0,U),:]
        dyu[...] = dy_ref[pl.ds(t0,U),:]
        gs = [[g_sc[pl.ds(8*s,8), pl.ds(128*c,128)] for s in range(2)] for c in range(C//128)]
        for i in range(U):
            loc = i if rev else (U-1-i)
            tt = t0 + loc
            r = pl.multiple_of(tt*STATE, STATE)
            cc = [cb[pl.ds(r+8*s, 8), :] for s in range(2)]
            edge = (i==U-1)
            for c in range(C//128):
                col = pl.ds(128*c,128)
                d = dlu[pl.ds(loc,1), col]
                dy = dyu[pl.ds(loc,1), col]
                if not edge:
                    hp = hall_ref[pl.ds(pl.multiple_of((tt+1 if rev else tt-1)*STATE,STATE),STATE), col].astype(F32)
                else:
                    rr = (t0+U if rev else t0-1)
                    inside = (rr < tb) if rev else (rr >= 0)
                    rc = jnp.clip(rr,0,tb-1)
                    hin = hall_ref[pl.ds(pl.multiple_of(rc*STATE,STATE),STATE), col].astype(F32)
                    hout = hprev_ref[:, col].astype(F32)*first
                    hp = jnp.where(inside, hin, hout)
                gg=[]; qq=[]
                for s in range(2):
                    an = an_ref[pl.ds(8*s,8), col]
                    a = jnp.exp2(d*a2_ref[pl.ds(8*s,8), col])
                    gt = dy*cc[s] + gs[c][s]
                    car = a*gt
                    gs[c][s] = car
                    q = car*hp[8*s:8*s+8]
                    dalog_ref[pl.ds(8*s,8), col] += q*d
                    gg.append(gt); qq.append(q*an)
                gb[pl.ds(loc*STATE,STATE), col] = jnp.concatenate(gg,0).astype(BF)
                qb[pl.ds(loc*STATE,STATE), col] = jnp.concatenate(qq,0).astype(BF)
        for c in range(C//128):
            for s in range(2):
                g_sc[pl.ds(8*s,8), pl.ds(128*c,128)] = gs[c][s]
        rows = pl.ds(t0,U)
        bd = diag_of(proj_ref[rows,:], 96)
        ones = (iota((U,U*STATE),1)//STATE == iota((U,U*STATE),0)).astype(F32).astype(BF)
        gall = gb[...]
        S = dot(bd, gall)
        Q = dot(ones, qb[...])
        act = act_ref[rows,:].astype(F32)
        dd = dl[rows,:]
        dy = dy_ref[rows,:]
        sig = 1.0-jnp.exp(-dd)
        dpre_ref[rows,:] = ((Q + act*S)*sig).astype(BF)
        dact_ref[rows,:] = dd*S
        di = fold(dot_nt((dd*act).astype(BF), gall))
        hrows = hall_ref[pl.ds(pl.multiple_of(t0*STATE,U*STATE),U*STATE),:]
        dr = fold(dot_nt(dy.astype(BF), hrows))
        lane = iota((U,128),1)
        dcoef_ref[rows,:] = jnp.where(lane<96, 0.0, jnp.where(lane<112, di, dr))
        return 0
    lax.fori_loop(0, tb//U, group, 0)

def scan_bwd(proj, act, dy, hall, dtw, dtb, a2, an, rev, tb=64, U=16):
    T, C = act.shape
    nb = T//tb
    blk = (lambda j:(j,0)) if rev else (lambda j: (nb-1-j,0))
    hp = (lambda j: (jnp.minimum((j+1)*tb, T-1),0)) if rev else (lambda j: (jnp.maximum((nb-1-j)*tb-1,0),0))
    whole = lambda j:(0,0)
    return pl.pallas_call(
        functools.partial(bwd_kernel, rev, tb, U),
        grid=(nb,),
        in_specs=[pl.BlockSpec((tb,128),blk), pl.BlockSpec((tb,C),blk), pl.BlockSpec((tb,C),blk), pl.BlockSpec((tb*STATE,C),blk), pl.BlockSpec((STATE,C),hp), pl.BlockSpec((128,C),whole), pl.BlockSpec((1,C),whole), pl.BlockSpec((STATE,C),whole), pl.BlockSpec((STATE,C),whole)],
        out_specs=[pl.BlockSpec((tb,C),blk), pl.BlockSpec((tb,C),blk), pl.BlockSpec((tb,128),blk), pl.BlockSpec((STATE,C),whole)],
        out_shape=[jax.ShapeDtypeStruct((T,C),BF), jax.ShapeDtypeStruct((T,C),F32), jax.ShapeDtypeStruct((T,128),F32), jax.ShapeDtypeStruct((STATE,C),F32)],
        scratch_shapes=[pltpu.VMEM((STATE,C),F32), pltpu.VMEM((tb*STATE,128),F32), pltpu.VMEM((tb,C),F32), pltpu.VMEM((U*STATE,C),BF), pltpu.VMEM((U*STATE,C),BF), pltpu.VMEM((U,C),F32), pltpu.VMEM((U,C),F32)],
        compiler_params=pltpu.CompilerParams(vmem_limit_bytes=48<<20),
        cost_estimate=pl.CostEstimate(flops=int(T*STATE*C*60), bytes_accessed=120000000, transcendentals=T*STATE*C),
        name="scan_bwd",
    )(proj, act, dy, hall, hall, dtw, dtb, a2, an)

MESH = pl.DeviceIdType.MESH
VMEM_SPEC = pl.BlockSpec(memory_space=pltpu.VMEM)


def sibling_of(s):
    return s + 1 - 2 * lax.rem(s, 2)


def across_of(s):
    return lax.rem(s + 2, 4)


def remote(src, dst, sems, slot, peer):
    return pltpu.make_async_remote_copy(
        src_ref=src,
        dst_ref=dst,
        send_sem=sems[0].at[slot],
        recv_sem=sems[1].at[slot],
        device_id=peer,
        device_id_type=MESH,
    )


def greet(peers):
    barrier = pltpu.get_barrier_semaphore()
    for peer in peers:
        pl.semaphore_signal(barrier, inc=1, device_id=peer, device_id_type=MESH)
    pl.semaphore_wait(barrier, len(peers))


def comm_params(collective_id, mib=48):
    return pltpu.CompilerParams(
        collective_id=collective_id, has_side_effects=True, vmem_limit_bytes=mib << 20
    )


def gather_kernel(n_dp, tok_ref, mod_ref, all_ref, row_ref, send, recv, msend, mrecv, lsem):
    d, s = lax.axis_index("dp"), lax.axis_index("seq")
    sib, far = sibling_of(s), across_of(s)
    others = [lax.rem(d + k, n_dp) for k in range(1, n_dp)]
    greet([{"seq": sib}, {"seq": far}] + [{"dp": other} for other in others])
    sems = (send, recv)
    to_far = remote(tok_ref, all_ref.at[s], sems, 0, {"seq": far})
    to_sib = remote(tok_ref, all_ref.at[s], sems, 1, {"seq": sib})
    own = pltpu.make_async_copy(tok_ref, all_ref.at[s], lsem.at[0])
    own_row = pltpu.make_async_copy(mod_ref.at[d], row_ref.at[d], lsem.at[1])
    to_far.start()
    rows = []
    for k, other in enumerate(others):
        copy = remote(mod_ref.at[other], row_ref.at[d], (msend, mrecv), k, {"dp": other})
        copy.start()
        rows.append(copy)
    to_sib.start()
    own.start()
    own_row.start()
    to_far.wait()
    forward = remote(all_ref.at[far], all_ref.at[far], sems, 2, {"seq": sib})
    forward.start()
    for copy in rows:
        copy.wait()
    own.wait()
    own_row.wait()
    to_sib.wait()
    forward.wait()


def gather_tokens(tokens, mod_rows):
    n_dp = mod_rows.shape[0]
    dma = pltpu.SemaphoreType.DMA
    return pl.pallas_call(
        functools.partial(gather_kernel, n_dp),
        out_shape=[
            jax.ShapeDtypeStruct((4,) + tokens.shape, tokens.dtype),
            jax.ShapeDtypeStruct(mod_rows.shape, mod_rows.dtype),
        ],
        in_specs=[VMEM_SPEC] * 2,
        out_specs=[VMEM_SPEC] * 2,
        scratch_shapes=[dma((3,)), dma((3,)), dma((n_dp,)), dma((n_dp,)), dma((2,))],
        compiler_params=comm_params(0),
        name="gather_tokens",
    )(tokens, mod_rows)


def reduce_kernel(x_ref, out_ref, from_sib, half, from_x, send, recv):
    s = lax.axis_index("seq")
    sib, far = sibling_of(s), across_of(s)
    c = lax.rem(s, 2)
    greet([{"seq": sib}, {"seq": far}])
    sems = (send, recv)
    first = remote(x_ref.at[1 - c], from_sib, sems, 0, {"seq": sib})
    first.start()
    first.wait()
    half[...] = x_ref[c] + from_sib[...]
    second = remote(half, from_x, sems, 1, {"seq": far})
    second.start()
    second.wait()
    out_ref[c] = half[...] + from_x[...]
    third = remote(out_ref.at[c], out_ref.at[c], sems, 2, {"seq": sib})
    third.start()
    third.wait()


def seq_reduce(x, collective_id):
    _, rows, width = x.shape
    dma = pltpu.SemaphoreType.DMA
    return pl.pallas_call(
        reduce_kernel,
        out_shape=jax.ShapeDtypeStruct(x.shape, F32),
        in_specs=[VMEM_SPEC],
        out_specs=VMEM_SPEC,
        scratch_shapes=[pltpu.VMEM((rows, width), F32)] * 3 + [dma((3,)), dma((3,))],
        compiler_params=comm_params(collective_id),
        name="seq_reduce",
    )(x)


class DpScatter:
    def __init__(self, x, got, acc, far, sems):
        self.x, self.got, self.acc, self.far = x, got, acc, far
        self.sems = sems
        d = lax.axis_index("dp")
        n = lax.axis_size("dp") // 2
        self.n = n
        self.y = lax.rem(d, 2)
        self.z = d // 2
        self.order = [lax.rem(self.z + k, n) for k in range(1, n + 1)]

    @staticmethod
    def scratch(n_dp, block):
        n = n_dp // 2
        dma = pltpu.SemaphoreType.DMA
        return [pltpu.VMEM((n,) + block, BF)] * 3 + [dma((4, n))]

    def near_copy(self, k):
        z = self.order[k]
        peer = 2 * self.z + 1 - self.y
        return pltpu.make_async_remote_copy(
            src_ref=self.x.at[2 * z + 1 - self.y],
            dst_ref=self.got.at[z],
            send_sem=self.sems.at[0, k],
            recv_sem=self.sems.at[1, k],
            device_id={"dp": peer},
            device_id_type=MESH,
        )

    def near_arrival(self, k):
        return self.near_copy(k)

    def far_copy(self, k):
        z = self.order[k]
        return pltpu.make_async_remote_copy(
            src_ref=self.acc.at[z],
            dst_ref=self.far.at[k],
            send_sem=self.sems.at[2, k],
            recv_sem=self.sems.at[3, k],
            device_id={"dp": 2 * z + self.y},
            device_id_type=MESH,
        )

    def start(self):
        for k in range(self.n):
            self.near_copy(k).start()

    def pair(self, k):
        z = self.order[k]
        self.near_copy(k).wait()
        self.acc[z] = (self.x[2 * z + self.y].astype(F32) + self.got[z].astype(F32)).astype(BF)
        if k < self.n - 1:
            self.far_copy(k).start()

    def finish(self):
        for k in range(self.n - 1):
            self.far_copy(k).wait()
        total = self.x[2 * self.z + self.y].astype(F32) + self.got[self.z].astype(F32)
        for k in range(self.n - 1):
            total = total + self.far[k].astype(F32)
        return total


class SeqScatter:
    def __init__(self, x, from_sib, to_x, from_x, sems):
        s = lax.axis_index("seq")
        self.s, self.far = s, across_of(s)
        sib = sibling_of(s)
        self.x, self.from_sib, self.to_x, self.from_x = x, from_sib, to_x, from_x
        pair = (sems.at[0], sems.at[1])
        self.first = remote(x.at[across_of(sib)], from_sib.at[0], pair, 0, {"seq": sib})
        self.second = remote(x.at[sib], from_sib.at[1], pair, 1, {"seq": sib})
        self.third = remote(to_x, from_x, pair, 2, {"seq": self.far})

    @staticmethod
    def scratch(rows, width):
        return [
            pltpu.VMEM((2, rows, width), BF),
            pltpu.VMEM((rows, width), BF),
            pltpu.VMEM((rows, width), BF),
            pltpu.SemaphoreType.DMA((2, 3)),
        ]

    def start(self):
        self.first.start()
        self.second.start()

    def cross(self):
        self.first.wait()
        self.to_x[...] = (self.x[self.far].astype(F32) + self.from_sib[0].astype(F32)).astype(BF)
        self.third.start()

    def finish(self):
        self.second.wait()
        self.third.wait()
        return (
            self.x[self.s].astype(F32) + self.from_sib[1].astype(F32) + self.from_x[...].astype(F32)
        )


class SeqSwap:
    def __init__(self, src, dst, sems):
        s = lax.axis_index("seq")
        self.s, self.src, self.dst = s, src, dst
        pair = (sems.at[0], sems.at[1])
        self.copies = [
            remote(src.at[lax.rem(s + k, 4)], dst.at[s], pair, k - 1, {"seq": lax.rem(s + k, 4)})
            for k in (2, 1, 3)
        ]

    def start(self):
        for copy in self.copies:
            copy.start()
        self.dst[self.s] = self.src[self.s]

    def finish(self):
        for copy in self.copies:
            copy.wait()


def dp_others():
    n = lax.axis_size("dp")
    d = lax.axis_index("dp")
    return [lax.rem(d + k, n) for k in range(1, n)]


def seq_others():
    s = lax.axis_index("seq")
    return [lax.rem(s + k, 4) for k in (1, 2, 3)]


def greet_all():
    greet([{"seq": other} for other in seq_others()] + [{"dp": other} for other in dp_others()])


def middle_kernel(*refs):
    branch_in, out_in, z_in, branch_ref, out_ref, z_ref = refs[:6]
    seq = SeqScatter(branch_in, *refs[6:10])
    outs = DpScatter(out_in, *refs[10:14])
    zs = DpScatter(z_in, *refs[14:18])
    red, swap_sems = refs[18:]
    swap = SeqSwap(red, z_ref, swap_sems)
    greet_all()
    seq.start()
    outs.start()
    seq.cross()
    zs.start()
    for k in range(outs.n):
        outs.pair(k)
    for k in range(zs.n):
        zs.pair(k)
    branch_ref[...] = seq.finish()
    out_ref[...] = outs.finish().astype(BF)
    red[...] = zs.finish().astype(BF)
    swap.start()
    swap.finish()


def middle_exchange(branch, out_part, z_part, collective_id):
    n_dp = out_part.shape[0]
    _, rows, width = branch.shape
    shapes = [
        jax.ShapeDtypeStruct((rows, width), F32),
        jax.ShapeDtypeStruct(out_part.shape[1:], BF),
        jax.ShapeDtypeStruct(z_part.shape[1:], BF),
    ]
    return pl.pallas_call(
        middle_kernel,
        out_shape=shapes,
        in_specs=[VMEM_SPEC] * 3,
        out_specs=[VMEM_SPEC] * 3,
        scratch_shapes=SeqScatter.scratch(rows, width)
        + DpScatter.scratch(n_dp, out_part.shape[1:])
        + DpScatter.scratch(n_dp, z_part.shape[1:])
        + [pltpu.VMEM(z_part.shape[1:], BF), pltpu.SemaphoreType.DMA((2, 3))],
        compiler_params=comm_params(collective_id),
        name="middle_exchange",
    )(branch, out_part, z_part)


def last_kernel(*refs):
    (hid_in, x_in, small_in, tok_ref, cot_ref, flag_ref, scale_ref, gate_ref) = refs[:8]
    x_ref, small_ref, tokg_ref, table_ref = refs[8:12]
    seq = SeqScatter(hid_in, *refs[12:16])
    xs = DpScatter(x_in, *refs[16:20])
    smalls = DpScatter(small_in, *refs[20:24])
    red, swap_sems, row, rows_in, row_sems, table_sems, spread_sems = refs[24:]
    swap = SeqSwap(red, x_ref, swap_sems)
    d, s = lax.axis_index("dp"), lax.axis_index("seq")
    sib, far = sibling_of(s), across_of(s)
    n = smalls.n
    y, z = smalls.y, smalls.z
    greet_all()
    seq.start()
    smalls.start()
    seq.cross()
    xs.start()
    for k in range(n):
        smalls.pair(k)
    for k in range(n):
        xs.pair(k)

    width = tok_ref.shape[1]
    grad = seq.finish()
    tokens = tok_ref[...].astype(F32)
    centred = tokens - jnp.mean(tokens, axis=1, keepdims=True)
    inv_std = lax.rsqrt(jnp.mean(centred * centred, axis=1, keepdims=True) + epsilon)
    normed = centred * inv_std
    grad_normed = grad * (1.0 + scale_ref[...])
    inner_product = jnp.mean(grad_normed * normed, axis=1, keepdims=True)
    tokg_ref[...] = (
        cot_ref[...].astype(F32)
        + inv_std * (grad_normed - jnp.mean(grad_normed, axis=1, keepdims=True) - normed * inner_product)
    ).astype(BF)
    row[:, :width] = jnp.sum(grad, axis=0, keepdims=True)
    row[:, width : 2 * width] = jnp.sum(grad * normed, axis=0, keepdims=True)
    row[:, 2 * width : 3 * width] = gate_ref[...]
    row[:, 3 * width :] = jnp.sum(grad * flag_ref[...], axis=0, keepdims=True)
    pair = (row_sems.at[0], row_sems.at[1])
    row_copies = [
        remote(row, rows_in.at[k], pair, k, {"seq": other}) for k, other in enumerate(seq_others())
    ]
    for copy in row_copies:
        copy.start()

    small_ref[s, y, z] = smalls.finish().astype(BF)
    block = small_ref.at[s, y, z]
    spread_pair = (spread_sems.at[0], spread_sems.at[1])
    along_z = [
        remote(block, block, spread_pair, k, {"dp": 2 * smalls.order[k] + y}) for k in range(n - 1)
    ]
    for copy in along_z:
        copy.start()

    for copy in row_copies:
        copy.wait()
    total = row[...] + rows_in[1] + (rows_in[0] + rows_in[2])
    table_ref[d] = total
    table_pair = (table_sems.at[0], table_sems.at[1])
    table_copies = [
        remote(table_ref.at[d], table_ref.at[d], table_pair, k, {"dp": other})
        for k, other in enumerate(dp_others())
    ]
    for copy in table_copies:
        copy.start()

    for copy in along_z:
        copy.wait()
    plane = small_ref.at[s, y]
    along_y = remote(plane, plane, spread_pair, n - 1, {"dp": 2 * z + 1 - y})
    along_y.start()

    red[...] = xs.finish().astype(BF)
    swap.start()

    along_y.wait()
    mine = small_ref.at[s]
    along_x = remote(mine, mine, spread_pair, n, {"seq": far})
    to_sib = remote(mine, mine, spread_pair, n + 1, {"seq": sib})
    along_x.start()
    to_sib.start()
    along_x.wait()
    others = small_ref.at[far]
    forward = remote(others, others, spread_pair, n + 2, {"seq": sib})
    forward.start()
    swap.finish()
    for copy in table_copies:
        copy.wait()
    to_sib.wait()
    forward.wait()


def last_exchange(hid, x_part, small, tokens, cot, flags, scale, gate, collective_id):
    n_dp = x_part.shape[0]
    n = n_dp // 2
    _, rows, width = hid.shape
    dma = pltpu.SemaphoreType.DMA
    shapes = [
        jax.ShapeDtypeStruct(x_part.shape[1:], BF),
        jax.ShapeDtypeStruct((4, 2, n) + small.shape[1:], BF),
        jax.ShapeDtypeStruct((rows, width), BF),
        jax.ShapeDtypeStruct((n_dp, 1, 4 * width), F32),
    ]
    return pl.pallas_call(
        last_kernel,
        out_shape=shapes,
        in_specs=[VMEM_SPEC] * 8,
        out_specs=[VMEM_SPEC] * 4,
        scratch_shapes=SeqScatter.scratch(rows, width)
        + DpScatter.scratch(n_dp, x_part.shape[1:])
        + DpScatter.scratch(n_dp, small.shape[1:])
        + [
            pltpu.VMEM(x_part.shape[1:], BF),
            dma((2, 3)),
            pltpu.VMEM((1, 4 * width), F32),
            pltpu.VMEM((3, 1, 4 * width), F32),
            dma((2, 3)),
            dma((2, n_dp)),
            dma((2, n + 3)),
        ],
        compiler_params=comm_params(collective_id),
        name="last_exchange",
    )(hid, x_part, small, tokens, cot, flags, scale, gate)

def time_embedding(step_ids, model_width):
    halfway = model_width // 2
    frequency = jnp.exp(-math.log(10000.0) * jnp.arange(halfway, dtype=jnp.float32) / halfway)
    angles = step_ids.astype(jnp.float32)[:, None] * frequency[None, :]
    return jnp.concatenate([jnp.cos(angles), jnp.sin(angles)], axis=1)


def silu_slope(values):
    sigma = jax.nn.sigmoid(values)
    return sigma * (1.0 + values * (1.0 - sigma))


def shards(
    tokens,
    cotangent,
    timesteps,
    grid_widths,
    scan_path,
    ada_weight,
    ada_bias,
    edge,
    in_weight,
    conv_weight,
    conv_bias,
    xproj_weight,
    dt_weight,
    dt_bias,
    a_log,
    skip,
    out_weight,
):
    seg_len, width = tokens.shape[1:]
    inner = in_weight.shape[1] // 2
    rank = dt_weight.shape[1]
    taps = conv_weight.shape[1]
    rim = taps - 1
    columns = ada_weight.shape[1]
    n_seq = lax.axis_size("seq")
    n_dp = lax.axis_size("dp")
    dp_index = lax.axis_index("dp")
    seq_index = lax.axis_index("seq")
    length = seg_len * n_seq
    chans = inner // n_seq

    def mine(weight, dim, first=0):
        return lax.dynamic_slice_in_dim(weight, first + seq_index * chans, chans, dim)

    embedded = jax.nn.silu(time_embedding(timesteps, width)).astype(BF)
    modulation_part = jnp.dot(embedded, ada_weight, preferred_element_type=F32) + ada_bias
    gathered, modulation_own = gather_tokens(tokens[0], modulation_part[:, None, :])
    tokens_all = gathered.reshape(length, width)
    modulation_own = modulation_own.reshape(1, -1)
    shift_term = modulation_own[:, :width]
    scale_term = modulation_own[:, width : 2 * width]
    gate_term = modulation_own[:, 2 * width :]

    cotangent_all = lax.all_gather(cotangent[0], "seq", axis=0, tiled=True)
    path = lax.all_gather(scan_path[0], "seq", axis=0, tiled=True)

    def norm(values):
        values = values.astype(F32)
        centred = values - jnp.mean(values, axis=1, keepdims=True)
        inv_std = lax.rsqrt(jnp.mean(centred * centred, axis=1, keepdims=True) + epsilon)
        return centred * inv_std, inv_std

    def flags_of(item):
        return (jnp.remainder(item, grid_widths[0]) == grid_widths[0] - 1).astype(F32)[:, None]

    normed_all, _ = norm(tokens_all)
    hidden = (normed_all * (1.0 + scale_term) + shift_term + flags_of(path) * edge).astype(BF)
    grad_branch = (cotangent_all.astype(F32) * gate_term).astype(BF)
    w_x, w_z = mine(in_weight, 1), mine(in_weight, 1, inner)
    w_out = mine(out_weight, 0)
    xin = jnp.dot(hidden, w_x, preferred_element_type=F32).astype(BF)
    gate_z = jnp.dot(hidden, w_z, preferred_element_type=F32)

    conv_w, conv_b = mine(conv_weight, 2), mine(conv_bias, 1)
    padded = jnp.pad(xin, ((rim, rim), (0, 0))).astype(F32)
    starts = [list(range(taps)), [2 * rim - tap for tap in range(taps)]]
    conv = [
        conv_b[d]
        + sum(conv_w[d, tap] * padded[starts[d][tap] : starts[d][tap] + length] for tap in range(taps))
        for d in range(2)
    ]
    act = [jax.nn.silu(item).astype(BF) for item in conv]
    xproj = mine(xproj_weight, 1)
    proj = seq_reduce(
        jnp.stack([jnp.dot(act[d], xproj[d], preferred_element_type=F32) for d in range(2)]), 1
    )
    dtw = jnp.pad(mine(dt_weight, 2), ((0, 0), (0, 128 - rank), (0, 0)))
    dtb = mine(dt_bias, 1)
    decay = -jnp.exp(jnp.swapaxes(mine(a_log, 1), 1, 2))
    decay2 = decay * LOG2E
    skips = mine(skip, 1)

    silu_z = jax.nn.silu(gate_z)
    grad_gated = lax.dot_general(
        grad_branch, w_out, (((1,), (1,)), ((), ())), preferred_element_type=F32
    )
    dy = grad_gated * silu_z

    y_total = skips[0] * act[0].astype(F32) + skips[1] * act[1].astype(F32)
    states = []
    for d in range(2):
        held, y = scan_fwd(proj[d], act[d], dtw[d], dtb[d : d + 1], decay2[d], d == 1)
        states.append(held)
        y_total = y_total + y
    gated = (y_total * silu_z).astype(BF)
    grad_z = (grad_gated * y_total * silu_slope(gate_z)).astype(BF)
    total = n_dp * n_seq

    def product(left, right):
        return lax.dot_general(
            left, right, (((0,), (0,)), ((), ())), preferred_element_type=F32
        ).astype(BF)

    def in_blocks(grad):
        return grad.reshape(n_dp, n_seq, width // total, chans)

    branch, out_rows, in_z = middle_exchange(
        jnp.dot(gated, w_out, preferred_element_type=F32).astype(BF).reshape(n_seq, seg_len, width),
        product(gated, grad_branch).reshape(n_dp, chans // n_dp, width),
        in_blocks(product(hidden, grad_z)),
        2,
    )
    out_grad = lax.ppermute(
        out_rows,
        ("dp", "seq"),
        [(d * n_seq + s, s * n_dp + d) for d in range(n_dp) for s in range(n_seq)],
    ).astype(F32)
    tok_float = tokens[0].astype(F32)
    cot_float = cotangent[0].astype(F32)
    result = (tok_float + gate_term * branch).astype(BF)
    gate_grad = jnp.sum(cot_float * branch, axis=0, keepdims=True)

    partial = []
    kept = []
    for d in range(2):
        dpre, dact, dcoef, dalog = scan_bwd(
            proj[d], act[d], dy, states[d], dtw[d], dtb[d : d + 1], decay2[d], decay[d], d == 1
        )
        partial.append(
            lax.dot_general(dpre, dtw[d], (((1,), (1,)), ((), ())), preferred_element_type=F32)
            + dcoef
        )
        kept.append((dpre, dact, dalog * decay[d]))
    dproj = seq_reduce(jnp.stack(partial), 3).astype(BF)
    grad_conv, small, xproj_grads = [], [], []
    for d in range(2):
        dpre, dact, dalog = kept[d]
        act_f = act[d].astype(F32)
        dact = (
            lax.dot_general(dproj[d], xproj[d], (((1,), (1,)), ((), ())), preferred_element_type=F32)
            + dact
            + dy * skips[d]
        )
        dconv = dact * silu_slope(conv[d])
        grad_conv.append(dconv)
        xproj_grads.append(
            lax.dot_general(
                dproj[d], act[d], (((0,), (0,)), ((), ())), preferred_element_type=F32
            )
        )
        dtw_grad = lax.dot_general(
            proj[d].astype(BF), dpre, (((0,), (0,)), ((), ())), preferred_element_type=F32
        )[:rank]
        conv_rows = jnp.stack(
            [jnp.sum(dconv * padded[first : first + length], axis=0) for first in starts[d]]
        )
        vectors = jnp.stack(
            [
                jnp.sum(dconv, axis=0),
                jnp.sum(dpre.astype(F32), axis=0),
                jnp.sum(dy * act_f, axis=0),
            ]
        )
        small.append(jnp.concatenate([dtw_grad, dalog, conv_rows, vectors], axis=0))
    dxin = 0.0
    for d in range(2):
        for tap in range(taps):
            first = starts[d][tap]
            dxin = dxin + jnp.pad(
                conv_w[d, tap] * grad_conv[d], ((first, 2 * rim - first), (0, 0))
            )
    dxin = dxin[rim : rim + length].astype(BF)
    grad_hidden = (
        lax.dot_general(dxin, w_x, (((1,), (1,)), ((), ())), preferred_element_type=F32)
        + lax.dot_general(grad_z, w_z, (((1,), (1,)), ((), ())), preferred_element_type=F32)
    ).astype(BF)
    rows = jnp.concatenate(
        [xproj_grads[0], small[0], xproj_grads[1], small[1]], axis=0
    )
    n_rows = rows.shape[0]
    rows = jnp.pad(rows.astype(BF), ((0, -n_rows % (16 * n_dp)), (0, 0)))
    in_x, rows, grad_tok, table = last_exchange(
        grad_hidden.reshape(n_seq, seg_len, width),
        in_blocks(product(hidden, dxin)),
        rows.reshape(n_dp, -1, chans),
        tokens[0],
        cotangent[0],
        flags_of(scan_path[0]),
        scale_term,
        gate_grad,
        4,
    )
    in_grad = jnp.concatenate([in_x, in_z], axis=0)
    in_grad = jnp.swapaxes(in_grad, 0, 1).reshape(-1, 2 * inner).astype(F32)
    table = table.reshape(n_dp, -1)
    edge_grad = jnp.sum(table[:, 3 * width :], axis=0)
    mod_columns = lax.dynamic_slice_in_dim(table[:, : 3 * width], dp_index * columns, columns, 1)
    ada_b_grad = jnp.sum(mod_columns, axis=0)
    ada_w_grad = jnp.dot(embedded.astype(F32).T, mod_columns, precision=highest)

    rows = jnp.transpose(rows, (2, 1, 3, 0, 4)).reshape(-1, inner)[:n_rows]
    rows = rows.reshape(2, -1, inner).astype(F32)
    cuts = [128, 128 + rank, 128 + rank + STATE, 128 + rank + STATE + taps]
    xproj_grad = jnp.swapaxes(rows[:, : cuts[0]], 1, 2)
    dtw_grad = rows[:, cuts[0] : cuts[1]]
    alog_grad = jnp.swapaxes(rows[:, cuts[1] : cuts[2]], 1, 2)
    convw_grad = rows[:, cuts[2] : cuts[3]]
    last = cuts[3]
    return (
        result[None],
        grad_tok[None],
        ada_w_grad,
        ada_b_grad,
        edge_grad,
        in_grad,
        convw_grad,
        rows[:, last],
        xproj_grad,
        dtw_grad,
        rows[:, last + 1],
        alog_grad,
        rows[:, last + 2],
        out_grad,
    )


def solution(mesh):
    in_specs = (
        P("dp", "seq", None),
        P("dp", "seq", None),
        P(),
        P("dp"),
        P("dp", "seq"),
        P(None, "dp"),
        P("dp"),
        P(),
        P(),
        P(),
        P(),
        P(),
        P(),
        P(),
        P(),
        P(),
        P(),
    )
    out_specs = (
        P("dp", "seq", None),
        P("dp", "seq", None),
        P(None, "dp"),
        P("dp"),
        P(),
        P(("dp", "seq"), None),
        P(),
        P(),
        P(),
        P(),
        P(),
        P(),
        P(),
        P(("dp", "seq"), None),
    )
    return jax.shard_map(shards, mesh=mesh, in_specs=in_specs, out_specs=out_specs, check_vma=False)
```

```python
import functools
import math

import jax
import jax.numpy as jnp
from jax import lax
from jax.experimental import pallas as pl
from jax.experimental.pallas import tpu as pltpu
from jax.sharding import PartitionSpec as P

STATE = 16
U = 16
TILE = 128
PARTS = 3
LOG2E = 1.4426950408889634
LN2 = 0.6931471805599453
F32 = jnp.float32
BF = jnp.bfloat16
epsilon = 1e-06
highest = lax.Precision.HIGHEST
MESH = pl.DeviceIdType.MESH
VMEM_SPEC = pl.BlockSpec(memory_space=pltpu.VMEM)


def iota(shape, dim):
    return lax.broadcasted_iota(jnp.int32, shape, dim)


def dot(a, b):
    return lax.dot_general(a, b, (((1,), (0,)), ((), ())), preferred_element_type=F32)


def dot_nt(a, b):
    return lax.dot_general(a, b, (((1,), (1,)), ((), ())), preferred_element_type=F32)


def dot_tn(a, b):
    return lax.dot_general(a, b, (((0,), (0,)), ((), ())), preferred_element_type=F32)


def softplus(x):
    return jnp.maximum(x, 0.0) + jnp.log1p(jnp.exp(-jnp.abs(x)))


def diag_of(rows, first):
    k = U * STATE
    pick = (iota((128, k), 0) - first == lax.rem(iota((128, k), 1), STATE)).astype(F32).astype(BF)
    keep = (iota((U, k), 1) // STATE == iota((U, k), 0)).astype(F32)
    return (dot(rows.astype(BF), pick) * keep).astype(BF)


def over_lanes(x, t):
    return jnp.broadcast_to(x[:, t : t + 1], (x.shape[0], 128))


def wide(x, n):
    return jnp.concatenate([x] * n, axis=1)


def lane_fold(x):
    acc = x[:, :128]
    for j in range(1, x.shape[1] // 128):
        acc = acc + x[:, 128 * j : 128 * (j + 1)]
    return acc


def interleave(steps, pieces):
    done = 0
    for i, step in enumerate(steps):
        step()
        while done < (i + 1) * len(pieces) // len(steps):
            pieces[done]()
            done += 1


def pipeline(groups, work, drain):
    interleave(work(0, 0), [])

    def two(p, carry):
        interleave(work(2 * p + 1, 1), drain(2 * p, 0))
        interleave(work(2 * p + 2, 0), drain(2 * p + 1, 1))
        return carry

    lax.fori_loop(0, groups // 2 - 1, two, 0)
    interleave(work(groups - 1, 1), drain(groups - 2, 0))
    interleave([lambda: None], drain(groups - 1, 1))


def forward_block(rev, dl, act, coef, a2, proj, dy, hp, put_y, dread, h_sc, hb_sc, slots, rows, red):
    length, chans = dl.shape
    groups = length // U
    part_width = chans // PARTS
    dlu, duu, dyu = rows
    dread[...] = jnp.zeros_like(dread)

    def place(k):
        return (groups - 1 - k) if rev else k

    def work(k, slot):
        g = place(k)
        t0 = pl.multiple_of(g * U, U)
        at = pl.ds(t0, U)
        dlu[...] = dl[at, :]
        duu[...] = dl[at, :] * act[at, :].astype(F32)
        dyu[...] = dy[at, :]
        inflow = coef[g][:STATE]
        spread = [over_lanes(inflow, t) for t in range(U)]
        hbuf = slots[slot]
        v = {}

        def token(part, i):
            col = pl.ds(part * part_width, part_width)
            if i == 0:
                v["a"], v["h"], v["hb"] = a2[:, col], h_sc[:, col], hb_sc[:, col]
            loc = (U - 1 - i) if rev else i
            one = pl.ds(loc, 1)
            h = jnp.exp2(dlu[one, col] * v["a"]) * v["h"] + duu[one, col] * wide(
                spread[loc], part_width // 128
            )
            hp[pl.ds(pl.multiple_of((t0 + loc) * STATE, STATE), STATE), col] = v["hb"]
            hb = h.astype(BF)
            hbuf[pl.ds(loc * STATE, STATE), col] = hb
            v["h"], v["hb"] = h, hb
            total = lane_fold(dyu[one, col] * h)
            if part:
                total = red[loc] + total
            if part < PARTS - 1:
                red[loc] = total
            else:
                here = iota((STATE, TILE), 1) == g * U + loc
                v["sum"] = jnp.where(here, jnp.sum(total, axis=1, keepdims=True), v.get("sum", 0.0))
                if i == U - 1:
                    dread[...] += v["sum"]
            if i == U - 1:
                h_sc[:, col] = h
                hb_sc[:, col] = hb

        return [functools.partial(token, part, i) for part in range(PARTS) for i in range(U)]

    def drain(k, slot):
        at = pl.ds(pl.multiple_of(place(k) * U, U), U)
        hbuf = slots[slot]
        v = {}

        def first():
            v["c"] = diag_of(proj[at, :], 128 - STATE)

        def out(c):
            col = pl.ds(256 * c, 256)
            put_y(at, col, dot(v["c"], hbuf[:, col]))

        return [first] + [functools.partial(out, c) for c in range(chans // 256)]

    pipeline(groups, work, drain)


def backward_block(
    rev, dl, act, coef, a2, proj, dy, skip, hp, dpre, dact, dflow, dalog, sums, g_sc, slots, rows, red
):
    length, chans = dl.shape
    groups = length // U
    part_width = chans // PARTS
    dlu, duu, dyu = rows
    dflow[...] = jnp.zeros_like(dflow)

    def place(k):
        return k if rev else (groups - 1 - k)

    def work(k, slot):
        g = place(k)
        t0 = pl.multiple_of(g * U, U)
        at = pl.ds(t0, U)
        dlu[...] = dl[at, :]
        duu[...] = dl[at, :] * act[at, :].astype(F32)
        dyu[...] = dy[at, :]
        readout = coef[g][STATE:]
        spread = [over_lanes(readout, t) for t in range(U)]
        gbuf, qbuf = slots[slot]
        v = {}

        def token(part, i):
            col = pl.ds(part * part_width, part_width)
            if i == 0:
                v["a"], v["car"], v["acc"] = a2[:, col], g_sc[:, col], dalog[:, col]
            loc = i if rev else (U - 1 - i)
            one = pl.ds(loc, 1)
            step = dlu[one, col]
            g_t = dyu[one, col] * wide(spread[loc], part_width // 128) + v["car"]
            car = jnp.exp2(step * v["a"]) * g_t
            before = hp[pl.ds(pl.multiple_of((t0 + loc) * STATE, STATE), STATE), col].astype(F32)
            q = car * before
            v["acc"] = v["acc"] + q * step
            v["car"] = car
            gbuf[pl.ds(loc * STATE, STATE), col] = g_t.astype(BF)
            total = lane_fold(duu[one, col] * g_t)
            if part:
                total = red[loc] + total
            if part < PARTS - 1:
                red[loc] = total
            else:
                here = iota((STATE, TILE), 1) == g * U + loc
                v["sum"] = jnp.where(here, jnp.sum(total, axis=1, keepdims=True), v.get("sum", 0.0))
                if i == U - 1:
                    dflow[...] += v["sum"]
            qa = q * v["a"]
            qa = qa[:8] + qa[8:]
            if i % 2 == 0:
                v["held"] = qa
            else:
                pair = [v["held"], qa] if rev else [qa, v["held"]]
                qbuf[pl.ds((loc // 2) * STATE, STATE), col] = jnp.concatenate(pair, 0).astype(BF)
            if i == U - 1:
                g_sc[:, col] = v["car"]
                dalog[:, col] = v["acc"]

        return [functools.partial(token, part, i) for part in range(PARTS) for i in range(U)]

    def drain(k, slot):
        at = pl.ds(pl.multiple_of(place(k) * U, U), U)
        gbuf, qbuf = slots[slot]
        v = {}

        def first():
            v["b"] = diag_of(proj[at, :], 128 - 2 * STATE)
            v["ones"] = (iota((U, U * 8), 1) // 8 == iota((U, U * 8), 0)).astype(F32).astype(BF)

        def cols(c):
            col = pl.ds(256 * c, 256)
            s = dot(v["b"], gbuf[:, col])
            q = dot(v["ones"], qbuf[:, col]) * LN2
            a = act[at, col].astype(F32)
            step = dl[at, col]
            grad = dy[at, col]
            pre = ((q + a * s) * (1.0 - jnp.exp(-step))).astype(BF)
            dpre[at, col] = pre
            dact[at, col] = step * s + skip[:, col] * grad
            sums[0, :, col] += pre.astype(F32)
            sums[1, :, col] += grad * a

        return [first] + [functools.partial(cols, c) for c in range(chans // 256)]

    pipeline(groups, work, drain)


def forward_kernel(
    proj, act, coef, dtw, dtb, a2, skip, dy, silu_z, slope_z, hidden, grad_branch, w_out,
    hp, dl, dread, branch, out_part, z_part, grad_z,
    y, h_sc, hb_sc, h_a, h_b, r0, r1, r2, red, gated,
):
    j = pl.program_id(0)
    blocks = pl.num_programs(0) // 2
    length, chans = dl.shape[1:]

    @pl.when(lax.rem(j, blocks) == 0)
    def _():
        h_sc[...] = jnp.zeros_like(h_sc)
        hb_sc[...] = jnp.zeros_like(hb_sc)

    pre = dot(proj[0].astype(BF), dtw[0]) + dtb[0]
    dl[0] = softplus(pre)

    def run(rev):
        base = (2 * blocks - 1 - j if rev else j) * length
        dy_block = dy.at[pl.ds(pl.multiple_of(base, length), length)]

        def put_y(at, col, value):
            value = value + skip[0, :, col] * act[0, at, col].astype(F32)
            rows = pl.ds(pl.multiple_of(base + at.start, U), U)
            if rev:
                value = value + y[rows, col]
            y[rows, col] = value

        forward_block(
            rev, dl.at[0], act.at[0], coef.at[0], a2.at[0], proj.at[0], dy_block, hp.at[0], put_y,
            dread.at[0, 0], h_sc, hb_sc, (h_a, h_b), (r0, r1, r2), red,
        )

    pl.when(j < blocks)(lambda: run(False))
    pl.when(j >= blocks)(lambda: run(True))

    @pl.when(j == 2 * blocks - 1)
    def _():
        total = y.shape[0]

        def rows_of(c, carry):
            at = pl.ds(pl.multiple_of(c * 64, 64), 64)
            value = y[at, :]
            gated[at, :] = (value * silu_z[at, :]).astype(BF)
            grad_z[at, :] = (value * slope_z[at, :]).astype(BF)
            return carry

        lax.fori_loop(0, total // 64, rows_of, 0)
        width = w_out.shape[1]

        def out_rows(c, carry):
            at = pl.ds(pl.multiple_of(c * 128, 128), 128)
            branch[at, :] = dot(gated[at, :], w_out[...]).astype(BF)
            return carry

        lax.fori_loop(0, total // 128, out_rows, 0)

        def out_cols(c, carry):
            at = pl.ds(pl.multiple_of(c * 128, 128), 128)
            out_part[at, :] = dot_tn(gated[:, at], grad_branch[...]).astype(BF)
            return carry

        lax.fori_loop(0, chans // 128, out_cols, 0)

        def z_cols(c, carry):
            at = pl.ds(pl.multiple_of(c * 128, 128), 128)
            z_part[at, :] = dot_tn(hidden[:, at], grad_z[...]).astype(BF)
            return carry

        lax.fori_loop(0, width // 128, z_cols, 0)


def scan_forward(proj, act, coef, dtw, dtb, a2, skip, dy, silu_z, slope_z, hidden, grad_branch, w_out):
    total, chans = dy.shape
    width = w_out.shape[1]
    blocks = total // TILE

    def place(j):
        d = j // blocks
        b = lax.rem(j, blocks)
        return d, b + d * (blocks - 1 - 2 * b)

    def tokens_of(j):
        d, b = place(j)
        return d, b, 0

    def direction_of(j):
        return j // blocks, 0, 0

    def cells(j):
        d, b = place(j)
        return d, b, 0, 0

    whole = VMEM_SPEC
    in_specs = [
        pl.BlockSpec((1, TILE, 128), tokens_of),
        pl.BlockSpec((1, TILE, chans), tokens_of),
        pl.BlockSpec((1, TILE // U, 2 * STATE, U), cells),
        pl.BlockSpec((1, 128, chans), direction_of),
        pl.BlockSpec((1, 1, chans), direction_of),
        pl.BlockSpec((1, STATE, chans), direction_of),
        pl.BlockSpec((1, 1, chans), direction_of),
    ] + [whole] * 6
    out_specs = [
        pl.BlockSpec((1, TILE * STATE, chans), tokens_of),
        pl.BlockSpec((1, TILE, chans), tokens_of),
        pl.BlockSpec((1, 1, STATE, TILE), cells),
    ] + [whole] * 4
    out_shape = [
        jax.ShapeDtypeStruct((2, total * STATE, chans), BF),
        jax.ShapeDtypeStruct((2, total, chans), F32),
        jax.ShapeDtypeStruct((2, blocks, STATE, TILE), F32),
        jax.ShapeDtypeStruct((total, width), BF),
        jax.ShapeDtypeStruct((chans, width), BF),
        jax.ShapeDtypeStruct((width, chans), BF),
        jax.ShapeDtypeStruct((total, chans), BF),
    ]
    return pl.pallas_call(
        forward_kernel,
        grid=(2 * blocks,),
        in_specs=in_specs,
        out_specs=out_specs,
        out_shape=out_shape,
        scratch_shapes=[
            pltpu.VMEM((total, chans), F32),
            pltpu.VMEM((STATE, chans), F32),
            pltpu.VMEM((STATE, chans), BF),
            pltpu.VMEM((U * STATE, chans), BF),
            pltpu.VMEM((U * STATE, chans), BF),
        ]
        + [pltpu.VMEM((U, chans), F32)] * 3
        + [pltpu.VMEM((U, STATE, 128), F32), pltpu.VMEM((total, chans), BF)],
        compiler_params=pltpu.CompilerParams(vmem_limit_bytes=60 << 20),
        name="scan_forward",
    )(proj, act, coef, dtw, dtb, a2, skip, dy, silu_z, slope_z, hidden, grad_branch, w_out)


def pre_kernel(
    s_ref, tok, cot, mod, flags, edge, w_x, w_z, w_out, conv_w, conv_b, xproj,
    hidden, grad_branch, xin, dy, silu_z, slope_z, act, slope, part, pad,
):
    j = pl.program_id(0)
    rows, width = tok.shape
    total, chans = xin.shape
    at = pl.ds(pl.multiple_of(j * rows, rows), rows)
    shift, scale, gate = (mod[:, k * width : (k + 1) * width] for k in range(3))
    tokens = tok[...].astype(F32)
    centred = tokens - jnp.mean(tokens, axis=1, keepdims=True)
    normed = centred * lax.rsqrt(jnp.mean(centred * centred, axis=1, keepdims=True) + epsilon)
    hid = (normed * (1.0 + scale) + shift + flags[...] * edge[...]).astype(BF)
    hidden[...] = hid
    grad = (cot[...].astype(F32) * gate).astype(BF)
    grad_branch[...] = grad
    xin[at, :] = dot(hid, w_x[...]).astype(BF)
    z = dot(hid, w_z[...])
    sigma = jax.nn.sigmoid(z)
    grad_gated = dot_nt(grad, w_out[...])
    silu_z[...] = z * sigma
    dy[...] = grad_gated * (z * sigma)
    slope_z[...] = grad_gated * (sigma * (1.0 + z * (1.0 - sigma)))

    @pl.when(j == pl.num_programs(0) - 1)
    def _():
        pad[:16, :] = jnp.zeros((16, chans), F32)
        pad[total + 16 :, :] = jnp.zeros((16, chans), F32)
        pad[16 : total + 16, :] = xin[...].astype(F32)
        step = 64

        def chunk(c, carry):
            base = pl.multiple_of(c * step, step)
            window = pad[pl.ds(base, step + 32), :]
            here = pl.ds(base, step)
            for d in range(2):
                value = conv_b[d : d + 1, :]
                for tap in range(4):
                    first = 13 + tap if d == 0 else 19 - tap
                    value = value + conv_w[d, tap : tap + 1, :] * window[first : first + step]
                sig = jax.nn.sigmoid(value)
                acted = (value * sig).astype(BF)
                act[d, here, :] = acted
                slope[d, here, :] = sig * (1.0 + value * (1.0 - sig))
                part[d, here, :] = dot(acted, xproj[d])
            return carry

        lax.fori_loop(0, total // step, chunk, 0)


def prepare(seq_index, tok, cot, mod, flags, edge, in_weight, out_weight, conv_w, conv_b, xproj):
    total, width = tok.shape
    inner = out_weight.shape[0]
    chans = inner // 4
    rows = 128

    def by_rows(j, s):
        return j, 0

    def fixed(j, s):
        return 0, 0

    token_rows = pl.BlockSpec((rows, width), by_rows)
    channel_rows = pl.BlockSpec((rows, chans), by_rows)
    in_specs = [
        token_rows,
        token_rows,
        pl.BlockSpec((1, 3 * width), fixed),
        pl.BlockSpec((rows, 1), by_rows),
        pl.BlockSpec((1, width), fixed),
        pl.BlockSpec((width, chans), lambda j, s: (0, s[0])),
        pl.BlockSpec((width, chans), lambda j, s: (0, 4 + s[0])),
        pl.BlockSpec((chans, width), lambda j, s: (s[0], 0)),
        pl.BlockSpec((2, 4, chans), lambda j, s: (0, 0, s[0])),
        pl.BlockSpec((2, chans), lambda j, s: (0, s[0])),
        pl.BlockSpec((2, chans, 128), lambda j, s: (0, s[0], 0)),
    ]
    out_specs = [token_rows, token_rows, pl.BlockSpec((total, chans), fixed)]
    out_specs += [channel_rows] * 3
    out_specs += [
        pl.BlockSpec((2, total, chans), lambda j, s: (0, 0, 0)),
        pl.BlockSpec((2, total, chans), lambda j, s: (0, 0, 0)),
        pl.BlockSpec((2, total, 128), lambda j, s: (0, 0, 0)),
    ]
    shape = jax.ShapeDtypeStruct
    out_shape = [
        shape((total, width), BF),
        shape((total, width), BF),
        shape((total, chans), BF),
        shape((total, chans), F32),
        shape((total, chans), F32),
        shape((total, chans), F32),
        shape((2, total, chans), BF),
        shape((2, total, chans), F32),
        shape((2, total, 128), F32),
    ]
    return pl.pallas_call(
        pre_kernel,
        grid_spec=pltpu.PrefetchScalarGridSpec(
            num_scalar_prefetch=1,
            grid=(total // rows,),
            in_specs=in_specs,
            out_specs=out_specs,
            scratch_shapes=[pltpu.VMEM((total + 32, chans), F32)],
        ),
        out_shape=out_shape,
        compiler_params=pltpu.CompilerParams(vmem_limit_bytes=60 << 20),
        name="prepare",
    )(seq_index, tok, cot, mod, flags, edge, in_weight, in_weight, out_weight, conv_w, conv_b, xproj)


def sibling_of(s):
    return s + 1 - 2 * lax.rem(s, 2)


def across_of(s):
    return lax.rem(s + 2, 4)


def remote(src, dst, sems, slot, peer):
    return pltpu.make_async_remote_copy(
        src_ref=src,
        dst_ref=dst,
        send_sem=sems[0].at[slot],
        recv_sem=sems[1].at[slot],
        device_id=peer,
        device_id_type=MESH,
    )


def greet(peers):
    barrier = pltpu.get_barrier_semaphore()
    for peer in peers:
        pl.semaphore_signal(barrier, inc=1, device_id=peer, device_id_type=MESH)
    pl.semaphore_wait(barrier, len(peers))


def comm_params(collective_id, mib=48):
    return pltpu.CompilerParams(
        collective_id=collective_id, has_side_effects=True, vmem_limit_bytes=mib << 20
    )


def gather_kernel(n_dp, tok_ref, mod_ref, all_ref, row_ref, send, recv, msend, mrecv, lsem):
    d, s = lax.axis_index("dp"), lax.axis_index("seq")
    sib, far = sibling_of(s), across_of(s)
    others = [lax.rem(d + k, n_dp) for k in range(1, n_dp)]
    greet([{"seq": sib}, {"seq": far}] + [{"dp": other} for other in others])
    sems = (send, recv)
    to_far = remote(tok_ref, all_ref.at[s], sems, 0, {"seq": far})
    to_sib = remote(tok_ref, all_ref.at[s], sems, 1, {"seq": sib})
    own = pltpu.make_async_copy(tok_ref, all_ref.at[s], lsem.at[0])
    own_row = pltpu.make_async_copy(mod_ref.at[d], row_ref.at[d], lsem.at[1])
    to_far.start()
    rows = []
    for k, other in enumerate(others):
        copy = remote(mod_ref.at[other], row_ref.at[d], (msend, mrecv), k, {"dp": other})
        copy.start()
        rows.append(copy)
    to_sib.start()
    own.start()
    own_row.start()
    to_far.wait()
    forward = remote(all_ref.at[far], all_ref.at[far], sems, 2, {"seq": sib})
    forward.start()
    for copy in rows:
        copy.wait()
    own.wait()
    own_row.wait()
    to_sib.wait()
    forward.wait()


def gather_tokens(tokens, mod_rows):
    n_dp = mod_rows.shape[0]
    dma = pltpu.SemaphoreType.DMA
    return pl.pallas_call(
        functools.partial(gather_kernel, n_dp),
        out_shape=[
            jax.ShapeDtypeStruct((4,) + tokens.shape, tokens.dtype),
            jax.ShapeDtypeStruct(mod_rows.shape, mod_rows.dtype),
        ],
        in_specs=[VMEM_SPEC] * 2,
        out_specs=[VMEM_SPEC] * 2,
        scratch_shapes=[dma((3,)), dma((3,)), dma((n_dp,)), dma((n_dp,)), dma((2,))],
        compiler_params=comm_params(0),
        name="gather_tokens",
    )(tokens, mod_rows)


def reduce_kernel(x_ref, out_ref, from_sib, half, from_x, send, recv):
    s = lax.axis_index("seq")
    sib, far = sibling_of(s), across_of(s)
    c = lax.rem(s, 2)
    greet([{"seq": sib}, {"seq": far}])
    sems = (send, recv)
    first = remote(x_ref.at[1 - c], from_sib, sems, 0, {"seq": sib})
    first.start()
    first.wait()
    half[...] = x_ref[c] + from_sib[...]
    second = remote(half, from_x, sems, 1, {"seq": far})
    second.start()
    second.wait()
    out_ref[c] = half[...] + from_x[...]
    third = remote(out_ref.at[c], out_ref.at[c], sems, 2, {"seq": sib})
    third.start()
    third.wait()


def seq_reduce(x, collective_id):
    _, rows, width = x.shape
    dma = pltpu.SemaphoreType.DMA
    return pl.pallas_call(
        reduce_kernel,
        out_shape=jax.ShapeDtypeStruct(x.shape, F32),
        in_specs=[VMEM_SPEC],
        out_specs=VMEM_SPEC,
        scratch_shapes=[pltpu.VMEM((rows, width), F32)] * 3 + [dma((3,)), dma((3,))],
        compiler_params=comm_params(collective_id),
        name="seq_reduce",
    )(x)


class DpScatter:
    def __init__(self, x, got, acc, far, sems):
        self.x, self.got, self.acc, self.far = x, got, acc, far
        self.sems = sems
        d = lax.axis_index("dp")
        n = lax.axis_size("dp") // 2
        self.n = n
        self.y = lax.rem(d, 2)
        self.z = d // 2
        self.order = [lax.rem(self.z + k, n) for k in range(1, n + 1)]

    @staticmethod
    def scratch(n_dp, block):
        n = n_dp // 2
        dma = pltpu.SemaphoreType.DMA
        return [pltpu.VMEM((n,) + block, BF)] * 3 + [dma((4, n))]

    def near_copy(self, k):
        z = self.order[k]
        peer = 2 * self.z + 1 - self.y
        return pltpu.make_async_remote_copy(
            src_ref=self.x.at[2 * z + 1 - self.y],
            dst_ref=self.got.at[z],
            send_sem=self.sems.at[0, k],
            recv_sem=self.sems.at[1, k],
            device_id={"dp": peer},
            device_id_type=MESH,
        )

    def near_arrival(self, k):
        return self.near_copy(k)

    def far_copy(self, k):
        z = self.order[k]
        return pltpu.make_async_remote_copy(
            src_ref=self.acc.at[z],
            dst_ref=self.far.at[k],
            send_sem=self.sems.at[2, k],
            recv_sem=self.sems.at[3, k],
            device_id={"dp": 2 * z + self.y},
            device_id_type=MESH,
        )

    def start(self):
        for k in range(self.n):
            self.near_copy(k).start()

    def pair(self, k):
        z = self.order[k]
        self.near_copy(k).wait()
        self.acc[z] = (self.x[2 * z + self.y].astype(F32) + self.got[z].astype(F32)).astype(BF)
        if k < self.n - 1:
            self.far_copy(k).start()

    def finish(self):
        for k in range(self.n - 1):
            self.far_copy(k).wait()
        total = self.x[2 * self.z + self.y].astype(F32) + self.got[self.z].astype(F32)
        for k in range(self.n - 1):
            total = total + self.far[k].astype(F32)
        return total


class SeqScatter:
    def __init__(self, x, from_sib, to_x, from_x, sems):
        s = lax.axis_index("seq")
        self.s, self.far = s, across_of(s)
        sib = sibling_of(s)
        self.x, self.from_sib, self.to_x, self.from_x = x, from_sib, to_x, from_x
        pair = (sems.at[0], sems.at[1])
        self.first = remote(x.at[across_of(sib)], from_sib.at[0], pair, 0, {"seq": sib})
        self.second = remote(x.at[sib], from_sib.at[1], pair, 1, {"seq": sib})
        self.third = remote(to_x, from_x, pair, 2, {"seq": self.far})

    @staticmethod
    def scratch(rows, width):
        return [
            pltpu.VMEM((2, rows, width), BF),
            pltpu.VMEM((rows, width), BF),
            pltpu.VMEM((rows, width), BF),
            pltpu.SemaphoreType.DMA((2, 3)),
        ]

    def start(self):
        self.first.start()
        self.second.start()

    def cross(self):
        self.first.wait()
        self.to_x[...] = (self.x[self.far].astype(F32) + self.from_sib[0].astype(F32)).astype(BF)
        self.third.start()

    def finish(self):
        self.second.wait()
        self.third.wait()
        return (
            self.x[self.s].astype(F32) + self.from_sib[1].astype(F32) + self.from_x[...].astype(F32)
        )


class SeqSwap:
    def __init__(self, src, dst, sems):
        s = lax.axis_index("seq")
        self.s, self.src, self.dst = s, src, dst
        pair = (sems.at[0], sems.at[1])
        self.copies = [
            remote(src.at[lax.rem(s + k, 4)], dst.at[s], pair, k - 1, {"seq": lax.rem(s + k, 4)})
            for k in (2, 1, 3)
        ]

    def start(self):
        for copy in self.copies:
            copy.start()
        self.dst[self.s] = self.src[self.s]

    def finish(self):
        for copy in self.copies:
            copy.wait()


def dp_others():
    n = lax.axis_size("dp")
    d = lax.axis_index("dp")
    return [lax.rem(d + k, n) for k in range(1, n)]


def seq_others():
    s = lax.axis_index("seq")
    return [lax.rem(s + k, 4) for k in (1, 2, 3)]


def greet_all():
    greet([{"seq": other} for other in seq_others()] + [{"dp": other} for other in dp_others()])


def last_kernel(*refs):
    (hid_in, x_in, small_in, tok_ref, cot_ref, flag_ref, scale_ref, gate_ref) = refs[:8]
    x_ref, small_ref, tokg_ref, table_ref = refs[8:12]
    seq = SeqScatter(hid_in, *refs[12:16])
    xs = DpScatter(x_in, *refs[16:20])
    smalls = DpScatter(small_in, *refs[20:24])
    red, swap_sems, row, rows_in, row_sems, table_sems, spread_sems = refs[24:]
    swap = SeqSwap(red, x_ref, swap_sems)
    d, s = lax.axis_index("dp"), lax.axis_index("seq")
    sib, far = sibling_of(s), across_of(s)
    n = smalls.n
    y, z = smalls.y, smalls.z
    greet_all()
    seq.start()
    smalls.start()
    seq.cross()
    xs.start()
    for k in range(n):
        smalls.pair(k)
    for k in range(n):
        xs.pair(k)

    width = tok_ref.shape[1]
    grad = seq.finish()
    tokens = tok_ref[...].astype(F32)
    centred = tokens - jnp.mean(tokens, axis=1, keepdims=True)
    inv_std = lax.rsqrt(jnp.mean(centred * centred, axis=1, keepdims=True) + epsilon)
    normed = centred * inv_std
    grad_normed = grad * (1.0 + scale_ref[...])
    inner_product = jnp.mean(grad_normed * normed, axis=1, keepdims=True)
    tokg_ref[...] = (
        cot_ref[...].astype(F32)
        + inv_std * (grad_normed - jnp.mean(grad_normed, axis=1, keepdims=True) - normed * inner_product)
    ).astype(BF)
    row[:, :width] = jnp.sum(grad, axis=0, keepdims=True)
    row[:, width : 2 * width] = jnp.sum(grad * normed, axis=0, keepdims=True)
    row[:, 2 * width : 3 * width] = gate_ref[...]
    row[:, 3 * width :] = jnp.sum(grad * flag_ref[...], axis=0, keepdims=True)
    pair = (row_sems.at[0], row_sems.at[1])
    row_copies = [
        remote(row, rows_in.at[k], pair, k, {"seq": other}) for k, other in enumerate(seq_others())
    ]
    for copy in row_copies:
        copy.start()

    small_ref[s, y, z] = smalls.finish().astype(BF)
    block = small_ref.at[s, y, z]
    spread_pair = (spread_sems.at[0], spread_sems.at[1])
    along_z = [
        remote(block, block, spread_pair, k, {"dp": 2 * smalls.order[k] + y}) for k in range(n - 1)
    ]
    for copy in along_z:
        copy.start()

    for copy in row_copies:
        copy.wait()
    total = row[...] + rows_in[1] + (rows_in[0] + rows_in[2])
    table_ref[d] = total
    table_pair = (table_sems.at[0], table_sems.at[1])
    table_copies = [
        remote(table_ref.at[d], table_ref.at[d], table_pair, k, {"dp": other})
        for k, other in enumerate(dp_others())
    ]
    for copy in table_copies:
        copy.start()

    for copy in along_z:
        copy.wait()
    plane = small_ref.at[s, y]
    along_y = remote(plane, plane, spread_pair, n - 1, {"dp": 2 * z + 1 - y})
    along_y.start()

    red[...] = xs.finish().astype(BF)
    swap.start()

    along_y.wait()
    mine = small_ref.at[s]
    along_x = remote(mine, mine, spread_pair, n, {"seq": far})
    to_sib = remote(mine, mine, spread_pair, n + 1, {"seq": sib})
    along_x.start()
    to_sib.start()
    along_x.wait()
    others = small_ref.at[far]
    forward = remote(others, others, spread_pair, n + 2, {"seq": sib})
    forward.start()
    swap.finish()
    for copy in table_copies:
        copy.wait()
    to_sib.wait()
    forward.wait()


def last_exchange(hid, x_part, small, tokens, cot, flags, scale, gate, collective_id):
    n_dp = x_part.shape[0]
    n = n_dp // 2
    _, rows, width = hid.shape
    dma = pltpu.SemaphoreType.DMA
    shapes = [
        jax.ShapeDtypeStruct(x_part.shape[1:], BF),
        jax.ShapeDtypeStruct((4, 2, n) + small.shape[1:], BF),
        jax.ShapeDtypeStruct((rows, width), BF),
        jax.ShapeDtypeStruct((n_dp, 1, 4 * width), F32),
    ]
    return pl.pallas_call(
        last_kernel,
        out_shape=shapes,
        in_specs=[VMEM_SPEC] * 8,
        out_specs=[VMEM_SPEC] * 4,
        scratch_shapes=SeqScatter.scratch(rows, width)
        + DpScatter.scratch(n_dp, x_part.shape[1:])
        + DpScatter.scratch(n_dp, small.shape[1:])
        + [
            pltpu.VMEM(x_part.shape[1:], BF),
            dma((2, 3)),
            pltpu.VMEM((1, 4 * width), F32),
            pltpu.VMEM((3, 1, 4 * width), F32),
            dma((2, 3)),
            dma((2, n_dp)),
            dma((2, n + 3)),
        ],
        compiler_params=comm_params(collective_id),
        name="last_exchange",
    )(hid, x_part, small, tokens, cot, flags, scale, gate)


def backward_kernel(*refs):
    (proj, act, coef, a2, skip, dl, hp, dy, branch_in, out_in, z_in) = refs[:11]
    (dpre, dact, dflow, dalog, sums, branch_ref, out_ref, z_ref) = refs[11:19]
    g_sc, g_a, g_b, q_a, q_b, r0, r1, r2, red = refs[19:28]
    seq = SeqScatter(branch_in, *refs[28:32])
    outs = DpScatter(out_in, *refs[32:36])
    zs = DpScatter(z_in, *refs[36:40])
    z_red, z_got, swap_sems = refs[40:]
    swap = SeqSwap(z_red, z_got, swap_sems)
    j = pl.program_id(0)
    blocks = pl.num_programs(0) // 2
    length = dl.shape[1]
    n = outs.n

    @pl.when(j == 0)
    def _():
        greet_all()
        seq.start()
        outs.start()

    @pl.when(j == 1)
    def _():
        seq.cross()

    for k in range(n):

        @pl.when(j == 2 + (k * 2) // n)
        def _(k=k):
            outs.pair(k)
            zs.near_copy(k).start()

        @pl.when(j == 5 + (k * 2) // n)
        def _(k=k):
            zs.pair(k)

    @pl.when(lax.rem(j, blocks) == 0)
    def _():
        g_sc[...] = jnp.zeros_like(g_sc)
        dalog[...] = jnp.zeros_like(dalog)
        sums[...] = jnp.zeros_like(sums)

    def run(rev):
        base = (j - blocks if rev else blocks - 1 - j) * length
        dy_block = dy.at[pl.ds(pl.multiple_of(base, length), length)]
        backward_block(
            rev, dl.at[0], act.at[0], coef.at[0], a2.at[0], proj.at[0], dy_block, skip.at[0], hp.at[0],
            dpre.at[0], dact.at[0], dflow.at[0, 0], dalog.at[0], sums.at[0], g_sc,
            ((g_a, q_a), (g_b, q_b)), (r0, r1, r2), red,
        )

    pl.when(j < blocks)(lambda: run(False))
    pl.when(j >= blocks)(lambda: run(True))

    @pl.when(j == 2 * blocks - 1)
    def _():
        branch_ref[...] = seq.finish()
        out_ref[...] = outs.finish().astype(BF)
        z_red[...] = zs.finish().astype(BF)
        swap.start()
        swap.finish()
        z_ref[...] = z_got[...]


def scan_backward(proj, act, coef, a2, skip, dl, hp, dy, branch, out_part, z_part, collective_id):
    total, chans = dy.shape
    blocks = total // TILE
    n_dp = out_part.shape[0]
    _, rows, width = branch.shape

    def place(j):
        d = j // blocks
        b = lax.rem(j, blocks)
        return d, blocks - 1 - b + d * (2 * b - blocks + 1)

    def tokens_of(j):
        d, b = place(j)
        return d, b, 0

    def direction_of(j):
        return j // blocks, 0, 0

    def cells(j):
        d, b = place(j)
        return d, b, 0, 0

    whole = VMEM_SPEC
    in_specs = [
        pl.BlockSpec((1, TILE, 128), tokens_of),
        pl.BlockSpec((1, TILE, chans), tokens_of),
        pl.BlockSpec((1, TILE // U, 2 * STATE, U), cells),
        pl.BlockSpec((1, STATE, chans), direction_of),
        pl.BlockSpec((1, 1, chans), direction_of),
        pl.BlockSpec((1, TILE, chans), tokens_of),
        pl.BlockSpec((1, TILE * STATE, chans), tokens_of),
    ] + [whole] * 4
    out_specs = [
        pl.BlockSpec((1, TILE, chans), tokens_of),
        pl.BlockSpec((1, TILE, chans), tokens_of),
        pl.BlockSpec((1, 1, STATE, TILE), cells),
        pl.BlockSpec((1, STATE, chans), direction_of),
        pl.BlockSpec((1, 2, U, chans), lambda j: (j // blocks, 0, 0, 0)),
    ] + [whole] * 3
    shape = jax.ShapeDtypeStruct
    out_shape = [
        shape((2, total, chans), BF),
        shape((2, total, chans), F32),
        shape((2, blocks, STATE, TILE), F32),
        shape((2, STATE, chans), F32),
        shape((2, 2, U, chans), F32),
        shape((rows, width), F32),
        shape(out_part.shape[1:], BF),
        shape(z_part.shape[1:], BF),
    ]
    return pl.pallas_call(
        backward_kernel,
        grid=(2 * blocks,),
        in_specs=in_specs,
        out_specs=out_specs,
        out_shape=out_shape,
        scratch_shapes=[
            pltpu.VMEM((STATE, chans), F32),
            pltpu.VMEM((U * STATE, chans), BF),
            pltpu.VMEM((U * STATE, chans), BF),
            pltpu.VMEM((U * 8, chans), BF),
            pltpu.VMEM((U * 8, chans), BF),
        ]
        + [pltpu.VMEM((U, chans), F32)] * 3
        + [pltpu.VMEM((U, STATE, 128), F32)]
        + SeqScatter.scratch(rows, width)
        + DpScatter.scratch(n_dp, out_part.shape[1:])
        + DpScatter.scratch(n_dp, z_part.shape[1:])
        + [pltpu.VMEM(z_part.shape[1:], BF)] * 2
        + [pltpu.SemaphoreType.DMA((2, 3))],
        compiler_params=comm_params(collective_id, 60),
        name="scan_backward",
    )(proj, act, coef, a2, skip, dl, hp, dy, branch, out_part, z_part)


def time_embedding(step_ids, model_width):
    halfway = model_width // 2
    frequency = jnp.exp(-math.log(10000.0) * jnp.arange(halfway, dtype=jnp.float32) / halfway)
    angles = step_ids.astype(jnp.float32)[:, None] * frequency[None, :]
    return jnp.concatenate([jnp.cos(angles), jnp.sin(angles)], axis=1)


def silu_slope(values):
    sigma = jax.nn.sigmoid(values)
    return sigma * (1.0 + values * (1.0 - sigma))


def shards(
    tokens,
    cotangent,
    timesteps,
    grid_widths,
    scan_path,
    ada_weight,
    ada_bias,
    edge,
    in_weight,
    conv_weight,
    conv_bias,
    xproj_weight,
    dt_weight,
    dt_bias,
    a_log,
    skip,
    out_weight,
):
    seg_len, width = tokens.shape[1:]
    inner = in_weight.shape[1] // 2
    rank = dt_weight.shape[1]
    taps = conv_weight.shape[1]
    rim = taps - 1
    columns = ada_weight.shape[1]
    n_seq = lax.axis_size("seq")
    n_dp = lax.axis_size("dp")
    dp_index = lax.axis_index("dp")
    seq_index = lax.axis_index("seq")
    length = seg_len * n_seq
    chans = inner // n_seq

    def mine(weight, dim, first=0):
        return lax.dynamic_slice_in_dim(weight, first + seq_index * chans, chans, dim)

    embedded = jax.nn.silu(time_embedding(timesteps, width)).astype(BF)
    modulation_part = jnp.dot(embedded, ada_weight, preferred_element_type=F32) + ada_bias
    gathered, modulation_own = gather_tokens(tokens[0], modulation_part[:, None, :])
    tokens_all = gathered.reshape(length, width)
    modulation_own = modulation_own.reshape(1, -1)
    scale_term = modulation_own[:, width : 2 * width]
    gate_term = modulation_own[:, 2 * width :]

    cotangent_all = lax.all_gather(cotangent[0], "seq", axis=0, tiled=True)
    path = lax.all_gather(scan_path[0], "seq", axis=0, tiled=True)

    def norm(values):
        values = values.astype(F32)
        centred = values - jnp.mean(values, axis=1, keepdims=True)
        inv_std = lax.rsqrt(jnp.mean(centred * centred, axis=1, keepdims=True) + epsilon)
        return centred * inv_std, inv_std

    def flags_of(item):
        return (jnp.remainder(item, grid_widths[0]) == grid_widths[0] - 1).astype(F32)[:, None]

    hidden, grad_branch, xin, dy, silu_z, slope_z, act, slope, part = prepare(
        seq_index.astype(jnp.int32)[None],
        tokens_all,
        cotangent_all,
        modulation_own,
        flags_of(path),
        edge[None],
        in_weight,
        out_weight,
        conv_weight,
        conv_bias,
        xproj_weight,
    )
    w_x, w_z = mine(in_weight, 1), mine(in_weight, 1, inner)
    w_out = mine(out_weight, 0)
    conv_w = mine(conv_weight, 2)
    padded = jnp.pad(xin, ((rim, rim), (0, 0))).astype(F32)
    starts = [list(range(taps)), [2 * rim - tap for tap in range(taps)]]
    xproj = mine(xproj_weight, 1)
    proj = seq_reduce(part, 1)
    dtw = jnp.pad(mine(dt_weight, 2), ((0, 0), (0, 128 - rank), (0, 0)))
    dtb = mine(dt_bias, 1)
    decay = -jnp.exp(jnp.swapaxes(mine(a_log, 1), 1, 2))
    decay2 = decay * LOG2E
    skips = mine(skip, 1)

    coef = jnp.swapaxes(proj[:, :, 128 - 2 * STATE :].reshape(2, length // U, U, 2 * STATE), 2, 3)
    held, delta, dread, branch, out_part, z_part, grad_z = scan_forward(
        proj, act, coef, dtw, dtb[:, None], decay2, skips[:, None], dy, silu_z, slope_z, hidden,
        grad_branch, w_out,
    )
    total = n_dp * n_seq

    def product(left, right):
        return lax.dot_general(
            left, right, (((0,), (0,)), ((), ())), preferred_element_type=F32
        ).astype(BF)

    def in_blocks(grad):
        return grad.reshape(n_dp, n_seq, width // total, chans)

    dpre, dact, dflow, dalog, sums, branch, out_rows, in_z = scan_backward(
        proj, act, coef, decay2, skips[:, None], delta, held, dy,
        branch.reshape(n_seq, seg_len, width),
        out_part.reshape(n_dp, chans // n_dp, width),
        in_blocks(z_part),
        2,
    )
    out_grad = lax.ppermute(
        out_rows,
        ("dp", "seq"),
        [(d * n_seq + s, s * n_dp + d) for d in range(n_dp) for s in range(n_seq)],
    ).astype(F32)
    tok_float = tokens[0].astype(F32)
    cot_float = cotangent[0].astype(F32)
    result = (tok_float + gate_term * branch).astype(BF)
    gate_grad = jnp.sum(cot_float * branch, axis=0, keepdims=True)

    coef_grad = jnp.concatenate([dflow, dread], axis=2)
    coef_grad = jnp.swapaxes(coef_grad, 2, 3).reshape(2, length, 2 * STATE)
    partial = jnp.stack(
        [
            lax.dot_general(dpre[d], dtw[d], (((1,), (1,)), ((), ())), preferred_element_type=F32)
            for d in range(2)
        ]
    ) + jnp.pad(coef_grad, ((0, 0), (0, 0), (128 - 2 * STATE, 0)))
    dproj = seq_reduce(partial, 3).astype(BF)
    dalog = dalog * decay
    sums = jnp.sum(sums, axis=2)
    grad_conv, small, xproj_grads = [], [], []
    for d in range(2):
        grad_act = (
            lax.dot_general(dproj[d], xproj[d], (((1,), (1,)), ((), ())), preferred_element_type=F32)
            + dact[d]
        )
        dconv = grad_act * slope[d]
        grad_conv.append(dconv)
        xproj_grads.append(
            lax.dot_general(
                dproj[d], act[d], (((0,), (0,)), ((), ())), preferred_element_type=F32
            )
        )
        dtw_grad = lax.dot_general(
            proj[d].astype(BF), dpre[d], (((0,), (0,)), ((), ())), preferred_element_type=F32
        )[:rank]
        conv_rows = jnp.stack(
            [jnp.sum(dconv * padded[first : first + length], axis=0) for first in starts[d]]
        )
        vectors = jnp.concatenate([jnp.sum(dconv, axis=0)[None], sums[d]], axis=0)
        small.append(jnp.concatenate([dtw_grad, dalog[d], conv_rows, vectors], axis=0))
    dxin = 0.0
    for d in range(2):
        for tap in range(taps):
            first = starts[d][tap]
            dxin = dxin + jnp.pad(
                conv_w[d, tap] * grad_conv[d], ((first, 2 * rim - first), (0, 0))
            )
    dxin = dxin[rim : rim + length].astype(BF)
    grad_hidden = (
        lax.dot_general(dxin, w_x, (((1,), (1,)), ((), ())), preferred_element_type=F32)
        + lax.dot_general(grad_z, w_z, (((1,), (1,)), ((), ())), preferred_element_type=F32)
    ).astype(BF)
    rows = jnp.concatenate(
        [xproj_grads[0], small[0], xproj_grads[1], small[1]], axis=0
    )
    n_rows = rows.shape[0]
    rows = jnp.pad(rows.astype(BF), ((0, -n_rows % (16 * n_dp)), (0, 0)))
    in_x, rows, grad_tok, table = last_exchange(
        grad_hidden.reshape(n_seq, seg_len, width),
        in_blocks(product(hidden, dxin)),
        rows.reshape(n_dp, -1, chans),
        tokens[0],
        cotangent[0],
        flags_of(scan_path[0]),
        scale_term,
        gate_grad,
        4,
    )
    in_grad = jnp.concatenate([in_x, in_z], axis=0)
    in_grad = jnp.swapaxes(in_grad, 0, 1).reshape(-1, 2 * inner).astype(F32)
    table = table.reshape(n_dp, -1)
    edge_grad = jnp.sum(table[:, 3 * width :], axis=0)
    mod_columns = lax.dynamic_slice_in_dim(table[:, : 3 * width], dp_index * columns, columns, 1)
    ada_b_grad = jnp.sum(mod_columns, axis=0)
    ada_w_grad = jnp.dot(embedded.astype(F32).T, mod_columns, precision=highest)

    rows = jnp.transpose(rows, (2, 1, 3, 0, 4)).reshape(-1, inner)[:n_rows]
    rows = rows.reshape(2, -1, inner).astype(F32)
    cuts = [128, 128 + rank, 128 + rank + STATE, 128 + rank + STATE + taps]
    xproj_grad = jnp.swapaxes(rows[:, : cuts[0]], 1, 2)
    dtw_grad = rows[:, cuts[0] : cuts[1]]
    alog_grad = jnp.swapaxes(rows[:, cuts[1] : cuts[2]], 1, 2)
    convw_grad = rows[:, cuts[2] : cuts[3]]
    last = cuts[3]
    return (
        result[None],
        grad_tok[None],
        ada_w_grad,
        ada_b_grad,
        edge_grad,
        in_grad,
        convw_grad,
        rows[:, last],
        xproj_grad,
        dtw_grad,
        rows[:, last + 1],
        alog_grad,
        rows[:, last + 2],
        out_grad,
    )


def solution(mesh):
    in_specs = (
        P("dp", "seq", None),
        P("dp", "seq", None),
        P(),
        P("dp"),
        P("dp", "seq"),
        P(None, "dp"),
        P("dp"),
        P(),
        P(),
        P(),
        P(),
        P(),
        P(),
        P(),
        P(),
        P(),
        P(),
    )
    out_specs = (
        P("dp", "seq", None),
        P("dp", "seq", None),
        P(None, "dp"),
        P("dp"),
        P(),
        P(("dp", "seq"), None),
        P(),
        P(),
        P(),
        P(),
        P(),
        P(),
        P(),
        P(("dp", "seq"), None),
    )
    return jax.shard_map(shards, mesh=mesh, in_specs=in_specs, out_specs=out_specs, check_vma=False)
```

```python
import functools
import math

import jax
import jax.numpy as jnp
from jax import lax
from jax.experimental import pallas as pl
from jax.experimental.pallas import tpu as pltpu
from jax.sharding import PartitionSpec as P

STATE = 16
U = 16
PARTS = 3
LOG2E = 1.4426950408889634
LN2 = 0.6931471805599453
F32 = jnp.float32
BF = jnp.bfloat16
epsilon = 1e-06
highest = lax.Precision.HIGHEST
MESH = pl.DeviceIdType.MESH
VMEM_SPEC = pl.BlockSpec(memory_space=pltpu.VMEM)


def iota(shape, dim):
    return lax.broadcasted_iota(jnp.int32, shape, dim)


def dot(a, b):
    return lax.dot_general(a, b, (((1,), (0,)), ((), ())), preferred_element_type=F32)


def dot_nt(a, b):
    return lax.dot_general(a, b, (((1,), (1,)), ((), ())), preferred_element_type=F32)


def dot_tn(a, b):
    return lax.dot_general(a, b, (((0,), (0,)), ((), ())), preferred_element_type=F32)


def softplus(x):
    return jnp.maximum(x, 0.0) + jnp.log1p(jnp.exp(-jnp.abs(x)))


def diag_of(rows, first):
    k = U * STATE
    pick = (iota((128, k), 0) - first == lax.rem(iota((128, k), 1), STATE)).astype(F32).astype(BF)
    keep = (iota((U, k), 1) // STATE == iota((U, k), 0)).astype(F32)
    return (dot(rows.astype(BF), pick) * keep).astype(BF)


def over_lanes(x, t):
    return jnp.broadcast_to(x[:, t : t + 1], (x.shape[0], 128))


def wide(x, n):
    return jnp.concatenate([x] * n, axis=1)


def lane_fold(x):
    acc = x[:, :128]
    for j in range(1, x.shape[1] // 128):
        acc = acc + x[:, 128 * j : 128 * (j + 1)]
    return acc


def interleave(steps, pieces):
    done = 0
    for i, step in enumerate(steps):
        step()
        while done < (i + 1) * len(pieces) // len(steps):
            pieces[done]()
            done += 1


def pipeline(groups, work, drain):
    interleave(work(0, 0), [])

    def two(p, carry):
        interleave(work(2 * p + 1, 1), drain(2 * p, 0))
        interleave(work(2 * p + 2, 0), drain(2 * p + 1, 1))
        return carry

    lax.fori_loop(0, groups // 2 - 1, two, 0)
    interleave(work(groups - 1, 1), drain(groups - 2, 0))
    interleave([lambda: None], drain(groups - 1, 1))


def forward_block(rev, dl, act, coef, a2, proj, dy, hp, put_y, dread, h_sc, hb_sc, slots, rows, red):
    length, chans = dl.shape
    groups = length // U
    part_width = chans // PARTS
    dlu, duu, dyu = rows
    dread[...] = jnp.zeros_like(dread)

    def place(k):
        return (groups - 1 - k) if rev else k

    def work(k, slot):
        g = place(k)
        t0 = pl.multiple_of(g * U, U)
        at = pl.ds(t0, U)
        dlu[...] = dl[at, :]
        duu[...] = dl[at, :] * act[at, :].astype(F32)
        dyu[...] = dy[at, :]
        inflow = coef[g][:STATE]
        spread = [over_lanes(inflow, t) for t in range(U)]
        hbuf = slots[slot]
        v = {}

        def token(part, i):
            col = pl.ds(part * part_width, part_width)
            if i == 0:
                v["a"], v["h"], v["hb"] = a2[:, col], h_sc[:, col], hb_sc[:, col]
            loc = (U - 1 - i) if rev else i
            one = pl.ds(loc, 1)
            h = jnp.exp2(dlu[one, col] * v["a"]) * v["h"] + duu[one, col] * wide(
                spread[loc], part_width // 128
            )
            hp[pl.ds(pl.multiple_of((t0 + loc) * STATE, STATE), STATE), col] = v["hb"]
            hb = h.astype(BF)
            hbuf[pl.ds(loc * STATE, STATE), col] = hb
            v["h"], v["hb"] = h, hb
            total = lane_fold(dyu[one, col] * h)
            if part:
                total = red[loc] + total
            if part < PARTS - 1:
                red[loc] = total
            else:
                here = iota(dread.shape, 1) == g * U + loc
                v["sum"] = jnp.where(here, jnp.sum(total, axis=1, keepdims=True), v.get("sum", 0.0))
                if i == U - 1:
                    dread[...] += v["sum"]
            if i == U - 1:
                h_sc[:, col] = h
                hb_sc[:, col] = hb

        return [functools.partial(token, part, i) for part in range(PARTS) for i in range(U)]

    def drain(k, slot):
        at = pl.ds(pl.multiple_of(place(k) * U, U), U)
        hbuf = slots[slot]
        v = {}

        def first():
            v["c"] = diag_of(proj[at, :], 128 - STATE)

        def out(c):
            col = pl.ds(256 * c, 256)
            put_y(at, col, dot(v["c"], hbuf[:, col]))

        return [first] + [functools.partial(out, c) for c in range(chans // 256)]

    pipeline(groups, work, drain)


def backward_block(
    rev, dl, act, coef, a2, proj, dy, skip, hp, dpre, dact, dflow, dalog, sums, g_sc, slots, rows, red
):
    length, chans = dl.shape
    groups = length // U
    part_width = chans // PARTS
    dlu, duu, dyu = rows
    dflow[...] = jnp.zeros_like(dflow)

    def place(k):
        return k if rev else (groups - 1 - k)

    def work(k, slot):
        g = place(k)
        t0 = pl.multiple_of(g * U, U)
        at = pl.ds(t0, U)
        dlu[...] = dl[at, :]
        duu[...] = dl[at, :] * act[at, :].astype(F32)
        dyu[...] = dy[at, :]
        readout = coef[g][STATE:]
        spread = [over_lanes(readout, t) for t in range(U)]
        gbuf, qbuf = slots[slot]
        v = {}

        def token(part, i):
            col = pl.ds(part * part_width, part_width)
            if i == 0:
                v["a"], v["car"], v["acc"] = a2[:, col], g_sc[:, col], dalog[:, col]
            loc = i if rev else (U - 1 - i)
            one = pl.ds(loc, 1)
            step = dlu[one, col]
            g_t = dyu[one, col] * wide(spread[loc], part_width // 128) + v["car"]
            car = jnp.exp2(step * v["a"]) * g_t
            before = hp[pl.ds(pl.multiple_of((t0 + loc) * STATE, STATE), STATE), col].astype(F32)
            q = car * before
            v["acc"] = v["acc"] + q * step
            v["car"] = car
            gbuf[pl.ds(loc * STATE, STATE), col] = g_t.astype(BF)
            total = lane_fold(duu[one, col] * g_t)
            if part:
                total = red[loc] + total
            if part < PARTS - 1:
                red[loc] = total
            else:
                here = iota(dflow.shape, 1) == g * U + loc
                v["sum"] = jnp.where(here, jnp.sum(total, axis=1, keepdims=True), v.get("sum", 0.0))
                if i == U - 1:
                    dflow[...] += v["sum"]
            qa = q * v["a"]
            qa = qa[:8] + qa[8:]
            if i % 2 == 0:
                v["held"] = qa
            else:
                pair = [v["held"], qa] if rev else [qa, v["held"]]
                qbuf[pl.ds((loc // 2) * STATE, STATE), col] = jnp.concatenate(pair, 0).astype(BF)
            if i == U - 1:
                g_sc[:, col] = v["car"]
                dalog[:, col] = v["acc"]

        return [functools.partial(token, part, i) for part in range(PARTS) for i in range(U)]

    def drain(k, slot):
        at = pl.ds(pl.multiple_of(place(k) * U, U), U)
        gbuf, qbuf = slots[slot]
        v = {}

        def first():
            v["b"] = diag_of(proj[at, :], 128 - 2 * STATE)
            v["ones"] = (iota((U, U * 8), 1) // 8 == iota((U, U * 8), 0)).astype(F32).astype(BF)

        def cols(c):
            col = pl.ds(256 * c, 256)
            s = dot(v["b"], gbuf[:, col])
            q = dot(v["ones"], qbuf[:, col]) * LN2
            a = act[at, col].astype(F32)
            step = dl[at, col]
            grad = dy[at, col]
            pre = ((q + a * s) * (1.0 - jnp.exp(-step))).astype(BF)
            dpre[at, col] = pre
            dact[at, col] = step * s + skip[:, col] * grad
            sums[0, :, col] += pre.astype(F32)
            sums[1, :, col] += grad * a

        return [first] + [functools.partial(cols, c) for c in range(chans // 256)]

    pipeline(groups, work, drain)


def forward_kernel(
    proj, act, coef, dtw, dtb, a2, skip, dy, silu_z, slope_z, hidden, grad_branch, w_out,
    hp, dl, dread, branch, out_part, z_part, grad_z,
    y, h_sc, hb_sc, h_a, h_b, r0, r1, r2, red, gated,
):
    j = pl.program_id(0)
    blocks = pl.num_programs(0) // 2
    length, chans = dl.shape[1:]

    @pl.when(lax.rem(j, blocks) == 0)
    def _():
        h_sc[...] = jnp.zeros_like(h_sc)
        hb_sc[...] = jnp.zeros_like(hb_sc)

    pre = dot(proj[0].astype(BF), dtw[0]) + dtb[0]
    dl[0] = softplus(pre)

    def run(rev):
        base = (2 * blocks - 1 - j if rev else j) * length
        dy_block = dy.at[pl.ds(pl.multiple_of(base, length), length)]

        def put_y(at, col, value):
            value = value + skip[0, :, col] * act[0, at, col].astype(F32)
            rows = pl.ds(pl.multiple_of(base + at.start, U), U)
            if rev:
                value = value + y[rows, col]
            y[rows, col] = value

        forward_block(
            rev, dl.at[0], act.at[0], coef.at[0], a2.at[0], proj.at[0], dy_block, hp.at[0], put_y,
            dread.at[0, 0], h_sc, hb_sc, (h_a, h_b), (r0, r1, r2), red,
        )

    pl.when(j < blocks)(lambda: run(False))
    pl.when(j >= blocks)(lambda: run(True))

    @pl.when(j == 2 * blocks - 1)
    def _():
        total = y.shape[0]

        def rows_of(c, carry):
            at = pl.ds(pl.multiple_of(c * 64, 64), 64)
            value = y[at, :]
            gated[at, :] = (value * silu_z[at, :]).astype(BF)
            grad_z[at, :] = (value * slope_z[at, :]).astype(BF)
            return carry

        lax.fori_loop(0, total // 64, rows_of, 0)
        width = w_out.shape[1]

        for c in range(2):
            at = slice(c * total // 2, (c + 1) * total // 2)
            branch[at, :] = dot(gated[at, :], w_out[...]).astype(BF)

        for c in range(2):
            at = slice(c * chans // 2, (c + 1) * chans // 2)
            out_part[at, :] = dot_tn(gated[:, at], grad_branch[...]).astype(BF)
        for c in range(2):
            at = slice(c * width // 2, (c + 1) * width // 2)
            z_part[at, :] = dot_tn(hidden[:, at], grad_z[...]).astype(BF)


def scan_forward(proj, act, coef, dtw, dtb, a2, skip, dy, silu_z, slope_z, hidden, grad_branch, w_out, tile):
    total, chans = dy.shape
    width = w_out.shape[1]
    blocks = total // tile

    def place(j):
        d = j // blocks
        b = lax.rem(j, blocks)
        return d, b + d * (blocks - 1 - 2 * b)

    def tokens_of(j):
        d, b = place(j)
        return d, b, 0

    def direction_of(j):
        return j // blocks, 0, 0

    def cells(j):
        d, b = place(j)
        return d, b, 0, 0

    whole = VMEM_SPEC
    in_specs = [
        pl.BlockSpec((1, tile, 128), tokens_of),
        pl.BlockSpec((1, tile, chans), tokens_of),
        pl.BlockSpec((1, tile // U, 2 * STATE, U), cells),
        pl.BlockSpec((1, 128, chans), direction_of),
        pl.BlockSpec((1, 1, chans), direction_of),
        pl.BlockSpec((1, STATE, chans), direction_of),
        pl.BlockSpec((1, 1, chans), direction_of),
    ] + [whole] * 6
    out_specs = [
        pl.BlockSpec((1, tile * STATE, chans), tokens_of),
        pl.BlockSpec((1, tile, chans), tokens_of),
        pl.BlockSpec((1, 1, STATE, tile), cells),
    ] + [whole] * 4
    out_shape = [
        jax.ShapeDtypeStruct((2, total * STATE, chans), BF),
        jax.ShapeDtypeStruct((2, total, chans), F32),
        jax.ShapeDtypeStruct((2, blocks, STATE, tile), F32),
        jax.ShapeDtypeStruct((total, width), BF),
        jax.ShapeDtypeStruct((chans, width), BF),
        jax.ShapeDtypeStruct((width, chans), BF),
        jax.ShapeDtypeStruct((total, chans), BF),
    ]
    return pl.pallas_call(
        forward_kernel,
        grid=(2 * blocks,),
        in_specs=in_specs,
        out_specs=out_specs,
        out_shape=out_shape,
        scratch_shapes=[
            pltpu.VMEM((total, chans), F32),
            pltpu.VMEM((STATE, chans), F32),
            pltpu.VMEM((STATE, chans), BF),
            pltpu.VMEM((U * STATE, chans), BF),
            pltpu.VMEM((U * STATE, chans), BF),
        ]
        + [pltpu.VMEM((U, chans), F32)] * 3
        + [pltpu.VMEM((U, STATE, 128), F32), pltpu.VMEM((total, chans), BF)],
        compiler_params=pltpu.CompilerParams(vmem_limit_bytes=60 << 20),
        name="scan_forward",
    )(proj, act, coef, dtw, dtb, a2, skip, dy, silu_z, slope_z, hidden, grad_branch, w_out)


def pre_kernel(
    s_ref, tok, cot, mod, flags, edge, w_x, w_z, w_out, conv_w, conv_b, xproj,
    hidden, grad_branch, xin, dy, silu_z, slope_z, act, slope, part, pad,
):
    j = pl.program_id(0)
    rows, width = tok.shape
    total, chans = xin.shape
    at = pl.ds(pl.multiple_of(j * rows, rows), rows)
    shift, scale, gate = (mod[:, k * width : (k + 1) * width] for k in range(3))
    tokens = tok[...].astype(F32)
    centred = tokens - jnp.mean(tokens, axis=1, keepdims=True)
    normed = centred * lax.rsqrt(jnp.mean(centred * centred, axis=1, keepdims=True) + epsilon)
    hid = (normed * (1.0 + scale) + shift + flags[...] * edge[...]).astype(BF)
    hidden[...] = hid
    grad = (cot[...].astype(F32) * gate).astype(BF)
    grad_branch[...] = grad
    xin[at, :] = dot(hid, w_x[...]).astype(BF)
    z = dot(hid, w_z[...])
    sigma = jax.nn.sigmoid(z)
    grad_gated = dot_nt(grad, w_out[...])
    silu_z[...] = z * sigma
    dy[...] = grad_gated * (z * sigma)
    slope_z[...] = grad_gated * (sigma * (1.0 + z * (1.0 - sigma)))

    @pl.when(j == pl.num_programs(0) - 1)
    def _():
        pad[:16, :] = jnp.zeros((16, chans), F32)
        pad[total + 16 :, :] = jnp.zeros((16, chans), F32)
        pad[16 : total + 16, :] = xin[...].astype(F32)
        step = 64

        def chunk(c, carry):
            base = pl.multiple_of(c * step, step)
            window = pad[pl.ds(base, step + 32), :]
            here = pl.ds(base, step)
            for d in range(2):
                value = conv_b[d : d + 1, :]
                for tap in range(4):
                    first = 13 + tap if d == 0 else 19 - tap
                    value = value + conv_w[d, tap : tap + 1, :] * window[first : first + step]
                sig = jax.nn.sigmoid(value)
                acted = (value * sig).astype(BF)
                act[d, here, :] = acted
                slope[d, here, :] = (sig * (1.0 + value * (1.0 - sig))).astype(BF)
                part[d, here, :] = dot(acted, xproj[d])
            return carry

        lax.fori_loop(0, total // step, chunk, 0)


def prepare(seq_index, tok, cot, mod, flags, edge, in_weight, out_weight, conv_w, conv_b, xproj):
    total, width = tok.shape
    inner = out_weight.shape[0]
    chans = inner // 4
    rows = 128

    def by_rows(j, s):
        return j, 0

    def fixed(j, s):
        return 0, 0

    token_rows = pl.BlockSpec((rows, width), by_rows)
    channel_rows = pl.BlockSpec((rows, chans), by_rows)
    in_specs = [
        token_rows,
        token_rows,
        pl.BlockSpec((1, 3 * width), fixed),
        pl.BlockSpec((rows, 1), by_rows),
        pl.BlockSpec((1, width), fixed),
        pl.BlockSpec((width, chans), lambda j, s: (0, s[0])),
        pl.BlockSpec((width, chans), lambda j, s: (0, 4 + s[0])),
        pl.BlockSpec((chans, width), lambda j, s: (s[0], 0)),
        pl.BlockSpec((2, 4, chans), lambda j, s: (0, 0, s[0])),
        pl.BlockSpec((2, chans), lambda j, s: (0, s[0])),
        pl.BlockSpec((2, chans, 128), lambda j, s: (0, s[0], 0)),
    ]
    out_specs = [token_rows, token_rows, pl.BlockSpec((total, chans), fixed)]
    out_specs += [channel_rows] * 3
    out_specs += [
        pl.BlockSpec((2, total, chans), lambda j, s: (0, 0, 0)),
        pl.BlockSpec((2, total, chans), lambda j, s: (0, 0, 0)),
        pl.BlockSpec((2, total, 128), lambda j, s: (0, 0, 0)),
    ]
    shape = jax.ShapeDtypeStruct
    out_shape = [
        shape((total, width), BF),
        shape((total, width), BF),
        shape((total, chans), BF),
        shape((total, chans), F32),
        shape((total, chans), F32),
        shape((total, chans), F32),
        shape((2, total, chans), BF),
        shape((2, total, chans), BF),
        shape((2, total, 128), F32),
    ]
    return pl.pallas_call(
        pre_kernel,
        grid_spec=pltpu.PrefetchScalarGridSpec(
            num_scalar_prefetch=1,
            grid=(total // rows,),
            in_specs=in_specs,
            out_specs=out_specs,
            scratch_shapes=[pltpu.VMEM((total + 32, chans), F32)],
        ),
        out_shape=out_shape,
        compiler_params=pltpu.CompilerParams(vmem_limit_bytes=60 << 20),
        name="prepare",
    )(seq_index, tok, cot, mod, flags, edge, in_weight, in_weight, out_weight, conv_w, conv_b, xproj)


def sibling_of(s):
    return s + 1 - 2 * lax.rem(s, 2)


def across_of(s):
    return lax.rem(s + 2, 4)


def remote(src, dst, sems, slot, peer):
    return pltpu.make_async_remote_copy(
        src_ref=src,
        dst_ref=dst,
        send_sem=sems[0].at[slot],
        recv_sem=sems[1].at[slot],
        device_id=peer,
        device_id_type=MESH,
    )


def greet(peers, more=0):
    barrier = pltpu.get_barrier_semaphore()
    for peer in peers:
        pl.semaphore_signal(barrier, inc=1, device_id=peer, device_id_type=MESH)
    pl.semaphore_wait(barrier, len(peers) + more)


def comm_params(collective_id, mib=48):
    return pltpu.CompilerParams(
        collective_id=collective_id, has_side_effects=True, vmem_limit_bytes=mib << 20
    )


def gather_kernel(n_dp, tok_ref, mod_ref, all_ref, row_ref, send, recv, msend, mrecv, lsem):
    d, s = lax.axis_index("dp"), lax.axis_index("seq")
    sib, far = sibling_of(s), across_of(s)
    others = [lax.rem(d + k, n_dp) for k in range(1, n_dp)]
    greet([{"seq": sib}, {"seq": far}] + [{"dp": other} for other in others])
    sems = (send, recv)
    to_far = remote(tok_ref, all_ref.at[s], sems, 0, {"seq": far})
    to_sib = remote(tok_ref, all_ref.at[s], sems, 1, {"seq": sib})
    own = pltpu.make_async_copy(tok_ref, all_ref.at[s], lsem.at[0])
    own_row = pltpu.make_async_copy(mod_ref.at[d], row_ref.at[d], lsem.at[1])
    to_far.start()
    rows = []
    for k, other in enumerate(others):
        copy = remote(mod_ref.at[other], row_ref.at[d], (msend, mrecv), k, {"dp": other})
        copy.start()
        rows.append(copy)
    to_sib.start()
    own.start()
    own_row.start()
    to_far.wait()
    forward = remote(all_ref.at[far], all_ref.at[far], sems, 2, {"seq": sib})
    forward.start()
    for copy in rows:
        copy.wait()
    own.wait()
    own_row.wait()
    to_sib.wait()
    forward.wait()


def gather_tokens(tokens, mod_rows):
    n_dp = mod_rows.shape[0]
    dma = pltpu.SemaphoreType.DMA
    return pl.pallas_call(
        functools.partial(gather_kernel, n_dp),
        out_shape=[
            jax.ShapeDtypeStruct((4,) + tokens.shape, tokens.dtype),
            jax.ShapeDtypeStruct(mod_rows.shape, mod_rows.dtype),
        ],
        in_specs=[VMEM_SPEC] * 2,
        out_specs=[VMEM_SPEC] * 2,
        scratch_shapes=[dma((3,)), dma((3,)), dma((n_dp,)), dma((n_dp,)), dma((2,))],
        compiler_params=comm_params(0),
        name="gather_tokens",
    )(tokens, mod_rows)


def reduce_kernel(x_ref, out_ref, from_sib, half, from_x, send, recv):
    s = lax.axis_index("seq")
    sib, far = sibling_of(s), across_of(s)
    c = lax.rem(s, 2)
    greet([{"seq": sib}, {"seq": far}])
    sems = (send, recv)
    first = remote(x_ref.at[1 - c], from_sib, sems, 0, {"seq": sib})
    first.start()
    first.wait()
    half[...] = x_ref[c] + from_sib[...]
    second = remote(half, from_x, sems, 1, {"seq": far})
    second.start()
    second.wait()
    out_ref[c] = half[...] + from_x[...]
    third = remote(out_ref.at[c], out_ref.at[c], sems, 2, {"seq": sib})
    third.start()
    third.wait()


def seq_reduce(x, collective_id):
    _, rows, width = x.shape
    dma = pltpu.SemaphoreType.DMA
    return pl.pallas_call(
        reduce_kernel,
        out_shape=jax.ShapeDtypeStruct(x.shape, F32),
        in_specs=[VMEM_SPEC],
        out_specs=VMEM_SPEC,
        scratch_shapes=[pltpu.VMEM((rows, width), F32)] * 3 + [dma((3,)), dma((3,))],
        compiler_params=comm_params(collective_id),
        name="seq_reduce",
    )(x)


class DpScatter:
    def __init__(self, x, got, acc, far, sems, out=None):
        self.x, self.got, self.acc, self.far = x, got, acc, far
        self.out = x if out is None else out
        self.sems = sems
        d = lax.axis_index("dp")
        n = lax.axis_size("dp") // 2
        self.n = n
        self.y = lax.rem(d, 2)
        self.z = d // 2
        self.order = [lax.rem(self.z + k, n) for k in range(1, n + 1)]

    @staticmethod
    def scratch(n_dp, block):
        n = n_dp // 2
        dma = pltpu.SemaphoreType.DMA
        return [pltpu.VMEM((n,) + block, BF)] * 3 + [dma((4, n))]

    def near_copy(self, k):
        z = self.order[k]
        peer = 2 * self.z + 1 - self.y
        return pltpu.make_async_remote_copy(
            src_ref=self.out.at[2 * z + 1 - self.y],
            dst_ref=self.got.at[z],
            send_sem=self.sems.at[0, k],
            recv_sem=self.sems.at[1, k],
            device_id={"dp": peer},
            device_id_type=MESH,
        )

    def near_arrival(self, k):
        return self.near_copy(k)

    def far_copy(self, k):
        z = self.order[k]
        return pltpu.make_async_remote_copy(
            src_ref=self.acc.at[z],
            dst_ref=self.far.at[k],
            send_sem=self.sems.at[2, k],
            recv_sem=self.sems.at[3, k],
            device_id={"dp": 2 * z + self.y},
            device_id_type=MESH,
        )

    def start(self):
        for k in range(self.n):
            self.near_copy(k).start()

    def pair(self, k):
        z = self.order[k]
        self.near_copy(k).wait()
        self.acc[z] = (self.x[2 * z + self.y].astype(F32) + self.got[z].astype(F32)).astype(BF)
        if k < self.n - 1:
            self.far_copy(k).start()

    def finish(self):
        for k in range(self.n - 1):
            self.far_copy(k).wait()
        total = self.acc[self.z].astype(F32)
        for k in range(self.n - 1):
            total = total + self.far[k].astype(F32)
        return total


class SeqScatter:
    def __init__(self, x, from_sib, to_x, from_x, sems, out=None):
        out = x if out is None else out
        s = lax.axis_index("seq")
        self.s, self.far = s, across_of(s)
        sib = sibling_of(s)
        self.x, self.from_sib, self.to_x, self.from_x = x, from_sib, to_x, from_x
        pair = (sems.at[0], sems.at[1])
        self.first = remote(out.at[across_of(sib)], from_sib.at[0], pair, 0, {"seq": sib})
        self.second = remote(out.at[sib], from_sib.at[1], pair, 1, {"seq": sib})
        self.third = remote(to_x, from_x, pair, 2, {"seq": self.far})

    @staticmethod
    def scratch(rows, width):
        return [
            pltpu.VMEM((2, rows, width), BF),
            pltpu.VMEM((rows, width), BF),
            pltpu.VMEM((rows, width), BF),
            pltpu.SemaphoreType.DMA((2, 3)),
        ]

    def start(self):
        self.first.start()
        self.second.start()

    def cross(self):
        self.first.wait()
        self.to_x[...] = (self.x[self.far].astype(F32) + self.from_sib[0].astype(F32)).astype(BF)
        self.third.start()

    def finish(self):
        self.second.wait()
        self.third.wait()
        return (
            self.x[self.s].astype(F32) + self.from_sib[1].astype(F32) + self.from_x[...].astype(F32)
        )


class SeqSwap:
    def __init__(self, src, dst, sems):
        s = lax.axis_index("seq")
        self.s, self.src, self.dst = s, src, dst
        pair = (sems.at[0], sems.at[1])
        self.copies = [
            remote(src.at[lax.rem(s + k, 4)], dst.at[s], pair, k - 1, {"seq": lax.rem(s + k, 4)})
            for k in (2, 1, 3)
        ]

    def start(self):
        for copy in self.copies:
            copy.start()
        self.dst[self.s] = self.src[self.s]

    def finish(self):
        for copy in self.copies:
            copy.wait()


def dp_others():
    n = lax.axis_size("dp")
    d = lax.axis_index("dp")
    return [lax.rem(d + k, n) for k in range(1, n)]


def seq_others():
    s = lax.axis_index("seq")
    return [lax.rem(s + k, 4) for k in (1, 2, 3)]


def greet_all(more=0):
    greet([{"seq": other} for other in seq_others()] + [{"dp": other} for other in dp_others()], more)


class Spread:
    def __init__(self, buf, sems):
        d, s = lax.axis_index("dp"), lax.axis_index("seq")
        n = lax.axis_size("dp") // 2
        y, z = lax.rem(d, 2), d // 2
        sib, far = sibling_of(s), across_of(s)
        pair = (sems.at[0], sems.at[1])
        block, column, mine, other = buf.at[s, z, y], buf.at[s, :, y], buf.at[s], buf.at[far]
        self.along_z = [
            remote(block, block, pair, k, {"dp": 2 * lax.rem(z + k + 1, n) + y}) for k in range(n - 1)
        ]
        self.along_y = remote(column, column, pair, n - 1, {"dp": 2 * z + 1 - y})
        self.along_x = remote(mine, mine, pair, n, {"seq": far})
        self.to_sib = remote(mine, mine, pair, n + 1, {"seq": sib})
        self.forward = remote(other, other, pair, n + 2, {"seq": sib})
        self.place = (s, z, y)

    @staticmethod
    def scratch(n_dp, block):
        n = n_dp // 2
        return [pltpu.VMEM((4, n, 2) + block, BF), pltpu.SemaphoreType.DMA((2, n + 3))]

    def go_z(self):
        for copy in self.along_z:
            copy.start()

    def go_y(self):
        for copy in self.along_z:
            copy.wait()
        self.along_y.start()

    def go_x(self):
        self.along_y.wait()
        self.along_x.start()
        self.to_sib.start()

    def go_sib(self):
        self.along_x.wait()
        self.forward.start()

    def finish(self):
        self.to_sib.wait()
        self.forward.wait()


class SeqReduce:
    def __init__(self, x, total, from_sib, half, from_x, sems):
        s = lax.axis_index("seq")
        self.c = c = lax.rem(s, 2)
        sib, far = sibling_of(s), across_of(s)
        pair = (sems.at[0], sems.at[1])
        self.x, self.total, self.from_sib, self.half, self.from_x = x, total, from_sib, half, from_x
        self.first = remote(x.at[1 - c], from_sib, pair, 0, {"seq": sib})
        self.second = remote(half, from_x, pair, 1, {"seq": far})
        self.third = remote(total.at[c], total.at[c], pair, 2, {"seq": sib})

    @staticmethod
    def scratch(rows, width):
        return (
            [pltpu.VMEM((2, rows, width), F32)] * 2
            + [pltpu.VMEM((rows, width), F32)] * 3
            + [pltpu.SemaphoreType.DMA((2, 3))]
        )

    def start(self):
        self.first.start()

    def cross(self):
        self.first.wait()
        self.half[...] = self.x[self.c] + self.from_sib[...]
        self.second.start()

    def back(self):
        self.second.wait()
        self.total[self.c] = self.half[...] + self.from_x[...]
        self.third.start()

    def finish(self):
        self.third.wait()


class Turn:
    def __init__(self, src, dst, sems):
        d, s = lax.axis_index("dp"), lax.axis_index("seq")
        n_dp = lax.axis_size("dp")
        here, target = 4 * d + s, s * n_dp + d
        self.apart = here != target
        self.source = {"dp": lax.rem(here, n_dp), "seq": here // n_dp}
        self.copy = remote(
            src, dst, (sems.at[0], sems.at[1]), 0, {"dp": target // 4, "seq": lax.rem(target, 4)}
        )
        self.src, self.dst = src, dst

    def greet(self):
        @pl.when(self.apart)
        def _():
            barrier = pltpu.get_barrier_semaphore()
            pl.semaphore_signal(barrier, inc=1, device_id=self.source, device_id_type=MESH)

        return jnp.where(self.apart, 1, 0)

    def start(self):
        pl.when(self.apart)(self.copy.start)

        @pl.when(jnp.logical_not(self.apart))
        def _():
            self.dst[...] = self.src[...]

    def finish(self):
        pl.when(self.apart)(self.copy.wait)


def rows_in_eights(x):
    total = x[:8]
    for k in range(1, x.shape[0] // 8):
        total = total + x[8 * k : 8 * k + 8]
    return total


def backward_kernel(*refs):
    refs = list(refs)

    def take(count):
        taken = refs[:count]
        del refs[:count]
        return taken

    (dl, hp, proj, act, coef, a2, skip, dy, dread, decay, conv_w) = take(11)
    (tok, cot, gate, scale, flags) = take(5)
    far_inputs = take(10)
    in_weight, xproj_weight = far_inputs[4:6]
    (result, tokg, in_ref, out_ref, a_ref, x0_ref, x1_ref, cv_ref, table_ref) = take(9)
    g_sc, g_a, g_b, q_a, q_b, r0, r1, r2, red = take(9)
    dpre, dc, dflow, dalog, sums = take(5)
    slope, xpad, hidden, grad_z, w_x, w_z, xproj, dtw, hid_in, out_in, xs_in, local_sems = take(12)
    conv_acc, dxin, gate_row = take(3)
    seq1 = SeqScatter(hid_in, *take(4), out=far_inputs[7])
    outs = DpScatter(out_in, *take(4), out=far_inputs[8])
    zs = DpScatter(xs_in, *take(4), out=far_inputs[9])
    out_red, out_got, turn_sems = take(3)
    turn = Turn(out_red, out_got, turn_sems)
    z_red, z_got, z_swap_sems = take(3)
    z_swap = SeqSwap(z_red, z_got, z_swap_sems)
    c7 = SeqReduce(*take(6))
    smalls = []
    for _ in range(5):
        source = take(1)[0]
        scatter = DpScatter(source, *take(4))
        buf, sems = take(2)
        smalls.append((source, scatter, buf, Spread(buf, sems)))
    parts_a, parts_x, part_c = smalls[:2], smalls[2:4], smalls[4]
    seq2 = SeqScatter(hid_in, *take(4))
    xs = DpScatter(xs_in, *take(4))
    x_red, x_got, x_swap_sems = take(3)
    x_swap = SeqSwap(x_red, x_got, x_swap_sems)
    row, rows_in, row_sems, table, table_sems, result_sems = take(6)

    j = pl.program_id(0)
    blocks = pl.num_programs(0) // 2
    length = dl.shape[1]
    total = blocks * length
    chans = dl.shape[2]
    width = tok.shape[1]
    n = outs.n
    n_dp = 2 * n
    d_index, s_index = lax.axis_index("dp"), lax.axis_index("seq")

    def loads():
        own = pl.ds(pl.multiple_of(s_index * chans, 128), chans)
        own_z = pl.ds(pl.multiple_of((4 + s_index) * chans, 128), chans)
        pairs = [
            (far_inputs[0], slope),
            (far_inputs[1], xpad.at[pl.ds(16, total)]),
            (far_inputs[2], hidden),
            (far_inputs[3], grad_z),
            (in_weight.at[:, own], w_x),
            (in_weight.at[:, own_z], w_z),
            (xproj_weight.at[:, own], xproj),
            (far_inputs[6], dtw),
            (far_inputs[7], hid_in),
            (far_inputs[8], out_in),
            (far_inputs[9], xs_in),
        ]
        return [pltpu.make_async_copy(a, b, local_sems.at[i]) for i, (a, b) in enumerate(pairs)]

    def results():
        pairs = []
        for d in range(2):
            buf = parts_a[d][2]
            pairs += [(buf.at[q], a_ref.at[d, :, :, :, pl.ds(q * chans, chans)]) for q in range(4)]
        pairs += [(parts_x[0][2], x0_ref), (parts_x[1][2], x1_ref), (part_c[2], cv_ref)]
        return [pltpu.make_async_copy(a, b, result_sems.at[i]) for i, (a, b) in enumerate(pairs)]

    near = [(outs, k) for k in range(n)] + [(zs, k) for k in range(n)]
    start_at = [0, 0, 1, 3, 4, 6, 7, 8]
    pair_at = [4, 5, 6, 7, 8, 8, 8, 8]

    def step_of(plan, i):
        return plan[i * 8 // (2 * n)]

    unit = 2 * blocks // 8

    @pl.when(j == 0)
    def _():
        greet_all(turn.greet())
        seq1.start()
        for copy in loads():
            copy.start()
        for d in range(2):
            dc[d, :16, :] = jnp.zeros((16, chans), F32)
            dc[d, total + 16 :, :] = jnp.zeros((16, chans), F32)
        xpad[:16, :] = jnp.zeros((16, chans), BF)
        xpad[total + 16 :, :] = jnp.zeros((16, chans), BF)
        dalog[...] = jnp.zeros_like(dalog)
        sums[...] = jnp.zeros_like(sums)
        conv_acc[...] = jnp.zeros_like(conv_acc)

    for i, (scatter, k) in enumerate(near):
        if step_of(pair_at, i) < 8:
            pl.when(j == unit * step_of(pair_at, i))(functools.partial(scatter.pair, k))
        if step_of(start_at, i) < 8:
            pl.when(j == unit * step_of(start_at, i))(scatter.near_copy(k).start)

    @pl.when(j == 2 * unit)
    def _():
        loads()[8].wait()
        seq1.cross()

    @pl.when(j == 3 * unit)
    def _():
        loads()[9].wait()
        loads()[10].wait()


    @pl.when(j == 5 * unit)
    def _():
        branch = seq1.finish()
        result[...] = (tok[...].astype(F32) + gate[...] * branch).astype(BF)
        gate_row[...] = jnp.sum(cot[...].astype(F32) * branch, axis=0, keepdims=True)

    @pl.when(lax.rem(j, blocks) == 0)
    def _():
        g_sc[...] = jnp.zeros_like(g_sc)

    def run(rev):
        d = int(rev)
        block = j - blocks if rev else blocks - 1 - j
        base = pl.multiple_of(block * length, length)
        here = pl.ds(base, length)
        backward_block(
            rev, dl.at[0], act.at[d, here], coef.at[0], a2.at[d],
            proj.at[d, here], dy.at[here], skip.at[d], hp.at[0], dpre.at[d, here],
            dc.at[d, pl.ds(pl.multiple_of(base + 16, 16), length)], dflow.at[d, block], dalog.at[d],
            sums.at[d], g_sc, ((g_a, q_a), (g_b, q_b)), (r0, r1, r2), red,
        )

    pl.when(j < blocks)(lambda: run(False))
    pl.when(j >= blocks)(lambda: run(True))

    @pl.when(j == 2 * blocks - 1)
    def _():
        late = [i for i in range(2 * n) if step_of(start_at, i) >= 8]
        for i in late:
            near[i][0].near_copy(near[i][1]).start()
        for copy in loads()[:8]:
            copy.wait()
        for d in range(2):
            value = dot_nt(dpre[d], dtw[d])
            for b in range(blocks):
                at = slice(b * length, (b + 1) * length)
                square = jnp.concatenate(
                    [jnp.zeros((128 - 2 * STATE, length), F32), dflow[d, b], dread[d, b]], axis=0
                )
                c7.x[d, at] = value[at] + square.T
        c7.start()
        late = [i for i in range(2 * n) if step_of(pair_at, i) >= 8]
        quarter = len(late) // 4
        rank = 128 - 2 * STATE
        per_d = 128 // n_dp
        for d in range(2):
            source, scatter, _, _ = parts_a[d]
            lines = dot_tn(proj[d].astype(BF), dpre[d])[:rank]
            extra = [jnp.sum(sums[d, i], axis=0, keepdims=True) for i in range(2)]
            lines = jnp.concatenate(
                [lines, dalog[d] * decay[d]] + extra + [jnp.zeros((STATE - 2, chans), F32)], axis=0
            ).astype(BF)
            for b in range(n_dp):
                source[b] = lines[b * per_d : (b + 1) * per_d]
            scatter.start()
        c7.cross()
        for i in late[:quarter]:
            near[i][0].pair(near[i][1])
        for _, scatter, _, _ in parts_a:
            for k in range(n):
                scatter.pair(k)
        c7.back()
        for i in late[quarter : 2 * quarter]:
            near[i][0].pair(near[i][1])
        c7.finish()

        rows_x = chans // n_dp
        for d in range(2):
            dproj = c7.total[d].astype(BF)
            source, scatter, _, _ = parts_x[d]
            grad = dot_tn(act[d], dproj).astype(BF)
            for b in range(n_dp):
                source[b] = grad[b * rows_x : (b + 1) * rows_x]
            scatter.start()

            def act_rows(c, carry, d=d):
                at = pl.ds(pl.multiple_of(c * 128, 128), 128)
                shifted = pl.ds(pl.multiple_of(c * 128 + 16, 16), 128)
                value = dot_nt(c7.total[d, at].astype(BF), xproj[d]) + dc[d, shifted]
                dc[d, shifted] = value * slope[d, at].astype(F32)
                return carry

            lax.fori_loop(0, total // 128, act_rows, 0)

        step = 32

        def conv_rows(c, carry):
            base = pl.multiple_of(c * step, step)
            window = pl.ds(base, step + 32)
            x_w = xpad[window, :].astype(F32)
            grad = jnp.zeros((step, chans), F32)
            for d in range(2):
                d_w = dc[d, window]
                here = d_w[16 : 16 + step]
                conv_acc[5 * d + 4] += rows_in_eights(here)
                for tap in range(4):
                    off = tap - 3 if d == 0 else 3 - tap
                    conv_acc[5 * d + tap] += rows_in_eights(here * x_w[16 + off : 16 + off + step])
                    grad = grad + conv_w[d, tap : tap + 1] * d_w[16 - off : 16 - off + step]
            dxin[pl.ds(base, step), :] = grad.astype(BF)
            return carry

        lax.fori_loop(0, total // step, conv_rows, 0)
        for i in late[2 * quarter :]:
            near[i][0].pair(near[i][1])

        rb = width // (4 * n_dp)
        half = n_dp // 2
        for h in range(2):
            cols = slice(h * width // 2, (h + 1) * width // 2)
            grad = dot_tn(hidden[:, cols], dxin[...]).astype(BF)
            for b in range(half):
                for q in range(4):
                    first = (4 * b + q) * rb
                    xs_in[h * half + b, q] = grad[first : first + rb]
        xs.start()
        for _, scatter, buf, spread in parts_a:
            buf[spread.place] = scatter.finish().astype(BF)
            spread.go_z()
        seg = tok.shape[0]
        for h in range(2):
            cols = slice(h * width // 2, (h + 1) * width // 2)
            grad = (dot_nt(dxin[...], w_x[cols, :]) + dot_nt(grad_z[...], w_z[cols, :])).astype(BF)
            for q in range(4):
                hid_in[q, :, cols] = grad[q * seg : (q + 1) * seg]
        seq2.start()
        for _, scatter, _, _ in parts_x:
            for k in range(n):
                scatter.pair(k)
        source, scatter, _, _ = part_c
        conv_lines = [jnp.sum(conv_acc[i], axis=0, keepdims=True) for i in range(10)]
        conv_lines = jnp.concatenate(conv_lines + [jnp.zeros((6, chans), F32)], axis=0)
        for b in range(n_dp):
            source[b, :, :rows_x] = conv_lines[:, b * rows_x : (b + 1) * rows_x].astype(BF)
            source[b, :, rows_x:] = jnp.zeros((16, 128 - rows_x), BF)
        scatter.start()
        seq2.cross()
        out_red[...] = outs.finish().astype(BF)
        turn.start()
        for _, _, _, spread in parts_a:
            spread.go_y()
        z_red[...] = zs.finish().astype(BF)
        for k in range(n):
            part_c[1].pair(k)
        for _, scatter, buf, spread in parts_x:
            buf[spread.place] = scatter.finish().astype(BF)
            spread.go_z()

        grad = seq2.finish()
        z_swap.start()
        for _, _, _, spread in parts_a:
            spread.go_x()
        tokens = tok[...].astype(F32)
        centred = tokens - jnp.mean(tokens, axis=1, keepdims=True)
        inv_std = lax.rsqrt(jnp.mean(centred * centred, axis=1, keepdims=True) + epsilon)
        normed = centred * inv_std
        grad_normed = grad * (1.0 + scale[...])
        inner_product = jnp.mean(grad_normed * normed, axis=1, keepdims=True)
        tokg[...] = (
            cot[...].astype(F32)
            + inv_std
            * (grad_normed - jnp.mean(grad_normed, axis=1, keepdims=True) - normed * inner_product)
        ).astype(BF)
        row[:, :width] = jnp.sum(grad, axis=0, keepdims=True)
        row[:, width : 2 * width] = jnp.sum(grad * normed, axis=0, keepdims=True)
        row[:, 2 * width : 3 * width] = gate_row[...]
        row[:, 3 * width :] = jnp.sum(grad * flags[...], axis=0, keepdims=True)
        pair = (row_sems.at[0], row_sems.at[1])
        row_copies = [
            remote(row, rows_in.at[k], pair, k, {"seq": other})
            for k, other in enumerate(seq_others())
        ]
        for copy in row_copies:
            copy.start()
        source, scatter, buf, spread_c = part_c
        buf[spread_c.place] = scatter.finish().astype(BF)
        spread_c.go_z()
        for k in range(n // 2):
            xs.pair(k)
        for copy in row_copies:
            copy.wait()
        table[d_index] = row[...] + rows_in[1] + (rows_in[0] + rows_in[2])
        pair = (table_sems.at[0], table_sems.at[1])
        table_copies = [
            remote(table.at[d_index], table.at[d_index], pair, k, {"dp": other})
            for k, other in enumerate(dp_others())
        ]
        for copy in table_copies:
            copy.start()
        spreads_x = [item[3] for item in parts_x] + [spread_c]
        for spread in spreads_x:
            spread.go_y()
        for _, _, _, spread in parts_a:
            spread.go_sib()
        for k in range(n // 2, n - 1):
            xs.pair(k)
        for spread in spreads_x:
            spread.go_x()
        xs.pair(n - 1)
        turn.finish()
        out_ref[...] = out_got[...]
        z_swap.finish()
        for q in range(4):
            in_ref[:, (4 + q) * chans : (5 + q) * chans] = z_got[q]
        for spread in spreads_x:
            spread.go_sib()
        for (_, _, buf, spread), d in zip(parts_a, range(2)):
            spread.finish()
            for copy in results()[4 * d : 4 * d + 4]:
                copy.start()
        for copy in table_copies:
            copy.wait()
        table_ref[...] = table[...]
        x_red[...] = xs.finish().astype(BF)
        x_swap.start()
        for spread in spreads_x:
            spread.finish()
        for copy in results()[8:]:
            copy.start()
        x_swap.finish()
        for q in range(4):
            in_ref[:, q * chans : (q + 1) * chans] = x_got[q]
        for copy in results():
            copy.wait()


def scan_backward(
    dl, hp, proj, act, coef, a2, skip, dy, dread, decay, conv_w, branch, out_part, z_part,
    tok, cot, gate, scale, flags, slope, xin, hidden, grad_z, in_weight, xproj_weight, dtw, collective_id, tile,
):
    total, chans = dy.shape
    blocks = total // tile
    n_dp = out_part.shape[0]
    n = n_dp // 2
    rows, width = tok.shape
    rb = width // (4 * n_dp)
    rows_x = chans // n_dp
    per_d = 128 // n_dp

    def place(j):
        d = j // blocks
        b = lax.rem(j, blocks)
        return d, blocks - 1 - b + d * (2 * b - blocks + 1)

    def tokens_of(j):
        d, b = place(j)
        return d, b, 0

    def cells(j):
        d, b = place(j)
        return d, b, 0, 0

    any_spec = pl.BlockSpec(memory_space=pl.ANY)
    in_specs = (
        [
            pl.BlockSpec((1, tile, chans), tokens_of),
            pl.BlockSpec((1, tile * STATE, chans), tokens_of),
        ]
        + [VMEM_SPEC] * 2
        + [pl.BlockSpec((1, tile // U, 2 * STATE, U), cells)]
        + [VMEM_SPEC] * 11
        + [any_spec] * 10
    )
    shape = jax.ShapeDtypeStruct
    in_out = (4, n, 2)
    out_shape = [
        shape((rows, width), BF),
        shape((rows, width), BF),
        shape((rb, 8 * chans), BF),
        shape(out_part.shape[1:], BF),
        shape((2, n, 2, per_d, 4 * chans), BF),
        shape(in_out + (rows_x, 128), BF),
        shape(in_out + (rows_x, 128), BF),
        shape(in_out + (16, 128), BF),
        shape((n_dp, 1, 4 * width), F32),
    ]
    dma = pltpu.SemaphoreType.DMA
    vmem = pltpu.VMEM
    scratch = [
        vmem((STATE, chans), F32),
        vmem((U * STATE, chans), BF),
        vmem((U * STATE, chans), BF),
        vmem((U * 8, chans), BF),
        vmem((U * 8, chans), BF),
    ]
    scratch += [vmem((U, chans), F32)] * 3 + [vmem((U, STATE, 128), F32)]
    scratch += [
        vmem((2, total, chans), BF),
        vmem((2, total + 32, chans), F32),
        vmem((2, blocks, STATE, tile), F32),
        vmem((2, STATE, chans), F32),
        vmem((2, 2, U, chans), F32),
    ]
    scratch += [
        vmem(slope.shape, BF),
        vmem((total + 32, chans), BF),
        vmem(hidden.shape, BF),
        vmem(grad_z.shape, BF),
        vmem((width, chans), BF),
        vmem((width, chans), BF),
        vmem((2, chans, 128), BF),
        vmem(dtw.shape, BF),
        vmem((4, rows, width), BF),
        vmem(out_part.shape, BF),
        vmem(z_part.shape, BF),
        dma((11,)),
    ]
    scratch += [
        vmem((10, 8, chans), F32),
        vmem((total, chans), BF),
        vmem((1, width), F32),
    ]
    scratch += SeqScatter.scratch(rows, width)
    scratch += DpScatter.scratch(n_dp, out_part.shape[1:]) + DpScatter.scratch(n_dp, z_part.shape[1:])
    scratch += [vmem(out_part.shape[1:], BF)] * 2 + [dma((2, 1))]
    scratch += [vmem(z_part.shape[1:], BF)] * 2 + [dma((2, 3))]
    scratch += SeqReduce.scratch(total, 128)
    for block in [(per_d, chans)] * 2 + [(rows_x, 128)] * 2 + [(16, 128)]:
        scratch += [vmem((n_dp,) + block, BF)] + DpScatter.scratch(n_dp, block)
        scratch += Spread.scratch(n_dp, block)
    scratch += SeqScatter.scratch(rows, width)
    scratch += DpScatter.scratch(n_dp, z_part.shape[1:])
    scratch += [vmem(z_part.shape[1:], BF)] * 2 + [dma((2, 3))]
    scratch += [
        vmem((1, 4 * width), F32),
        vmem((3, 1, 4 * width), F32),
        dma((2, 3)),
        vmem((n_dp, 1, 4 * width), F32),
        dma((2, n_dp)),
        dma((11,)),
    ]
    return pl.pallas_call(
        backward_kernel,
        grid=(2 * blocks,),
        in_specs=in_specs,
        out_specs=[VMEM_SPEC] * 4 + [any_spec] * 4 + [VMEM_SPEC],
        out_shape=out_shape,
        scratch_shapes=scratch,
        compiler_params=comm_params(collective_id, 62),
        name="scan_backward",
    )(
        dl, hp, proj, act, coef, a2, skip, dy, dread, decay, conv_w, tok, cot, gate, scale, flags,
        slope, xin, hidden, grad_z, in_weight, xproj_weight, dtw, branch, out_part, z_part,
    )


def time_embedding(step_ids, model_width):
    halfway = model_width // 2
    frequency = jnp.exp(-math.log(10000.0) * jnp.arange(halfway, dtype=jnp.float32) / halfway)
    angles = step_ids.astype(jnp.float32)[:, None] * frequency[None, :]
    return jnp.concatenate([jnp.cos(angles), jnp.sin(angles)], axis=1)


def silu_slope(values):
    sigma = jax.nn.sigmoid(values)
    return sigma * (1.0 + values * (1.0 - sigma))


def shards(
    tokens,
    cotangent,
    timesteps,
    grid_widths,
    scan_path,
    ada_weight,
    ada_bias,
    edge,
    in_weight,
    conv_weight,
    conv_bias,
    xproj_weight,
    dt_weight,
    dt_bias,
    a_log,
    skip,
    out_weight,
):
    seg_len, width = tokens.shape[1:]
    inner = in_weight.shape[1] // 2
    rank = dt_weight.shape[1]
    taps = conv_weight.shape[1]
    rim = taps - 1
    columns = ada_weight.shape[1]
    n_seq = lax.axis_size("seq")
    n_dp = lax.axis_size("dp")
    dp_index = lax.axis_index("dp")
    seq_index = lax.axis_index("seq")
    length = seg_len * n_seq
    chans = inner // n_seq

    def mine(weight, dim, first=0):
        return lax.dynamic_slice_in_dim(weight, first + seq_index * chans, chans, dim)

    embedded = jax.nn.silu(time_embedding(timesteps, width)).astype(BF)
    modulation_part = jnp.dot(embedded, ada_weight, preferred_element_type=F32) + ada_bias
    gathered, modulation_own = gather_tokens(tokens[0], modulation_part[:, None, :])
    tokens_all = gathered.reshape(length, width)
    modulation_own = modulation_own.reshape(1, -1)
    scale_term = modulation_own[:, width : 2 * width]
    gate_term = modulation_own[:, 2 * width :]

    cotangent_all = lax.all_gather(cotangent[0], "seq", axis=0, tiled=True)
    path = lax.all_gather(scan_path[0], "seq", axis=0, tiled=True)

    def flags_of(item):
        return (jnp.remainder(item, grid_widths[0]) == grid_widths[0] - 1).astype(F32)[:, None]

    hidden, grad_branch, xin, dy, silu_z, slope_z, act, slope, part = prepare(
        seq_index.astype(jnp.int32)[None],
        tokens_all,
        cotangent_all,
        modulation_own,
        flags_of(path),
        edge[None],
        in_weight,
        out_weight,
        conv_weight,
        conv_bias,
        xproj_weight,
    )
    w_out = mine(out_weight, 0)
    conv_w = mine(conv_weight, 2)
    proj = seq_reduce(part, 1)
    dtw = jnp.pad(mine(dt_weight, 2), ((0, 0), (0, 128 - rank), (0, 0)))
    dtb = mine(dt_bias, 1)
    decay = -jnp.exp(jnp.swapaxes(mine(a_log, 1), 1, 2))
    decay2 = decay * LOG2E
    skips = mine(skip, 1)

    tile = 128 if n_dp <= 8 else 32
    coef = jnp.swapaxes(proj[:, :, 128 - 2 * STATE :].reshape(2, length // U, U, 2 * STATE), 2, 3)
    held, delta, dread, branch, out_part, z_part, grad_z = scan_forward(
        proj, act, coef, dtw, dtb[:, None], decay2, skips[:, None], dy, silu_z, slope_z, hidden,
        grad_branch, w_out, tile,
    )
    total = n_dp * n_seq

    def in_blocks(grad):
        return grad.reshape(n_dp, n_seq, width // total, chans)

    result, grad_tok, in_rows, out_rows, lines, x0, x1, conv_lines, table = scan_backward(
        delta, held, proj, act, coef, decay2, skips[:, None], dy, dread, decay, conv_w,
        branch.reshape(n_seq, seg_len, width),
        out_part.reshape(n_dp, chans // n_dp, width),
        in_blocks(z_part),
        tokens[0], cotangent[0], gate_term, scale_term, flags_of(scan_path[0]),
        slope, xin, hidden, grad_z, in_weight, xproj_weight, dtw, 2, tile,
    )
    table = table.reshape(n_dp, -1)
    edge_grad = jnp.sum(table[:, 3 * width :], axis=0)
    mod_columns = lax.dynamic_slice_in_dim(table[:, : 3 * width], dp_index * columns, columns, 1)
    ada_b_grad = jnp.sum(mod_columns, axis=0)
    ada_w_grad = jnp.dot(embedded.astype(F32).T, mod_columns, precision=highest)
    lines = lines.reshape(2, 128, inner).astype(F32)
    alog_grad = jnp.swapaxes(lines[:, rank : rank + STATE], 1, 2)
    xproj_grad = jnp.stack([item.reshape(inner, 128) for item in (x0, x1)]).astype(F32)
    conv_lines = jnp.moveaxis(conv_lines[..., : chans // n_dp], 3, 0).reshape(16, inner).astype(F32)
    conv_lines = conv_lines[: 2 * (taps + 1)].reshape(2, taps + 1, inner)
    return (
        result[None],
        grad_tok[None],
        ada_w_grad,
        ada_b_grad,
        edge_grad,
        in_rows.astype(F32),
        conv_lines[:, :taps],
        conv_lines[:, taps],
        xproj_grad,
        lines[:, :rank],
        lines[:, rank + STATE],
        alog_grad,
        lines[:, rank + STATE + 1],
        out_rows.astype(F32),
    )


def solution(mesh):
    in_specs = (
        P("dp", "seq", None),
        P("dp", "seq", None),
        P(),
        P("dp"),
        P("dp", "seq"),
        P(None, "dp"),
        P("dp"),
        P(),
        P(),
        P(),
        P(),
        P(),
        P(),
        P(),
        P(),
        P(),
        P(),
    )
    out_specs = (
        P("dp", "seq", None),
        P("dp", "seq", None),
        P(None, "dp"),
        P("dp"),
        P(),
        P(("dp", "seq"), None),
        P(),
        P(),
        P(),
        P(),
        P(),
        P(),
        P(),
        P(("dp", "seq"), None),
    )
    return jax.shard_map(shards, mesh=mesh, in_specs=in_specs, out_specs=out_specs, check_vma=False)
```

```python
import functools
import math

import jax
import jax.numpy as jnp
from jax import lax
from jax.experimental import pallas as pl
from jax.experimental.pallas import tpu as pltpu
from jax.sharding import PartitionSpec as P

STATE = 16
U = 16
PARTS = 3
LOG2E = 1.4426950408889634
LN2 = 0.6931471805599453
F32 = jnp.float32
BF = jnp.bfloat16
epsilon = 1e-06
highest = lax.Precision.HIGHEST
MESH = pl.DeviceIdType.MESH
VMEM_SPEC = pl.BlockSpec(memory_space=pltpu.VMEM)


def iota(shape, dim):
    return lax.broadcasted_iota(jnp.int32, shape, dim)


def dot(a, b):
    return lax.dot_general(a, b, (((1,), (0,)), ((), ())), preferred_element_type=F32)


def dot_nt(a, b):
    return lax.dot_general(a, b, (((1,), (1,)), ((), ())), preferred_element_type=F32)


def dot_tn(a, b):
    return lax.dot_general(a, b, (((0,), (0,)), ((), ())), preferred_element_type=F32)


def softplus(x):
    return jnp.maximum(x, 0.0) + jnp.log1p(jnp.exp(-jnp.abs(x)))


def diag_of(rows, first):
    k = U * STATE
    pick = (iota((128, k), 0) - first == lax.rem(iota((128, k), 1), STATE)).astype(F32).astype(BF)
    keep = (iota((U, k), 1) // STATE == iota((U, k), 0)).astype(F32)
    return (dot(rows.astype(BF), pick) * keep).astype(BF)


def over_lanes(x, t):
    return jnp.broadcast_to(x[:, t : t + 1], (x.shape[0], 128))


def wide(x, n):
    return jnp.concatenate([x] * n, axis=1)


def lane_fold(x):
    acc = x[:, :128]
    for j in range(1, x.shape[1] // 128):
        acc = acc + x[:, 128 * j : 128 * (j + 1)]
    return acc


def interleave(steps, pieces):
    done = 0
    for i, step in enumerate(steps):
        step()
        while done < (i + 1) * len(pieces) // len(steps):
            pieces[done]()
            done += 1


def pipeline(groups, work, drain):
    interleave(work(0, 0), [])

    def two(p, carry):
        interleave(work(2 * p + 1, 1), drain(2 * p, 0))
        interleave(work(2 * p + 2, 0), drain(2 * p + 1, 1))
        return carry

    lax.fori_loop(0, groups // 2 - 1, two, 0)
    interleave(work(groups - 1, 1), drain(groups - 2, 0))
    interleave([lambda: None], drain(groups - 1, 1))


def forward_block(rev, dl, act, coef, a2, proj, dy, hp, put_y, dread, h_sc, hb_sc, slots, rows, red):
    length, chans = dl.shape
    groups = length // U
    part_width = chans // PARTS
    dlu, duu, dyu = rows
    dread[...] = jnp.zeros_like(dread)

    def place(k):
        return (groups - 1 - k) if rev else k

    def work(k, slot):
        g = place(k)
        t0 = pl.multiple_of(g * U, U)
        at = pl.ds(t0, U)
        dlu[...] = dl[at, :]
        duu[...] = dl[at, :] * act[at, :].astype(F32)
        dyu[...] = dy[at, :]
        inflow = coef[g][:STATE]
        spread = [over_lanes(inflow, t) for t in range(U)]
        hbuf = slots[slot]
        v = {}

        def token(part, i):
            col = pl.ds(part * part_width, part_width)
            if i == 0:
                v["a"], v["h"], v["hb"] = a2[:, col], h_sc[:, col], hb_sc[:, col]
            loc = (U - 1 - i) if rev else i
            one = pl.ds(loc, 1)
            h = jnp.exp2(dlu[one, col] * v["a"]) * v["h"] + duu[one, col] * wide(
                spread[loc], part_width // 128
            )
            hp[pl.ds(pl.multiple_of((t0 + loc) * STATE, STATE), STATE), col] = v["hb"]
            hb = h.astype(BF)
            hbuf[pl.ds(loc * STATE, STATE), col] = hb
            v["h"], v["hb"] = h, hb
            total = lane_fold(dyu[one, col] * h)
            if part:
                total = red[loc] + total
            if part < PARTS - 1:
                red[loc] = total
            else:
                here = iota(dread.shape, 1) == g * U + loc
                v["sum"] = jnp.where(here, jnp.sum(total, axis=1, keepdims=True), v.get("sum", 0.0))
                if i == U - 1:
                    dread[...] += v["sum"]
            if i == U - 1:
                h_sc[:, col] = h
                hb_sc[:, col] = hb

        return [functools.partial(token, part, i) for part in range(PARTS) for i in range(U)]

    def drain(k, slot):
        at = pl.ds(pl.multiple_of(place(k) * U, U), U)
        hbuf = slots[slot]
        v = {}

        def first():
            v["c"] = diag_of(proj[at, :], 128 - STATE)

        def out(c):
            col = pl.ds(256 * c, 256)
            put_y(at, col, dot(v["c"], hbuf[:, col]))

        return [first] + [functools.partial(out, c) for c in range(chans // 256)]

    pipeline(groups, work, drain)


def backward_block(
    rev, dl, act, coef, a2, proj, dy, skip, hp, dpre, dact, dflow, dalog, sums, g_sc, slots, rows, red
):
    length, chans = dl.shape
    groups = length // U
    part_width = chans // PARTS
    dlu, duu, dyu = rows
    dflow[...] = jnp.zeros_like(dflow)

    def place(k):
        return k if rev else (groups - 1 - k)

    def work(k, slot):
        g = place(k)
        t0 = pl.multiple_of(g * U, U)
        at = pl.ds(t0, U)
        dlu[...] = dl[at, :]
        duu[...] = dl[at, :] * act[at, :].astype(F32)
        dyu[...] = dy[at, :]
        readout = coef[g][STATE:]
        spread = [over_lanes(readout, t) for t in range(U)]
        gbuf, qbuf = slots[slot]
        v = {}

        def token(part, i):
            col = pl.ds(part * part_width, part_width)
            if i == 0:
                v["a"], v["car"], v["acc"] = a2[:, col], g_sc[:, col], dalog[:, col]
            loc = i if rev else (U - 1 - i)
            one = pl.ds(loc, 1)
            step = dlu[one, col]
            g_t = dyu[one, col] * wide(spread[loc], part_width // 128) + v["car"]
            car = jnp.exp2(step * v["a"]) * g_t
            before = hp[pl.ds(pl.multiple_of((t0 + loc) * STATE, STATE), STATE), col].astype(F32)
            q = car * before
            v["acc"] = v["acc"] + q * step
            v["car"] = car
            gbuf[pl.ds(loc * STATE, STATE), col] = g_t.astype(BF)
            total = lane_fold(duu[one, col] * g_t)
            if part:
                total = red[loc] + total
            if part < PARTS - 1:
                red[loc] = total
            else:
                here = iota(dflow.shape, 1) == g * U + loc
                v["sum"] = jnp.where(here, jnp.sum(total, axis=1, keepdims=True), v.get("sum", 0.0))
                if i == U - 1:
                    dflow[...] += v["sum"]
            qa = q * v["a"]
            qa = qa[:8] + qa[8:]
            if i % 2 == 0:
                v["held"] = qa
            else:
                pair = [v["held"], qa] if rev else [qa, v["held"]]
                qbuf[pl.ds((loc // 2) * STATE, STATE), col] = jnp.concatenate(pair, 0).astype(BF)
            if i == U - 1:
                g_sc[:, col] = v["car"]
                dalog[:, col] = v["acc"]

        return [functools.partial(token, part, i) for part in range(PARTS) for i in range(U)]

    def drain(k, slot):
        at = pl.ds(pl.multiple_of(place(k) * U, U), U)
        gbuf, qbuf = slots[slot]
        v = {}

        def first():
            v["b"] = diag_of(proj[at, :], 128 - 2 * STATE)
            v["ones"] = (iota((U, U * 8), 1) // 8 == iota((U, U * 8), 0)).astype(F32).astype(BF)

        def cols(c):
            col = pl.ds(256 * c, 256)
            s = dot(v["b"], gbuf[:, col])
            q = dot(v["ones"], qbuf[:, col]) * LN2
            a = act[at, col].astype(F32)
            step = dl[at, col]
            grad = dy[at, col]
            pre = ((q + a * s) * (1.0 - jnp.exp(-step))).astype(BF)
            dpre[at, col] = pre
            dact[at, col] = step * s + skip[:, col] * grad
            sums[0, :, col] += pre.astype(F32)
            sums[1, :, col] += grad * a

        return [first] + [functools.partial(cols, c) for c in range(chans // 256)]

    pipeline(groups, work, drain)


def forward_kernel(
    s_ref, proj, act, coef, dtw, dtb, a2, skip, dy, silu_z, slope_z, hidden, grad_branch, w_out,
    hp, dl, dread, branch, out_part, z_part, grad_z,
    y, h_sc, hb_sc, h_a, h_b, r0, r1, r2, red, gated,
):
    j = pl.program_id(0)
    blocks = pl.num_programs(0) // 2
    length, chans = dl.shape[1:]

    @pl.when(lax.rem(j, blocks) == 0)
    def _():
        h_sc[...] = jnp.zeros_like(h_sc)
        hb_sc[...] = jnp.zeros_like(hb_sc)

    def run(rev):
        own = slice(int(rev), int(rev) + 1)
        pre = dot(proj[0][:, : dtw.shape[1]].astype(BF), dtw[0]) + dtb[own]
        dl[0] = softplus(pre)
        base = (2 * blocks - 1 - j if rev else j) * length
        dy_block = dy.at[pl.ds(pl.multiple_of(base, length), length)]

        def put_y(at, col, value):
            value = value + skip[own, col] * act[0, at, col].astype(F32)
            rows = pl.ds(pl.multiple_of(base + at.start, U), U)
            if rev:
                value = value + y[rows, col]
            y[rows, col] = value

        forward_block(
            rev, dl.at[0], act.at[0], coef.at[0], a2.at[0], proj.at[0], dy_block, hp.at[0], put_y,
            dread.at[0, 0], h_sc, hb_sc, (h_a, h_b), (r0, r1, r2), red,
        )

    pl.when(j < blocks)(lambda: run(False))
    pl.when(j >= blocks)(lambda: run(True))

    @pl.when(j == 2 * blocks - 1)
    def _():
        total = y.shape[0]

        def rows_of(c, carry):
            at = pl.ds(pl.multiple_of(c * 64, 64), 64)
            value = y[at, :]
            gated[at, :] = (value * silu_z[at, :]).astype(BF)
            grad_z[at, :] = (value * slope_z[at, :]).astype(BF)
            return carry

        lax.fori_loop(0, total // 64, rows_of, 0)
        width = w_out.shape[1]

        for c in range(2):
            at = slice(c * total // 2, (c + 1) * total // 2)
            branch[at, :] = dot(gated[at, :], w_out[...]).astype(BF)

        for c in range(2):
            at = slice(c * chans // 2, (c + 1) * chans // 2)
            out_part[at, :] = dot_tn(gated[:, at], grad_branch[...]).astype(BF)
        for c in range(2):
            at = slice(c * width // 2, (c + 1) * width // 2)
            z_part[at, :] = dot_tn(hidden[:, at], grad_z[...]).astype(BF)


def scan_forward(
    seq_index, proj, act, coef, dtw, dtb, a2, skip, dy, silu_z, slope_z, hidden, grad_branch, w_out, tile
):
    total, chans = dy.shape
    width = w_out.shape[1]
    blocks = total // tile

    def place(j):
        d = j // blocks
        b = lax.rem(j, blocks)
        return d, b + d * (blocks - 1 - 2 * b)

    def tokens_of(j, s):
        d, b = place(j)
        return d, b, 0

    def direction_of(j, s):
        return j // blocks, 0, 0

    def channels_of(j, s):
        return j // blocks, 0, s[0]

    def cells(j, s):
        d, b = place(j)
        return d, b, 0, 0

    whole = VMEM_SPEC
    in_specs = [
        pl.BlockSpec((1, tile, 128), tokens_of),
        pl.BlockSpec((1, tile, chans), tokens_of),
        pl.BlockSpec((1, tile // U, 2 * STATE, U), cells),
        pl.BlockSpec((1, dtw.shape[1], chans), channels_of),
        pl.BlockSpec((2, chans), lambda j, s: (0, s[0])),
        pl.BlockSpec((1, STATE, chans), direction_of),
        pl.BlockSpec((2, chans), lambda j, s: (0, s[0])),
    ] + [whole] * 5
    in_specs += [pl.BlockSpec((chans, width), lambda j, s: (s[0], 0))]
    out_specs = [
        pl.BlockSpec((1, tile * STATE, chans), tokens_of),
        pl.BlockSpec((1, tile, chans), tokens_of),
        pl.BlockSpec((1, 1, STATE, tile), cells),
    ] + [whole] * 4
    out_shape = [
        jax.ShapeDtypeStruct((2, total * STATE, chans), BF),
        jax.ShapeDtypeStruct((2, total, chans), F32),
        jax.ShapeDtypeStruct((2, blocks, STATE, tile), F32),
        jax.ShapeDtypeStruct((total, width), BF),
        jax.ShapeDtypeStruct((chans, width), BF),
        jax.ShapeDtypeStruct((width, chans), BF),
        jax.ShapeDtypeStruct((total, chans), BF),
    ]
    return pl.pallas_call(
        forward_kernel,
        grid_spec=pltpu.PrefetchScalarGridSpec(
            num_scalar_prefetch=1,
            grid=(2 * blocks,),
            in_specs=in_specs,
            out_specs=out_specs,
            scratch_shapes=[
                pltpu.VMEM((total, chans), F32),
                pltpu.VMEM((STATE, chans), F32),
                pltpu.VMEM((STATE, chans), BF),
                pltpu.VMEM((U * STATE, chans), BF),
                pltpu.VMEM((U * STATE, chans), BF),
            ]
            + [pltpu.VMEM((U, chans), F32)] * 3
            + [pltpu.VMEM((U, STATE, 128), F32), pltpu.VMEM((total, chans), BF)],
        ),
        out_shape=out_shape,
        compiler_params=pltpu.CompilerParams(vmem_limit_bytes=60 << 20),
        name="scan_forward",
    )(seq_index, proj, act, coef, dtw, dtb, a2, skip, dy, silu_z, slope_z, hidden, grad_branch, w_out)


def sibling_of(s):
    return s + 1 - 2 * lax.rem(s, 2)


def across_of(s):
    return lax.rem(s + 2, 4)


def remote(src, dst, sems, slot, peer):
    return pltpu.make_async_remote_copy(
        src_ref=src,
        dst_ref=dst,
        send_sem=sems[0].at[slot],
        recv_sem=sems[1].at[slot],
        device_id=peer,
        device_id_type=MESH,
    )


def greet(peers, more=0):
    barrier = pltpu.get_barrier_semaphore()
    for peer in peers:
        pl.semaphore_signal(barrier, inc=1, device_id=peer, device_id_type=MESH)
    pl.semaphore_wait(barrier, len(peers) + more)


def comm_params(collective_id, mib=48):
    return pltpu.CompilerParams(
        collective_id=collective_id, has_side_effects=True, vmem_limit_bytes=mib << 20
    )


class DpScatter:
    def __init__(self, x, got, acc, far, sems, out=None):
        self.x, self.got, self.acc, self.far = x, got, acc, far
        self.out = x if out is None else out
        self.sems = sems
        d = lax.axis_index("dp")
        n = lax.axis_size("dp") // 2
        self.n = n
        self.y = lax.rem(d, 2)
        self.z = d // 2
        self.order = [lax.rem(self.z + k, n) for k in range(1, n + 1)]

    @staticmethod
    def scratch(n_dp, block):
        n = n_dp // 2
        dma = pltpu.SemaphoreType.DMA
        return [pltpu.VMEM((n,) + block, BF)] * 3 + [dma((4, n))]

    def near_copy(self, k):
        z = self.order[k]
        peer = 2 * self.z + 1 - self.y
        return pltpu.make_async_remote_copy(
            src_ref=self.out.at[2 * z + 1 - self.y],
            dst_ref=self.got.at[z],
            send_sem=self.sems.at[0, k],
            recv_sem=self.sems.at[1, k],
            device_id={"dp": peer},
            device_id_type=MESH,
        )

    def near_arrival(self, k):
        return self.near_copy(k)

    def far_copy(self, k):
        z = self.order[k]
        return pltpu.make_async_remote_copy(
            src_ref=self.acc.at[z],
            dst_ref=self.far.at[k],
            send_sem=self.sems.at[2, k],
            recv_sem=self.sems.at[3, k],
            device_id={"dp": 2 * z + self.y},
            device_id_type=MESH,
        )

    def start(self):
        for k in range(self.n):
            self.near_copy(k).start()

    def pair(self, k):
        z = self.order[k]
        self.near_copy(k).wait()
        self.acc[z] = (self.x[2 * z + self.y].astype(F32) + self.got[z].astype(F32)).astype(BF)
        if k < self.n - 1:
            self.far_copy(k).start()

    def finish(self):
        for k in range(self.n - 1):
            self.far_copy(k).wait()
        total = self.acc[self.z].astype(F32)
        for k in range(self.n - 1):
            total = total + self.far[k].astype(F32)
        return total


class SeqScatter:
    def __init__(self, x, from_sib, to_x, from_x, sems, out=None):
        out = x if out is None else out
        s = lax.axis_index("seq")
        self.s, self.far = s, across_of(s)
        sib = sibling_of(s)
        self.x, self.from_sib, self.to_x, self.from_x = x, from_sib, to_x, from_x
        pair = (sems.at[0], sems.at[1])
        self.first = remote(out.at[across_of(sib)], from_sib.at[0], pair, 0, {"seq": sib})
        self.second = remote(out.at[sib], from_sib.at[1], pair, 1, {"seq": sib})
        self.third = remote(to_x, from_x, pair, 2, {"seq": self.far})

    @staticmethod
    def scratch(rows, width):
        return [
            pltpu.VMEM((2, rows, width), BF),
            pltpu.VMEM((rows, width), BF),
            pltpu.VMEM((rows, width), BF),
            pltpu.SemaphoreType.DMA((2, 3)),
        ]

    def start(self):
        self.first.start()
        self.second.start()

    def cross(self):
        self.first.wait()
        self.to_x[...] = (self.x[self.far].astype(F32) + self.from_sib[0].astype(F32)).astype(BF)
        self.third.start()

    def finish(self):
        self.second.wait()
        self.third.wait()
        return (
            self.x[self.s].astype(F32) + self.from_sib[1].astype(F32) + self.from_x[...].astype(F32)
        )


class SeqSwap:
    def __init__(self, src, dst, sems):
        s = lax.axis_index("seq")
        self.s, self.src, self.dst = s, src, dst
        pair = (sems.at[0], sems.at[1])
        self.copies = [
            remote(src.at[lax.rem(s + k, 4)], dst.at[s], pair, k - 1, {"seq": lax.rem(s + k, 4)})
            for k in (2, 1, 3)
        ]

    def start(self):
        for copy in self.copies:
            copy.start()
        self.dst[self.s] = self.src[self.s]

    def finish(self):
        for copy in self.copies:
            copy.wait()


def dp_others():
    n = lax.axis_size("dp")
    d = lax.axis_index("dp")
    return [lax.rem(d + k, n) for k in range(1, n)]


def seq_others():
    s = lax.axis_index("seq")
    return [lax.rem(s + k, 4) for k in (1, 2, 3)]


def greet_all(more=0):
    greet([{"seq": other} for other in seq_others()] + [{"dp": other} for other in dp_others()], more)


class Spread:
    def __init__(self, buf, sems):
        d, s = lax.axis_index("dp"), lax.axis_index("seq")
        n = lax.axis_size("dp") // 2
        y, z = lax.rem(d, 2), d // 2
        sib, far = sibling_of(s), across_of(s)
        pair = (sems.at[0], sems.at[1])
        block, column, mine, other = buf.at[s, z, y], buf.at[s, :, y], buf.at[s], buf.at[far]
        self.along_z = [
            remote(block, block, pair, k, {"dp": 2 * lax.rem(z + k + 1, n) + y}) for k in range(n - 1)
        ]
        self.along_y = remote(column, column, pair, n - 1, {"dp": 2 * z + 1 - y})
        self.along_x = remote(mine, mine, pair, n, {"seq": far})
        self.to_sib = remote(mine, mine, pair, n + 1, {"seq": sib})
        self.forward = remote(other, other, pair, n + 2, {"seq": sib})
        self.place = (s, z, y)

    @staticmethod
    def scratch(n_dp, block):
        n = n_dp // 2
        return [pltpu.VMEM((4, n, 2) + block, BF), pltpu.SemaphoreType.DMA((2, n + 3))]

    def go_z(self):
        for copy in self.along_z:
            copy.start()

    def go_y(self):
        for copy in self.along_z:
            copy.wait()
        self.along_y.start()

    def go_x(self):
        self.along_y.wait()
        self.along_x.start()
        self.to_sib.start()

    def go_sib(self):
        self.along_x.wait()
        self.forward.start()

    def finish(self):
        self.to_sib.wait()
        self.forward.wait()


class SeqReduce:
    def __init__(self, x, total, from_sib, half, from_x, sems):
        s = lax.axis_index("seq")
        self.c = c = lax.rem(s, 2)
        sib, far = sibling_of(s), across_of(s)
        pair = (sems.at[0], sems.at[1])
        self.x, self.total, self.from_sib, self.half, self.from_x = x, total, from_sib, half, from_x
        self.first = remote(x.at[1 - c], from_sib, pair, 0, {"seq": sib})
        self.second = remote(half, from_x, pair, 1, {"seq": far})
        self.third = remote(total.at[c], total.at[c], pair, 2, {"seq": sib})

    @staticmethod
    def scratch(rows, width):
        return (
            [pltpu.VMEM((2, rows, width), F32)] * 2
            + [pltpu.VMEM((rows, width), F32)] * 3
            + [pltpu.SemaphoreType.DMA((2, 3))]
        )

    def start(self):
        self.first.start()

    def cross(self):
        self.first.wait()
        self.half[...] = self.x[self.c] + self.from_sib[...]
        self.second.start()

    def back(self):
        self.second.wait()
        self.total[self.c] = self.half[...] + self.from_x[...]
        self.third.start()

    def finish(self):
        self.third.wait()


class Turn:
    def __init__(self, src, dst, sems):
        d, s = lax.axis_index("dp"), lax.axis_index("seq")
        n_dp = lax.axis_size("dp")
        here, target = 4 * d + s, s * n_dp + d
        self.apart = here != target
        self.source = {"dp": lax.rem(here, n_dp), "seq": here // n_dp}
        self.copy = remote(
            src, dst, (sems.at[0], sems.at[1]), 0, {"dp": target // 4, "seq": lax.rem(target, 4)}
        )
        self.src, self.dst = src, dst

    def greet(self):
        @pl.when(self.apart)
        def _():
            barrier = pltpu.get_barrier_semaphore()
            pl.semaphore_signal(barrier, inc=1, device_id=self.source, device_id_type=MESH)

        return jnp.where(self.apart, 1, 0)

    def start(self):
        pl.when(self.apart)(self.copy.start)

        @pl.when(jnp.logical_not(self.apart))
        def _():
            self.dst[...] = self.src[...]

    def finish(self):
        pl.when(self.apart)(self.copy.wait)


def first_kernel(*refs):
    refs = list(refs)

    def take(count):
        taken = refs[:count]
        del refs[:count]
        return taken

    tok, cot, flag, emb, ada_b, edge = take(6)
    in_weight, out_weight, conv_weight, conv_bias, xproj_weight, ada_weight, a_log = take(7)
    hidden_o, branch_o, xin_o, act_o, slope_o, proj_o, dy_o, silu_o, slope_z_o, mod_o, a2_o = take(11)
    w_x, w_z, w_out, conv_w, conv_b, xproj, ada_w, rates, load_sems = take(9)
    toks, cots, flags, rows_out, rows_in = take(5)
    hidden, grad_branch, xin, z, act, slope, dy, silu_z, slope_z, pad = take(10)
    tok_sems, cot_sems, flag_sems, row_sems, own_sems, store_sems = take(6)
    c3 = SeqReduce(*take(6))
    d, s = lax.axis_index("dp"), lax.axis_index("seq")
    sib, far = sibling_of(s), across_of(s)
    diag = across_of(sib)
    n_dp = lax.axis_size("dp")
    seg, width = tok.shape
    total, chans = xin.shape

    own = pl.ds(pl.multiple_of(s * chans, 128), chans)
    own_z = pl.ds(pl.multiple_of((4 + s) * chans, 128), chans)
    loads = [
        (ada_weight, ada_w),
        (a_log.at[:, :, own], rates),
        (in_weight.at[:, own], w_x),
        (in_weight.at[:, own_z], w_z),
        (conv_weight.at[:, :, own], conv_w),
        (conv_bias.at[:, own], conv_b),
        (xproj_weight.at[:, own], xproj),
        (out_weight.at[own], w_out),
    ]
    loads = [pltpu.make_async_copy(a, b, load_sems.at[i]) for i, (a, b) in enumerate(loads)]
    for copy in loads:
        copy.start()
    greet_all()

    def spread_out(src, dst, sems):
        pair = (sems.at[0], sems.at[1])
        to_far = remote(src, dst.at[s], pair, 0, {"seq": far})
        to_sib = remote(src, dst.at[s], pair, 1, {"seq": sib})
        forward = remote(dst.at[far], dst.at[far], pair, 2, {"seq": sib})
        return to_far, to_sib, forward

    tok_far, tok_sib, tok_forward = spread_out(tok, toks, tok_sems)
    cot_far, cot_sib, cot_forward = spread_out(cot, cots, cot_sems)
    tok_far.start()
    tok_sib.start()
    pair = (flag_sems.at[0], flag_sems.at[1])
    flag_copies = [
        remote(flag, flags.at[s], pair, k, {"seq": other}) for k, other in enumerate(seq_others())
    ]
    for copy in flag_copies:
        copy.start()
    locals_ = [(tok, toks.at[s]), (cot, cots.at[s]), (flag, flags.at[s])]
    locals_ = [pltpu.make_async_copy(a, b, own_sems.at[i]) for i, (a, b) in enumerate(locals_)]
    for copy in locals_:
        copy.start()

    loads[0].wait()
    part = dot_nt(emb[...], ada_w[...]) + ada_b[...]
    columns = part.shape[1]
    for i in range(n_dp):
        rows_out[i] = part[i : i + 1]
    pair = (row_sems.at[0], row_sems.at[1])
    row_copies = [
        remote(rows_out.at[other], rows_in.at[d], pair, k, {"dp": other})
        for k, other in enumerate(dp_others())
    ]
    for copy in row_copies:
        copy.start()
    cot_far.start()
    cot_sib.start()
    rows_in[d] = rows_out[d]
    loads[1].wait()
    for k in range(2):
        a2_o[k] = -LOG2E * jnp.exp(rates[k])
    for copy in row_copies:
        copy.wait()
    for i in range(n_dp):
        mod_o[:, i * columns : (i + 1) * columns] = rows_in[i]
    for copy in flag_copies:
        copy.wait()
    for copy in locals_:
        copy.wait()
    for copy in loads[2:4]:
        copy.wait()

    def project(block):
        at = pl.ds(pl.multiple_of(block * seg, seg), seg)
        tokens = toks[block].astype(F32)
        centred = tokens - jnp.mean(tokens, axis=1, keepdims=True)
        normed = centred * lax.rsqrt(jnp.mean(centred * centred, axis=1, keepdims=True) + epsilon)
        marks = flags[block].T[:, :1]
        hid = normed * (1.0 + mod_o[:, width : 2 * width]) + mod_o[:, :width] + marks * edge[...]
        hid = hid.astype(BF)
        hidden[at, :] = hid
        xin[at, :] = dot(hid, w_x[...]).astype(BF)
        z[at, :] = dot(hid, w_z[...])

    project(s)
    tok_sib.wait()
    project(sib)
    tok_far.wait()
    tok_forward.start()
    project(far)
    tok_forward.wait()
    project(diag)

    stores = [
        (hidden, hidden_o), (xin, xin_o), (act, act_o), (slope, slope_o), (c3.total, proj_o),
        (grad_branch, branch_o), (dy, dy_o), (silu_z, silu_o), (slope_z, slope_z_o),
    ]
    stores = [pltpu.make_async_copy(a, b, store_sems.at[i]) for i, (a, b) in enumerate(stores)]
    stores[0].start()
    stores[1].start()
    pad[:16, :] = jnp.zeros((16, chans), F32)
    pad[total + 16 :, :] = jnp.zeros((16, chans), F32)
    pad[16 : total + 16, :] = xin[...].astype(F32)
    for copy in loads[4:]:
        copy.wait()
    step = 64

    def chunk(c, carry):
        base = pl.multiple_of(c * step, step)
        window = pad[pl.ds(base, step + 32), :]
        here = pl.ds(base, step)
        for k in range(2):
            value = conv_b[k : k + 1, :]
            for tap in range(4):
                first = 13 + tap if k == 0 else 19 - tap
                value = value + conv_w[k, tap : tap + 1, :] * window[first : first + step]
            sig = jax.nn.sigmoid(value)
            acted = (value * sig).astype(BF)
            act[k, here, :] = acted
            slope[k, here, :] = (sig * (1.0 + value * (1.0 - sig))).astype(BF)
            c3.x[k, here, :] = dot(acted, xproj[k])
        return carry

    lax.fori_loop(0, total // step, chunk, 0)
    c3.start()
    stores[2].start()
    stores[3].start()

    def gate_back(block):
        at = pl.ds(pl.multiple_of(block * seg, seg), seg)
        grad = (cots[block].astype(F32) * mod_o[:, 2 * width :]).astype(BF)
        grad_branch[at, :] = grad
        grad_gated = dot_nt(grad, w_out[...])
        value = z[at, :]
        sigma = jax.nn.sigmoid(value)
        silu_z[at, :] = value * sigma
        dy[at, :] = grad_gated * (value * sigma)
        slope_z[at, :] = grad_gated * (sigma * (1.0 + value * (1.0 - sigma)))

    cot_far.wait()
    cot_forward.start()
    gate_back(s)
    c3.cross()
    cot_sib.wait()
    gate_back(sib)
    gate_back(far)
    cot_forward.wait()
    gate_back(diag)
    for copy in stores[5:]:
        copy.start()
    c3.back()
    c3.finish()
    stores[4].start()
    for copy in stores:
        copy.wait()


def first_part(
    tok, cot, flag, emb, ada_b, edge, in_weight, out_weight, conv_weight, conv_bias, xproj_weight,
    ada_w, a_log, collective_id,
):
    seg, width = tok.shape
    total = 4 * seg
    chans = out_weight.shape[0] // 4
    n_dp = emb.shape[0]
    columns = ada_w.shape[0]
    any_spec = pl.BlockSpec(memory_space=pl.ANY)
    shape = jax.ShapeDtypeStruct
    out_shape = [
        shape((total, width), BF),
        shape((total, width), BF),
        shape((total, chans), BF),
        shape((2, total, chans), BF),
        shape((2, total, chans), BF),
        shape((2, total, 128), F32),
        shape((total, chans), F32),
        shape((total, chans), F32),
        shape((total, chans), F32),
        shape((1, 3 * width), F32),
        shape((2, STATE, chans), F32),
    ]
    dma = pltpu.SemaphoreType.DMA
    vmem = pltpu.VMEM
    scratch = [
        vmem((width, chans), BF),
        vmem((width, chans), BF),
        vmem((chans, width), BF),
        vmem((2, 4, chans), F32),
        vmem((2, chans), F32),
        vmem((2, chans, 128), BF),
        vmem(ada_w.shape, BF),
        vmem((2, STATE, chans), F32),
        dma((8,)),
        vmem((4, seg, width), BF),
        vmem((4, seg, width), BF),
        vmem((4, 8, 128), F32),
        vmem((n_dp, 1, columns), F32),
        vmem((n_dp, 1, columns), F32),
        vmem((total, width), BF),
        vmem((total, width), BF),
        vmem((total, chans), BF),
        vmem((total, chans), F32),
        vmem((2, total, chans), BF),
        vmem((2, total, chans), BF),
    ]
    scratch += [vmem((total, chans), F32)] * 3 + [vmem((total + 32, chans), F32)]
    scratch += [dma((2, 3)), dma((2, 3)), dma((2, 3)), dma((2, n_dp)), dma((3,)), dma((9,))]
    scratch += SeqReduce.scratch(total, 128)
    return pl.pallas_call(
        first_kernel,
        in_specs=[VMEM_SPEC] * 6 + [any_spec] * 7,
        out_specs=[any_spec] * 9 + [VMEM_SPEC] * 2,
        out_shape=out_shape,
        scratch_shapes=scratch,
        compiler_params=comm_params(collective_id, 60),
        name="first_part",
    )(
        tok, cot, flag, emb, ada_b, edge, in_weight, out_weight, conv_weight, conv_bias, xproj_weight,
        ada_w, a_log,
    )


def rows_in_eights(x):
    total = x[:8]
    for k in range(1, x.shape[0] // 8):
        total = total + x[8 * k : 8 * k + 8]
    return total


def backward_kernel(*refs):
    refs = list(refs)

    def take(count):
        taken = refs[:count]
        del refs[:count]
        return taken

    (dl, hp, proj, act, coef, a2, dy, dread) = take(8)
    (tok, cot, gate, scale, flags) = take(5)
    far_inputs = take(12)
    dt_weight, conv_weight, skip_all = far_inputs[6:9]
    in_weight, xproj_weight = far_inputs[4:6]
    (result, tokg, in_ref, out_ref, a_ref, x0_ref, x1_ref, cv_ref, table_ref) = take(9)
    g_sc, g_a, g_b, q_a, q_b, r0, r1, r2, red = take(9)
    dpre, dc, dflow, dalog, sums = take(5)
    slope, xpad, hidden, grad_z, w_x, w_z, xproj, dtw, conv_w, skip, hid_in, out_in, xs_in, local_sems = take(14)
    conv_acc, dxin, gate_row = take(3)
    seq1 = SeqScatter(hid_in, *take(4), out=far_inputs[9])
    outs = DpScatter(out_in, *take(4), out=far_inputs[10])
    zs = DpScatter(xs_in, *take(4), out=far_inputs[11])
    out_red, out_got, turn_sems = take(3)
    turn = Turn(out_red, out_got, turn_sems)
    z_red, z_got, z_swap_sems = take(3)
    z_swap = SeqSwap(z_red, z_got, z_swap_sems)
    c7 = SeqReduce(*take(6))
    smalls = []
    for _ in range(5):
        source = take(1)[0]
        scatter = DpScatter(source, *take(4))
        buf, sems = take(2)
        smalls.append((source, scatter, buf, Spread(buf, sems)))
    parts_a, parts_x, part_c = smalls[:2], smalls[2:4], smalls[4]
    seq2 = SeqScatter(hid_in, *take(4))
    xs = DpScatter(xs_in, *take(4))
    x_red, x_got, x_swap_sems = take(3)
    x_swap = SeqSwap(x_red, x_got, x_swap_sems)
    row, rows_in, row_sems, table, table_sems, result_sems = take(6)

    j = pl.program_id(0)
    blocks = pl.num_programs(0) // 2
    length = dl.shape[1]
    total = blocks * length
    chans = dl.shape[2]
    width = tok.shape[1]
    n = outs.n
    n_dp = 2 * n
    d_index, s_index = lax.axis_index("dp"), lax.axis_index("seq")

    def loads():
        own = pl.ds(pl.multiple_of(s_index * chans, 128), chans)
        own_z = pl.ds(pl.multiple_of((4 + s_index) * chans, 128), chans)
        pairs = [
            (far_inputs[0], slope),
            (far_inputs[1], xpad.at[pl.ds(16, total)]),
            (far_inputs[2], hidden),
            (far_inputs[3], grad_z),
            (in_weight.at[:, own], w_x),
            (in_weight.at[:, own_z], w_z),
            (xproj_weight.at[:, own], xproj),
            (dt_weight.at[:, :, own], dtw.at[:, pl.ds(0, dt_weight.shape[1])]),
            (conv_weight.at[:, :, own], conv_w),
            (far_inputs[9], hid_in),
            (far_inputs[10], out_in),
            (far_inputs[11], xs_in),
            (skip_all.at[:, own], skip),
        ]
        return [pltpu.make_async_copy(a, b, local_sems.at[i]) for i, (a, b) in enumerate(pairs)]

    def results():
        pairs = []
        for d in range(2):
            buf = parts_a[d][2]
            pairs += [(buf.at[q], a_ref.at[d, :, :, :, pl.ds(q * chans, chans)]) for q in range(4)]
        pairs += [(parts_x[0][2], x0_ref), (parts_x[1][2], x1_ref), (part_c[2], cv_ref)]
        return [pltpu.make_async_copy(a, b, result_sems.at[i]) for i, (a, b) in enumerate(pairs)]

    near = [(outs, k) for k in range(n)] + [(zs, k) for k in range(n)]
    start_at = [0, 0, 1, 3, 4, 6, 7, 8]
    pair_at = [4, 5, 6, 7, 8, 8, 8, 8]

    def step_of(plan, i):
        return plan[i * 8 // (2 * n)]

    unit = 2 * blocks // 8

    @pl.when(j == 0)
    def _():
        greet_all(turn.greet())
        seq1.start()
        for copy in loads():
            copy.start()
        loads()[12].wait()
        for d in range(2):
            dc[d, :16, :] = jnp.zeros((16, chans), F32)
            dc[d, total + 16 :, :] = jnp.zeros((16, chans), F32)
        xpad[:16, :] = jnp.zeros((16, chans), BF)
        xpad[total + 16 :, :] = jnp.zeros((16, chans), BF)
        dtw[:, dt_weight.shape[1] :, :] = jnp.zeros((2, 128 - dt_weight.shape[1], chans), BF)
        dalog[...] = jnp.zeros_like(dalog)
        sums[...] = jnp.zeros_like(sums)
        conv_acc[...] = jnp.zeros_like(conv_acc)

    for i, (scatter, k) in enumerate(near):
        if step_of(pair_at, i) < 8:
            pl.when(j == unit * step_of(pair_at, i))(functools.partial(scatter.pair, k))
        if step_of(start_at, i) < 8:
            pl.when(j == unit * step_of(start_at, i))(scatter.near_copy(k).start)

    @pl.when(j == 2 * unit)
    def _():
        loads()[9].wait()
        seq1.cross()

    @pl.when(j == 3 * unit)
    def _():
        loads()[10].wait()
        loads()[11].wait()


    @pl.when(j == 5 * unit)
    def _():
        branch = seq1.finish()
        result[...] = (tok[...].astype(F32) + gate[...] * branch).astype(BF)
        gate_row[...] = jnp.sum(cot[...].astype(F32) * branch, axis=0, keepdims=True)

    @pl.when(lax.rem(j, blocks) == 0)
    def _():
        g_sc[...] = jnp.zeros_like(g_sc)

    def run(rev):
        d = int(rev)
        block = j - blocks if rev else blocks - 1 - j
        base = pl.multiple_of(block * length, length)
        here = pl.ds(base, length)
        backward_block(
            rev, dl.at[0], act.at[d, here], coef.at[0], a2.at[d],
            proj.at[d, here], dy.at[here], skip.at[pl.ds(d, 1)], hp.at[0], dpre.at[d, here],
            dc.at[d, pl.ds(pl.multiple_of(base + 16, 16), length)], dflow.at[d, block], dalog.at[d],
            sums.at[d], g_sc, ((g_a, q_a), (g_b, q_b)), (r0, r1, r2), red,
        )

    pl.when(j < blocks)(lambda: run(False))
    pl.when(j >= blocks)(lambda: run(True))

    @pl.when(j == 2 * blocks - 1)
    def _():
        late = [i for i in range(2 * n) if step_of(start_at, i) >= 8]
        for i in late:
            near[i][0].near_copy(near[i][1]).start()
        for copy in loads()[:9]:
            copy.wait()
        for d in range(2):
            value = dot_nt(dpre[d], dtw[d])
            for b in range(blocks):
                at = slice(b * length, (b + 1) * length)
                square = jnp.concatenate(
                    [jnp.zeros((128 - 2 * STATE, length), F32), dflow[d, b], dread[d, b]], axis=0
                )
                c7.x[d, at] = value[at] + square.T
        c7.start()
        late = [i for i in range(2 * n) if step_of(pair_at, i) >= 8]
        quarter = len(late) // 4
        rank = 128 - 2 * STATE
        per_d = 128 // n_dp
        for d in range(2):
            source, scatter, _, _ = parts_a[d]
            lines = dot_tn(proj[d].astype(BF), dpre[d])[:rank]
            extra = [jnp.sum(sums[d, i], axis=0, keepdims=True) for i in range(2)]
            lines = jnp.concatenate(
                [lines, dalog[d] * (a2[d] * LN2)] + extra + [jnp.zeros((STATE - 2, chans), F32)], axis=0
            ).astype(BF)
            for b in range(n_dp):
                source[b] = lines[b * per_d : (b + 1) * per_d]
            scatter.start()
        c7.cross()
        for i in late[:quarter]:
            near[i][0].pair(near[i][1])
        for _, scatter, _, _ in parts_a:
            for k in range(n):
                scatter.pair(k)
        c7.back()
        for i in late[quarter : 2 * quarter]:
            near[i][0].pair(near[i][1])
        c7.finish()

        rows_x = chans // n_dp
        for d in range(2):
            dproj = c7.total[d].astype(BF)
            source, scatter, _, _ = parts_x[d]
            grad = dot_tn(act[d], dproj).astype(BF)
            for b in range(n_dp):
                source[b] = grad[b * rows_x : (b + 1) * rows_x]
            scatter.start()

            def act_rows(c, carry, d=d):
                at = pl.ds(pl.multiple_of(c * 128, 128), 128)
                shifted = pl.ds(pl.multiple_of(c * 128 + 16, 16), 128)
                value = dot_nt(c7.total[d, at].astype(BF), xproj[d]) + dc[d, shifted]
                dc[d, shifted] = value * slope[d, at].astype(F32)
                return carry

            lax.fori_loop(0, total // 128, act_rows, 0)

        step = 32

        def conv_rows(c, carry):
            base = pl.multiple_of(c * step, step)
            window = pl.ds(base, step + 32)
            x_w = xpad[window, :].astype(F32)
            grad = jnp.zeros((step, chans), F32)
            for d in range(2):
                d_w = dc[d, window]
                here = d_w[16 : 16 + step]
                conv_acc[5 * d + 4] += rows_in_eights(here)
                for tap in range(4):
                    off = tap - 3 if d == 0 else 3 - tap
                    conv_acc[5 * d + tap] += rows_in_eights(here * x_w[16 + off : 16 + off + step])
                    grad = grad + conv_w[d, tap : tap + 1] * d_w[16 - off : 16 - off + step]
            dxin[pl.ds(base, step), :] = grad.astype(BF)
            return carry

        lax.fori_loop(0, total // step, conv_rows, 0)
        for i in late[2 * quarter :]:
            near[i][0].pair(near[i][1])

        rb = width // (4 * n_dp)
        half = n_dp // 2
        for h in range(2):
            cols = slice(h * width // 2, (h + 1) * width // 2)
            grad = dot_tn(hidden[:, cols], dxin[...]).astype(BF)
            for b in range(half):
                for q in range(4):
                    first = (4 * b + q) * rb
                    xs_in[h * half + b, q] = grad[first : first + rb]
        xs.start()
        for _, scatter, buf, spread in parts_a:
            buf[spread.place] = scatter.finish().astype(BF)
            spread.go_z()
        seg = tok.shape[0]
        for h in range(2):
            cols = slice(h * width // 2, (h + 1) * width // 2)
            grad = (dot_nt(dxin[...], w_x[cols, :]) + dot_nt(grad_z[...], w_z[cols, :])).astype(BF)
            for q in range(4):
                hid_in[q, :, cols] = grad[q * seg : (q + 1) * seg]
        seq2.start()
        for _, scatter, _, _ in parts_x:
            for k in range(n):
                scatter.pair(k)
        source, scatter, _, _ = part_c
        conv_lines = [jnp.sum(conv_acc[i], axis=0, keepdims=True) for i in range(10)]
        conv_lines = jnp.concatenate(conv_lines + [jnp.zeros((6, chans), F32)], axis=0)
        for b in range(n_dp):
            source[b, :, :rows_x] = conv_lines[:, b * rows_x : (b + 1) * rows_x].astype(BF)
            source[b, :, rows_x:] = jnp.zeros((16, 128 - rows_x), BF)
        scatter.start()
        seq2.cross()
        out_red[...] = outs.finish().astype(BF)
        turn.start()
        for _, _, _, spread in parts_a:
            spread.go_y()
        z_red[...] = zs.finish().astype(BF)
        for k in range(n):
            part_c[1].pair(k)
        for _, scatter, buf, spread in parts_x:
            buf[spread.place] = scatter.finish().astype(BF)
            spread.go_z()

        grad = seq2.finish()
        z_swap.start()
        for _, _, _, spread in parts_a:
            spread.go_x()
        tokens = tok[...].astype(F32)
        centred = tokens - jnp.mean(tokens, axis=1, keepdims=True)
        inv_std = lax.rsqrt(jnp.mean(centred * centred, axis=1, keepdims=True) + epsilon)
        normed = centred * inv_std
        grad_normed = grad * (1.0 + scale[...])
        inner_product = jnp.mean(grad_normed * normed, axis=1, keepdims=True)
        tokg[...] = (
            cot[...].astype(F32)
            + inv_std
            * (grad_normed - jnp.mean(grad_normed, axis=1, keepdims=True) - normed * inner_product)
        ).astype(BF)
        row[:, :width] = jnp.sum(grad, axis=0, keepdims=True)
        row[:, width : 2 * width] = jnp.sum(grad * normed, axis=0, keepdims=True)
        row[:, 2 * width : 3 * width] = gate_row[...]
        row[:, 3 * width :] = jnp.sum(grad * flags[...], axis=0, keepdims=True)
        pair = (row_sems.at[0], row_sems.at[1])
        row_copies = [
            remote(row, rows_in.at[k], pair, k, {"seq": other})
            for k, other in enumerate(seq_others())
        ]
        for copy in row_copies:
            copy.start()
        source, scatter, buf, spread_c = part_c
        buf[spread_c.place] = scatter.finish().astype(BF)
        spread_c.go_z()
        for k in range(n // 2):
            xs.pair(k)
        for copy in row_copies:
            copy.wait()
        table[d_index] = row[...] + rows_in[1] + (rows_in[0] + rows_in[2])
        pair = (table_sems.at[0], table_sems.at[1])
        table_copies = [
            remote(table.at[d_index], table.at[d_index], pair, k, {"dp": other})
            for k, other in enumerate(dp_others())
        ]
        for copy in table_copies:
            copy.start()
        spreads_x = [item[3] for item in parts_x] + [spread_c]
        for spread in spreads_x:
            spread.go_y()
        for _, _, _, spread in parts_a:
            spread.go_sib()
        for k in range(n // 2, n - 1):
            xs.pair(k)
        for spread in spreads_x:
            spread.go_x()
        xs.pair(n - 1)
        turn.finish()
        out_ref[...] = out_got[...]
        z_swap.finish()
        for q in range(4):
            in_ref[:, (4 + q) * chans : (5 + q) * chans] = z_got[q]
        for spread in spreads_x:
            spread.go_sib()
        for (_, _, buf, spread), d in zip(parts_a, range(2)):
            spread.finish()
            for copy in results()[4 * d : 4 * d + 4]:
                copy.start()
        for copy in table_copies:
            copy.wait()
        table_ref[...] = table[...]
        x_red[...] = xs.finish().astype(BF)
        x_swap.start()
        for spread in spreads_x:
            spread.finish()
        for copy in results()[8:]:
            copy.start()
        x_swap.finish()
        for q in range(4):
            in_ref[:, q * chans : (q + 1) * chans] = x_got[q]
        for copy in results():
            copy.wait()


def scan_backward(
    dl, hp, proj, act, coef, a2, dy, dread, branch, out_part, z_part,
    tok, cot, gate, scale, flags, slope, xin, hidden, grad_z, in_weight, xproj_weight, dt_weight, conv_weight, skip,
    collective_id, tile,
):
    total, chans = dy.shape
    blocks = total // tile
    n_dp = out_part.shape[0]
    n = n_dp // 2
    rows, width = tok.shape
    rb = width // (4 * n_dp)
    rows_x = chans // n_dp
    per_d = 128 // n_dp

    def place(j):
        d = j // blocks
        b = lax.rem(j, blocks)
        return d, blocks - 1 - b + d * (2 * b - blocks + 1)

    def tokens_of(j):
        d, b = place(j)
        return d, b, 0

    def cells(j):
        d, b = place(j)
        return d, b, 0, 0

    any_spec = pl.BlockSpec(memory_space=pl.ANY)
    in_specs = (
        [
            pl.BlockSpec((1, tile, chans), tokens_of),
            pl.BlockSpec((1, tile * STATE, chans), tokens_of),
        ]
        + [VMEM_SPEC] * 2
        + [pl.BlockSpec((1, tile // U, 2 * STATE, U), cells)]
        + [VMEM_SPEC] * 8
        + [any_spec] * 12
    )
    shape = jax.ShapeDtypeStruct
    in_out = (4, n, 2)
    out_shape = [
        shape((rows, width), BF),
        shape((rows, width), BF),
        shape((rb, 8 * chans), BF),
        shape(out_part.shape[1:], BF),
        shape((2, n, 2, per_d, 4 * chans), BF),
        shape(in_out + (rows_x, 128), BF),
        shape(in_out + (rows_x, 128), BF),
        shape(in_out + (16, 128), BF),
        shape((n_dp, 1, 4 * width), F32),
    ]
    dma = pltpu.SemaphoreType.DMA
    vmem = pltpu.VMEM
    scratch = [
        vmem((STATE, chans), F32),
        vmem((U * STATE, chans), BF),
        vmem((U * STATE, chans), BF),
        vmem((U * 8, chans), BF),
        vmem((U * 8, chans), BF),
    ]
    scratch += [vmem((U, chans), F32)] * 3 + [vmem((U, STATE, 128), F32)]
    scratch += [
        vmem((2, total, chans), BF),
        vmem((2, total + 32, chans), F32),
        vmem((2, blocks, STATE, tile), F32),
        vmem((2, STATE, chans), F32),
        vmem((2, 2, U, chans), F32),
    ]
    scratch += [
        vmem(slope.shape, BF),
        vmem((total + 32, chans), BF),
        vmem(hidden.shape, BF),
        vmem(grad_z.shape, BF),
        vmem((width, chans), BF),
        vmem((width, chans), BF),
        vmem((2, chans, 128), BF),
        vmem((2, 128, chans), BF),
        vmem((2, 4, chans), F32),
        vmem((2, chans), F32),
        vmem((4, rows, width), BF),
        vmem(out_part.shape, BF),
        vmem(z_part.shape, BF),
        dma((13,)),
    ]
    scratch += [
        vmem((10, 8, chans), F32),
        vmem((total, chans), BF),
        vmem((1, width), F32),
    ]
    scratch += SeqScatter.scratch(rows, width)
    scratch += DpScatter.scratch(n_dp, out_part.shape[1:]) + DpScatter.scratch(n_dp, z_part.shape[1:])
    scratch += [vmem(out_part.shape[1:], BF)] * 2 + [dma((2, 1))]
    scratch += [vmem(z_part.shape[1:], BF)] * 2 + [dma((2, 3))]
    scratch += SeqReduce.scratch(total, 128)
    for block in [(per_d, chans)] * 2 + [(rows_x, 128)] * 2 + [(16, 128)]:
        scratch += [vmem((n_dp,) + block, BF)] + DpScatter.scratch(n_dp, block)
        scratch += Spread.scratch(n_dp, block)
    scratch += SeqScatter.scratch(rows, width)
    scratch += DpScatter.scratch(n_dp, z_part.shape[1:])
    scratch += [vmem(z_part.shape[1:], BF)] * 2 + [dma((2, 3))]
    scratch += [
        vmem((1, 4 * width), F32),
        vmem((3, 1, 4 * width), F32),
        dma((2, 3)),
        vmem((n_dp, 1, 4 * width), F32),
        dma((2, n_dp)),
        dma((11,)),
    ]
    return pl.pallas_call(
        backward_kernel,
        grid=(2 * blocks,),
        in_specs=in_specs,
        out_specs=[VMEM_SPEC] * 4 + [any_spec] * 4 + [VMEM_SPEC],
        out_shape=out_shape,
        scratch_shapes=scratch,
        compiler_params=comm_params(collective_id, 62),
        name="scan_backward",
    )(
        dl, hp, proj, act, coef, a2, dy, dread, tok, cot, gate, scale, flags, slope, xin, hidden,
        grad_z, in_weight, xproj_weight, dt_weight, conv_weight, skip, branch, out_part,
        z_part,
    )


def time_embedding(step_ids, model_width):
    halfway = model_width // 2
    frequency = jnp.exp(-math.log(10000.0) * jnp.arange(halfway, dtype=jnp.float32) / halfway)
    angles = step_ids.astype(jnp.float32)[:, None] * frequency[None, :]
    return jnp.concatenate([jnp.cos(angles), jnp.sin(angles)], axis=1)


def silu_slope(values):
    sigma = jax.nn.sigmoid(values)
    return sigma * (1.0 + values * (1.0 - sigma))


def shards(
    tokens,
    cotangent,
    timesteps,
    grid_widths,
    scan_path,
    ada_weight,
    ada_bias,
    edge,
    in_weight,
    conv_weight,
    conv_bias,
    xproj_weight,
    dt_weight,
    dt_bias,
    a_log,
    skip,
    out_weight,
):
    seg_len, width = tokens.shape[1:]
    inner = in_weight.shape[1] // 2
    rank = dt_weight.shape[1]
    taps = conv_weight.shape[1]
    rim = taps - 1
    columns = ada_weight.shape[1]
    n_seq = lax.axis_size("seq")
    n_dp = lax.axis_size("dp")
    dp_index = lax.axis_index("dp")
    seq_index = lax.axis_index("seq")
    length = seg_len * n_seq
    chans = inner // n_seq

    def flags_of(item):
        return (jnp.remainder(item, grid_widths[0]) == grid_widths[0] - 1).astype(F32)

    embedded = jax.nn.silu(time_embedding(timesteps, width)).astype(BF)
    own_flags = flags_of(scan_path)
    hidden, grad_branch, xin, act, slope, proj, dy, silu_z, slope_z, modulation, decay2 = first_part(
        tokens[0], cotangent[0], jnp.broadcast_to(own_flags, (8, seg_len)), embedded, ada_bias[None],
        edge[None], in_weight, out_weight, conv_weight, conv_bias, xproj_weight, ada_weight.T,
        jnp.swapaxes(a_log, 1, 2), 0,
    )
    scale_term = modulation[:, width : 2 * width]
    gate_term = modulation[:, 2 * width :]
    tile = 128 if n_dp <= 8 else 32
    coef = jnp.swapaxes(proj[:, :, 128 - 2 * STATE :].reshape(2, length // U, U, 2 * STATE), 2, 3)
    held, delta, dread, branch, out_part, z_part, grad_z = scan_forward(
        seq_index.astype(jnp.int32)[None], proj, act, coef, dt_weight, dt_bias, decay2,
        skip, dy, silu_z, slope_z, hidden, grad_branch, out_weight, tile,
    )
    total = n_dp * n_seq

    def in_blocks(grad):
        return grad.reshape(n_dp, n_seq, width // total, chans)

    result, grad_tok, in_rows, out_rows, lines, x0, x1, conv_lines, table = scan_backward(
        delta, held, proj, act, coef, decay2, dy, dread,
        branch.reshape(n_seq, seg_len, width),
        out_part.reshape(n_dp, chans // n_dp, width),
        in_blocks(z_part),
        tokens[0], cotangent[0], gate_term, scale_term, own_flags[0][:, None],
        slope, xin, hidden, grad_z, in_weight, xproj_weight, dt_weight, conv_weight, skip,
        2, tile,
    )
    table = table.reshape(n_dp, -1)
    edge_grad = jnp.sum(table[:, 3 * width :], axis=0)
    mod_columns = lax.dynamic_slice_in_dim(table[:, : 3 * width], dp_index * columns, columns, 1)
    ada_b_grad = jnp.sum(mod_columns, axis=0)
    ada_w_grad = jnp.dot(embedded.astype(F32).T, mod_columns, precision=highest)
    lines = lines.reshape(2, 128, inner).astype(F32)
    alog_grad = jnp.swapaxes(lines[:, rank : rank + STATE], 1, 2)
    xproj_grad = jnp.stack([item.reshape(inner, 128) for item in (x0, x1)]).astype(F32)
    conv_lines = jnp.moveaxis(conv_lines[..., : chans // n_dp], 3, 0).reshape(16, inner).astype(F32)
    conv_lines = conv_lines[: 2 * (taps + 1)].reshape(2, taps + 1, inner)
    return (
        result[None],
        grad_tok[None],
        ada_w_grad,
        ada_b_grad,
        edge_grad,
        in_rows.astype(F32),
        conv_lines[:, :taps],
        conv_lines[:, taps],
        xproj_grad,
        lines[:, :rank],
        lines[:, rank + STATE],
        alog_grad,
        lines[:, rank + STATE + 1],
        out_rows.astype(F32),
    )


def solution(mesh):
    in_specs = (
        P("dp", "seq", None),
        P("dp", "seq", None),
        P(),
        P("dp"),
        P("dp", "seq"),
        P(None, "dp"),
        P("dp"),
        P(),
        P(),
        P(),
        P(),
        P(),
        P(),
        P(),
        P(),
        P(),
        P(),
    )
    out_specs = (
        P("dp", "seq", None),
        P("dp", "seq", None),
        P(None, "dp"),
        P("dp"),
        P(),
        P(("dp", "seq"), None),
        P(),
        P(),
        P(),
        P(),
        P(),
        P(),
        P(),
        P(("dp", "seq"), None),
    )
    return jax.shard_map(shards, mesh=mesh, in_specs=in_specs, out_specs=out_specs, check_vma=False)
```

```python
import functools
import math

import jax
import jax.numpy as jnp
from jax import lax
from jax.experimental import pallas as pl
from jax.experimental.pallas import tpu as pltpu
from jax.sharding import PartitionSpec as P

STATE = 16
U = 16
PARTS = 3
LOG2E = 1.4426950408889634
LN2 = 0.6931471805599453
F32 = jnp.float32
BF = jnp.bfloat16
epsilon = 1e-06
highest = lax.Precision.HIGHEST
MESH = pl.DeviceIdType.MESH
VMEM_SPEC = pl.BlockSpec(memory_space=pltpu.VMEM)


def iota(shape, dim):
    return lax.broadcasted_iota(jnp.int32, shape, dim)


def dot(a, b):
    return lax.dot_general(a, b, (((1,), (0,)), ((), ())), preferred_element_type=F32)


def dot_nt(a, b):
    return lax.dot_general(a, b, (((1,), (1,)), ((), ())), preferred_element_type=F32)


def dot_tn(a, b):
    return lax.dot_general(a, b, (((0,), (0,)), ((), ())), preferred_element_type=F32)


def softplus(x):
    return jnp.maximum(x, 0.0) + jnp.log1p(jnp.exp(-jnp.abs(x)))


def diag_of(rows, first):
    k = U * STATE
    pick = (iota((128, k), 0) - first == lax.rem(iota((128, k), 1), STATE)).astype(F32).astype(BF)
    keep = (iota((U, k), 1) // STATE == iota((U, k), 0)).astype(F32)
    return (dot(rows.astype(BF), pick) * keep).astype(BF)


def over_lanes(x, t):
    return jnp.broadcast_to(x[:, t : t + 1], (x.shape[0], 128))


def wide(x, n):
    return jnp.concatenate([x] * n, axis=1)


def lane_fold(x):
    acc = x[:, :128]
    for j in range(1, x.shape[1] // 128):
        acc = acc + x[:, 128 * j : 128 * (j + 1)]
    return acc


def interleave(steps, pieces):
    done = 0
    for i, step in enumerate(steps):
        step()
        while done < (i + 1) * len(pieces) // len(steps):
            pieces[done]()
            done += 1


def pipeline(groups, work, drain):
    interleave(work(0, 0), [])

    def two(p, carry):
        interleave(work(2 * p + 1, 1), drain(2 * p, 0))
        interleave(work(2 * p + 2, 0), drain(2 * p + 1, 1))
        return carry

    lax.fori_loop(0, groups // 2 - 1, two, 0)
    interleave(work(groups - 1, 1), drain(groups - 2, 0))
    interleave([lambda: None], drain(groups - 1, 1))


def forward_block(rev, dl, act, coef, a2, proj, dy, hp, put_y, dread, h_sc, hb_sc, slots, rows, red):
    length, chans = dl.shape
    groups = length // U
    part_width = chans // PARTS
    dlu, duu, dyu = rows
    dread[...] = jnp.zeros_like(dread)

    def place(k):
        return (groups - 1 - k) if rev else k

    def work(k, slot):
        g = place(k)
        t0 = pl.multiple_of(g * U, U)
        at = pl.ds(t0, U)
        dlu[...] = dl[at, :]
        duu[...] = dl[at, :] * act[at, :].astype(F32)
        dyu[...] = dy[at, :]
        inflow = coef[g][:STATE]
        spread = [over_lanes(inflow, t) for t in range(U)]
        hbuf = slots[slot]
        v = {}

        def token(part, i):
            col = pl.ds(part * part_width, part_width)
            if i == 0:
                v["a"], v["h"], v["hb"] = a2[:, col], h_sc[:, col], hb_sc[:, col]
            loc = (U - 1 - i) if rev else i
            one = pl.ds(loc, 1)
            h = jnp.exp2(dlu[one, col] * v["a"]) * v["h"] + duu[one, col] * wide(
                spread[loc], part_width // 128
            )
            hp[pl.ds(pl.multiple_of((t0 + loc) * STATE, STATE), STATE), col] = v["hb"]
            hb = h.astype(BF)
            hbuf[pl.ds(loc * STATE, STATE), col] = hb
            v["h"], v["hb"] = h, hb
            total = lane_fold(dyu[one, col] * h)
            if part:
                total = red[loc] + total
            if part < PARTS - 1:
                red[loc] = total
            else:
                here = iota(dread.shape, 1) == g * U + loc
                v["sum"] = jnp.where(here, jnp.sum(total, axis=1, keepdims=True), v.get("sum", 0.0))
                if i == U - 1:
                    dread[...] += v["sum"]
            if i == U - 1:
                h_sc[:, col] = h
                hb_sc[:, col] = hb

        return [functools.partial(token, part, i) for part in range(PARTS) for i in range(U)]

    def drain(k, slot):
        at = pl.ds(pl.multiple_of(place(k) * U, U), U)
        hbuf = slots[slot]
        v = {}

        def first():
            v["c"] = diag_of(proj[at, :], 128 - STATE)

        def out(c):
            col = pl.ds(256 * c, 256)
            put_y(at, col, dot(v["c"], hbuf[:, col]))

        return [first] + [functools.partial(out, c) for c in range(chans // 256)]

    pipeline(groups, work, drain)


def backward_block(
    rev, dl, act, coef, a2, proj, dy, skip, hp, dpre, dact, dflow, dalog, sums, g_sc, slots, rows, red
):
    length, chans = dl.shape
    groups = length // U
    part_width = chans // PARTS
    dlu, duu, dyu = rows
    dflow[...] = jnp.zeros_like(dflow)

    def place(k):
        return k if rev else (groups - 1 - k)

    def work(k, slot):
        g = place(k)
        t0 = pl.multiple_of(g * U, U)
        at = pl.ds(t0, U)
        dlu[...] = dl[at, :]
        duu[...] = dl[at, :] * act[at, :].astype(F32)
        dyu[...] = dy[at, :]
        readout = coef[g][STATE:]
        spread = [over_lanes(readout, t) for t in range(U)]
        gbuf, qbuf = slots[slot]
        v = {}

        def token(part, i):
            col = pl.ds(part * part_width, part_width)
            if i == 0:
                v["a"], v["car"], v["acc"] = a2[:, col], g_sc[:, col], dalog[:, col]
            loc = i if rev else (U - 1 - i)
            one = pl.ds(loc, 1)
            step = dlu[one, col]
            g_t = dyu[one, col] * wide(spread[loc], part_width // 128) + v["car"]
            car = jnp.exp2(step * v["a"]) * g_t
            before = hp[pl.ds(pl.multiple_of((t0 + loc) * STATE, STATE), STATE), col].astype(F32)
            q = car * before
            v["acc"] = v["acc"] + q * step
            v["car"] = car
            gbuf[pl.ds(loc * STATE, STATE), col] = g_t.astype(BF)
            total = lane_fold(duu[one, col] * g_t)
            if part:
                total = red[loc] + total
            if part < PARTS - 1:
                red[loc] = total
            else:
                here = iota(dflow.shape, 1) == g * U + loc
                v["sum"] = jnp.where(here, jnp.sum(total, axis=1, keepdims=True), v.get("sum", 0.0))
                if i == U - 1:
                    dflow[...] += v["sum"]
            qa = q * v["a"]
            qa = qa[:8] + qa[8:]
            if i % 2 == 0:
                v["held"] = qa
            else:
                pair = [v["held"], qa] if rev else [qa, v["held"]]
                qbuf[pl.ds((loc // 2) * STATE, STATE), col] = jnp.concatenate(pair, 0).astype(BF)
            if i == U - 1:
                g_sc[:, col] = v["car"]
                dalog[:, col] = v["acc"]

        return [functools.partial(token, part, i) for part in range(PARTS) for i in range(U)]

    def drain(k, slot):
        at = pl.ds(pl.multiple_of(place(k) * U, U), U)
        gbuf, qbuf = slots[slot]
        v = {}

        def first():
            v["b"] = diag_of(proj[at, :], 128 - 2 * STATE)
            v["ones"] = (iota((U, U * 8), 1) // 8 == iota((U, U * 8), 0)).astype(F32).astype(BF)

        def cols(c):
            col = pl.ds(256 * c, 256)
            s = dot(v["b"], gbuf[:, col])
            q = dot(v["ones"], qbuf[:, col]) * LN2
            a = act[at, col].astype(F32)
            step = dl[at, col]
            grad = dy[at, col]
            pre = ((q + a * s) * (1.0 - jnp.exp(-step))).astype(BF)
            dpre[at, col] = pre
            dact[at, col] = step * s + skip[:, col] * grad
            sums[0, :, col] += pre.astype(F32)
            sums[1, :, col] += grad * a

        return [first] + [functools.partial(cols, c) for c in range(chans // 256)]

    pipeline(groups, work, drain)


def forward_kernel(
    s_ref, proj, act, coef, dtw, dtb, a2, skip, dy, silu_z, slope_z, hidden, w_out,
    hp, dl, dread, branch, sorted_gated, z_part, grad_z,
    y, h_sc, hb_sc, h_a, h_b, r0, r1, r2, red, gated,
):
    j = pl.program_id(0)
    blocks = pl.num_programs(0) // 2
    length, chans = dl.shape[1:]
    n_dp = lax.axis_size("dp")

    @pl.when(lax.rem(j, blocks) == 0)
    def _():
        h_sc[...] = jnp.zeros_like(h_sc)
        hb_sc[...] = jnp.zeros_like(hb_sc)

    def run(rev):
        own = slice(int(rev), int(rev) + 1)
        pre = dot(proj[0][:, : dtw.shape[1]].astype(BF), dtw[0]) + dtb[own]
        dl[0] = softplus(pre)
        base = (2 * blocks - 1 - j if rev else j) * length
        dy_block = dy.at[pl.ds(pl.multiple_of(base, length), length)]

        def put_y(at, col, value):
            value = value + skip[own, col] * act[0, at, col].astype(F32)
            rows = pl.ds(pl.multiple_of(base + at.start, U), U)
            if rev:
                value = value + y[rows, col]
            y[rows, col] = value

        forward_block(
            rev, dl.at[0], act.at[0], coef.at[0], a2.at[0], proj.at[0], dy_block, hp.at[0], put_y,
            dread.at[0, 0], h_sc, hb_sc, (h_a, h_b), (r0, r1, r2), red,
        )

    pl.when(j < blocks)(lambda: run(False))
    pl.when(j >= blocks)(lambda: run(True))

    @pl.when(j == 2 * blocks - 1)
    def _():
        total = y.shape[0]

        def rows_of(c, carry):
            at = pl.ds(pl.multiple_of(c * 64, 64), 64)
            value = y[at, :]
            opened = value * silu_z[at, :]
            gated[at, :] = opened.astype(BF)
            piece = 4 * sorted_gated.shape[2] // n_dp
            for q in range(4):
                pieces = [opened[:, b * piece : (b + 1) * piece] for b in range(q, n_dp, 4)]
                sorted_gated[q, at, :] = jnp.concatenate(pieces, axis=1).astype(BF)
            grad_z[at, :] = (value * slope_z[at, :]).astype(BF)
            return carry

        lax.fori_loop(0, total // 64, rows_of, 0)
        width = w_out.shape[1]

        for c in range(2):
            at = slice(c * total // 2, (c + 1) * total // 2)
            branch[at, :] = dot(gated[at, :], w_out[...]).astype(BF)

        for c in range(2):
            at = slice(c * width // 2, (c + 1) * width // 2)
            z_part[at, :] = dot_tn(hidden[:, at], grad_z[...]).astype(BF)


def scan_forward(
    seq_index, proj, act, coef, dtw, dtb, a2, skip, dy, silu_z, slope_z, hidden, w_out, tile
):
    total, chans = dy.shape
    width = w_out.shape[1]
    blocks = total // tile

    def place(j):
        d = j // blocks
        b = lax.rem(j, blocks)
        return d, b + d * (blocks - 1 - 2 * b)

    def tokens_of(j, s):
        d, b = place(j)
        return d, b, 0

    def direction_of(j, s):
        return j // blocks, 0, 0

    def channels_of(j, s):
        return j // blocks, 0, s[0]

    def cells(j, s):
        d, b = place(j)
        return d, b, 0, 0

    whole = VMEM_SPEC
    in_specs = [
        pl.BlockSpec((1, tile, 128), tokens_of),
        pl.BlockSpec((1, tile, chans), tokens_of),
        pl.BlockSpec((1, tile // U, 2 * STATE, U), cells),
        pl.BlockSpec((1, dtw.shape[1], chans), channels_of),
        pl.BlockSpec((2, chans), lambda j, s: (0, s[0])),
        pl.BlockSpec((1, STATE, chans), direction_of),
        pl.BlockSpec((2, chans), lambda j, s: (0, s[0])),
    ] + [whole] * 4
    in_specs += [pl.BlockSpec((chans, width), lambda j, s: (s[0], 0))]
    out_specs = [
        pl.BlockSpec((1, tile * STATE, chans), tokens_of),
        pl.BlockSpec((1, tile, chans), tokens_of),
        pl.BlockSpec((1, 1, STATE, tile), cells),
    ] + [whole] * 4
    out_shape = [
        jax.ShapeDtypeStruct((2, total * STATE, chans), BF),
        jax.ShapeDtypeStruct((2, total, chans), F32),
        jax.ShapeDtypeStruct((2, blocks, STATE, tile), F32),
        jax.ShapeDtypeStruct((total, width), BF),
        jax.ShapeDtypeStruct((4, total, chans // 4), BF),
        jax.ShapeDtypeStruct((width, chans), BF),
        jax.ShapeDtypeStruct((total, chans), BF),
    ]
    return pl.pallas_call(
        forward_kernel,
        grid_spec=pltpu.PrefetchScalarGridSpec(
            num_scalar_prefetch=1,
            grid=(2 * blocks,),
            in_specs=in_specs,
            out_specs=out_specs,
            scratch_shapes=[
                pltpu.VMEM((total, chans), F32),
                pltpu.VMEM((STATE, chans), F32),
                pltpu.VMEM((STATE, chans), BF),
                pltpu.VMEM((U * STATE, chans), BF),
                pltpu.VMEM((U * STATE, chans), BF),
            ]
            + [pltpu.VMEM((U, chans), F32)] * 3
            + [pltpu.VMEM((U, STATE, 128), F32), pltpu.VMEM((total, chans), BF)],
        ),
        out_shape=out_shape,
        compiler_params=pltpu.CompilerParams(vmem_limit_bytes=60 << 20),
        name="scan_forward",
    )(seq_index, proj, act, coef, dtw, dtb, a2, skip, dy, silu_z, slope_z, hidden, w_out)


def sibling_of(s):
    return s + 1 - 2 * lax.rem(s, 2)


def across_of(s):
    return lax.rem(s + 2, 4)


def remote(src, dst, sems, slot, peer):
    return pltpu.make_async_remote_copy(
        src_ref=src,
        dst_ref=dst,
        send_sem=sems[0].at[slot],
        recv_sem=sems[1].at[slot],
        device_id=peer,
        device_id_type=MESH,
    )


def greet(peers):
    barrier = pltpu.get_barrier_semaphore()
    for peer in peers:
        pl.semaphore_signal(barrier, inc=1, device_id=peer, device_id_type=MESH)
    pl.semaphore_wait(barrier, len(peers))


def comm_params(collective_id, mib=48):
    return pltpu.CompilerParams(
        collective_id=collective_id, has_side_effects=True, vmem_limit_bytes=mib << 20
    )


class DpScatter:
    def __init__(self, x, got, acc, far, sems, out=None):
        self.x, self.got, self.acc, self.far = x, got, acc, far
        self.out = x if out is None else out
        self.sems = sems
        d = lax.axis_index("dp")
        n = lax.axis_size("dp") // 2
        self.n = n
        self.y = lax.rem(d, 2)
        self.z = d // 2
        self.order = sorted(range(n), key=lambda m: (m & -m or n, -m))

    def flipped(self, mask):
        z = self.z
        for bit in range(mask.bit_length()):
            if mask >> bit & 1:
                z = z + 2**bit * (1 - 2 * lax.rem(self.z // 2**bit, 2))
        return z

    @staticmethod
    def scratch(n_dp, block):
        n = n_dp // 2
        dma = pltpu.SemaphoreType.DMA
        return [pltpu.VMEM((n,) + block, BF)] * 3 + [dma((4, n))]

    def near_copy(self, k):
        z = self.flipped(self.order[k])
        return pltpu.make_async_remote_copy(
            src_ref=self.out.at[2 * z + 1 - self.y],
            dst_ref=self.got.at[k],
            send_sem=self.sems.at[0, k],
            recv_sem=self.sems.at[1, k],
            device_id={"dp": 2 * self.z + 1 - self.y},
            device_id_type=MESH,
        )

    def far_copy(self, k):
        mask = self.order[k]
        return pltpu.make_async_remote_copy(
            src_ref=self.acc.at[k],
            dst_ref=self.far.at[k],
            send_sem=self.sems.at[2, k],
            recv_sem=self.sems.at[3, k],
            device_id={"dp": 2 * self.flipped(mask & -mask) + self.y},
            device_id_type=MESH,
        )

    def start(self):
        for k in range(self.n):
            self.near_copy(k).start()

    def pair(self, k):
        mask = self.order[k]
        self.near_copy(k).wait()
        z = self.flipped(mask)
        total = self.x[2 * z + self.y].astype(F32) + self.got[k].astype(F32)
        bit = 1
        while mask and bit < mask & -mask:
            other = self.order.index(mask + bit)
            self.far_copy(other).wait()
            total = total + self.far[other].astype(F32)
            bit *= 2
        self.acc[k] = total.astype(BF)
        if mask:
            self.far_copy(k).start()

    def finish(self):
        total = self.acc[self.n - 1].astype(F32)
        bit = 1
        while bit < self.n:
            other = self.order.index(bit)
            self.far_copy(other).wait()
            total = total + self.far[other].astype(F32)
            bit *= 2
        return total


class DpDirect:
    def __init__(self, x, got, acc, far, sems, out=None):
        self.x, self.got, self.acc, self.far = x, got, acc, far
        self.out = x if out is None else out
        self.sems = sems
        d = lax.axis_index("dp")
        n = lax.axis_size("dp") // 2
        self.n = n
        self.y = lax.rem(d, 2)
        self.z = d // 2
        self.order = [lax.rem(self.z + k, n) for k in range(1, n + 1)]

    @staticmethod
    def scratch(n_dp, block):
        n = n_dp // 2
        dma = pltpu.SemaphoreType.DMA
        return [pltpu.VMEM((n,) + block, BF)] * 3 + [dma((4, n))]

    def near_copy(self, k):
        z = self.order[k]
        peer = 2 * self.z + 1 - self.y
        return pltpu.make_async_remote_copy(
            src_ref=self.out.at[2 * z + 1 - self.y],
            dst_ref=self.got.at[z],
            send_sem=self.sems.at[0, k],
            recv_sem=self.sems.at[1, k],
            device_id={"dp": peer},
            device_id_type=MESH,
        )

    def near_arrival(self, k):
        return self.near_copy(k)

    def far_copy(self, k):
        z = self.order[k]
        return pltpu.make_async_remote_copy(
            src_ref=self.acc.at[z],
            dst_ref=self.far.at[k],
            send_sem=self.sems.at[2, k],
            recv_sem=self.sems.at[3, k],
            device_id={"dp": 2 * z + self.y},
            device_id_type=MESH,
        )

    def start(self):
        for k in range(self.n):
            self.near_copy(k).start()

    def pair(self, k):
        z = self.order[k]
        self.near_copy(k).wait()
        self.acc[z] = (self.x[2 * z + self.y].astype(F32) + self.got[z].astype(F32)).astype(BF)
        if k < self.n - 1:
            self.far_copy(k).start()

    def finish(self):
        for k in range(self.n - 1):
            self.far_copy(k).wait()
        total = self.acc[self.z].astype(F32)
        for k in range(self.n - 1):
            total = total + self.far[k].astype(F32)
        return total


class SeqScatter:
    def __init__(self, x, from_sib, to_x, from_x, sems, out=None):
        out = x if out is None else out
        s = lax.axis_index("seq")
        self.s, self.far = s, across_of(s)
        sib = sibling_of(s)
        self.x, self.from_sib, self.to_x, self.from_x = x, from_sib, to_x, from_x
        pair = (sems.at[0], sems.at[1])
        self.first = remote(out.at[across_of(sib)], from_sib.at[0], pair, 0, {"seq": sib})
        self.second = remote(out.at[sib], from_sib.at[1], pair, 1, {"seq": sib})
        self.third = remote(to_x, from_x, pair, 2, {"seq": self.far})

    @staticmethod
    def scratch(rows, width):
        return [
            pltpu.VMEM((2, rows, width), BF),
            pltpu.VMEM((rows, width), BF),
            pltpu.VMEM((rows, width), BF),
            pltpu.SemaphoreType.DMA((2, 3)),
        ]

    def start(self):
        self.first.start()
        self.second.start()

    def cross(self):
        self.first.wait()
        self.to_x[...] = (self.x[self.far].astype(F32) + self.from_sib[0].astype(F32)).astype(BF)
        self.third.start()

    def finish(self):
        self.second.wait()
        self.third.wait()
        return (
            self.x[self.s].astype(F32) + self.from_sib[1].astype(F32) + self.from_x[...].astype(F32)
        )


class SeqSwap:
    def __init__(self, src, dst, sems):
        s = lax.axis_index("seq")
        self.s, self.src, self.dst = s, src, dst
        pair = (sems.at[0], sems.at[1])
        self.copies = [
            remote(src.at[lax.rem(s + k, 4)], dst.at[s], pair, k - 1, {"seq": lax.rem(s + k, 4)})
            for k in (2, 1, 3)
        ]

    def send(self):
        for copy in self.copies:
            copy.start()

    def start(self):
        self.send()
        self.dst[self.s] = self.src[self.s]

    def finish(self):
        for copy in self.copies:
            copy.wait()


def dp_others():
    n = lax.axis_size("dp")
    d = lax.axis_index("dp")
    return [lax.rem(d + k, n) for k in range(1, n)]


def seq_others():
    s = lax.axis_index("seq")
    return [lax.rem(s + k, 4) for k in (1, 2, 3)]


def greet_all():
    greet([{"seq": other} for other in seq_others()] + [{"dp": other} for other in dp_others()])


class Spread:
    def __init__(self, buf, sems):
        d, s = lax.axis_index("dp"), lax.axis_index("seq")
        n = lax.axis_size("dp") // 2
        y, z = lax.rem(d, 2), d // 2
        sib, far = sibling_of(s), across_of(s)
        pair = (sems.at[0], sems.at[1])
        block, column, mine, other = buf.at[s, z, y], buf.at[s, :, y], buf.at[s], buf.at[far]
        self.along_z = [
            remote(block, block, pair, k, {"dp": 2 * lax.rem(z + k + 1, n) + y})
            for k in range(n - 1)
        ]
        self.along_y = remote(column, column, pair, n - 1, {"dp": 2 * z + 1 - y})
        self.along_x = remote(mine, mine, pair, n, {"seq": far})
        self.to_sib = remote(mine, mine, pair, n + 1, {"seq": sib})
        self.forward = remote(other, other, pair, n + 2, {"seq": sib})
        self.place = (s, z, y)

    @staticmethod
    def scratch(n_dp, block):
        n = n_dp // 2
        return [pltpu.VMEM((4, n, 2) + block, BF), pltpu.SemaphoreType.DMA((2, n + 3))]

    def go_z(self):
        for copy in self.along_z:
            copy.start()

    def go_y(self):
        for copy in self.along_z:
            copy.wait()
        self.along_y.start()

    def go_x(self):
        self.along_y.wait()
        self.along_x.start()
        self.to_sib.start()

    def go_sib(self):
        self.along_x.wait()
        self.forward.start()

    def finish(self):
        self.to_sib.wait()
        self.forward.wait()


class SeqReduce:
    def __init__(self, x, total, from_sib, half, from_x, sems):
        s = lax.axis_index("seq")
        self.c = c = lax.rem(s, 2)
        sib, far = sibling_of(s), across_of(s)
        pair = (sems.at[0], sems.at[1])
        self.x, self.total, self.from_sib, self.half, self.from_x = x, total, from_sib, half, from_x
        self.first = remote(x.at[1 - c], from_sib, pair, 0, {"seq": sib})
        self.second = remote(half, from_x, pair, 1, {"seq": far})
        self.third = remote(total.at[c], total.at[c], pair, 2, {"seq": sib})

    @staticmethod
    def scratch(rows, width):
        return (
            [pltpu.VMEM((2, rows, width), F32)] * 2
            + [pltpu.VMEM((rows, width), F32)]
            + [pltpu.VMEM((rows, width), BF)] * 2
            + [pltpu.SemaphoreType.DMA((2, 3))]
        )

    def start(self):
        self.first.start()

    def cross(self):
        self.first.wait()
        self.half[...] = (self.x[self.c] + self.from_sib[...]).astype(BF)
        self.second.start()

    def back(self):
        self.second.wait()
        self.total[self.c] = self.half[...].astype(F32) + self.from_x[...].astype(F32)
        self.third.start()

    def finish(self):
        self.third.wait()


def first_kernel(*refs):
    refs = list(refs)

    def take(count):
        taken = refs[:count]
        del refs[:count]
        return taken

    tok, cot, flag, emb, ada_b, edge = take(6)
    in_weight, out_weight, conv_weight, conv_bias, xproj_weight, ada_weight, a_log = take(7)
    hidden_o, branch_o, xin_o, act_o, slope_o, proj_o, dy_o, silu_o, slope_z_o, mod_o, a2_o = take(11)
    w_x, w_z, w_out, conv_w, conv_b, xproj, ada_w, rates, load_sems = take(9)
    toks, cots, flags, rows_out, rows_in = take(5)
    hidden, grad_branch, xin, z, act, slope, dy, silu_z, slope_z, pad = take(10)
    tok_sems, cot_sems, flag_sems, row_sems, own_sems, store_sems = take(6)
    c3 = SeqReduce(*take(6))
    d, s = lax.axis_index("dp"), lax.axis_index("seq")
    sib, far = sibling_of(s), across_of(s)
    diag = across_of(sib)
    n_dp = lax.axis_size("dp")
    seg, width = tok.shape
    total, chans = xin.shape

    own = pl.ds(pl.multiple_of(s * chans, 128), chans)
    own_z = pl.ds(pl.multiple_of((4 + s) * chans, 128), chans)
    loads = [
        (ada_weight, ada_w),
        (a_log.at[:, :, own], rates),
        (in_weight.at[:, own], w_x),
        (in_weight.at[:, own_z], w_z),
        (conv_weight.at[:, :, own], conv_w),
        (conv_bias.at[:, own], conv_b),
        (xproj_weight.at[:, own], xproj),
        (out_weight.at[own], w_out),
    ]
    loads = [pltpu.make_async_copy(a, b, load_sems.at[i]) for i, (a, b) in enumerate(loads)]
    for copy in loads:
        copy.start()
    greet_all()

    def spread_out(src, dst, sems):
        pair = (sems.at[0], sems.at[1])
        to_far = remote(src, dst.at[s], pair, 0, {"seq": far})
        to_sib = remote(src, dst.at[s], pair, 1, {"seq": sib})
        forward = remote(dst.at[far], dst.at[far], pair, 2, {"seq": sib})
        return to_far, to_sib, forward

    tok_far, tok_sib, tok_forward = spread_out(tok, toks, tok_sems)
    cot_far, cot_sib, cot_forward = spread_out(cot, cots, cot_sems)
    tok_far.start()
    tok_sib.start()
    pair = (flag_sems.at[0], flag_sems.at[1])
    flag_copies = [
        remote(flag, flags.at[s], pair, k, {"seq": other}) for k, other in enumerate(seq_others())
    ]
    for copy in flag_copies:
        copy.start()
    locals_ = [(tok, toks.at[s]), (cot, cots.at[s]), (flag, flags.at[s])]
    locals_ = [pltpu.make_async_copy(a, b, own_sems.at[i]) for i, (a, b) in enumerate(locals_)]
    for copy in locals_:
        copy.start()

    loads[0].wait()
    part = dot_nt(emb[...], ada_w[...]) + ada_b[...]
    columns = part.shape[1]
    for i in range(n_dp):
        rows_out[i] = part[i : i + 1]
    pair = (row_sems.at[0], row_sems.at[1])
    row_copies = [
        remote(rows_out.at[other], rows_in.at[d], pair, k, {"dp": other})
        for k, other in enumerate(dp_others())
    ]
    for copy in row_copies:
        copy.start()
    cot_far.start()
    cot_sib.start()
    rows_in[d] = rows_out[d]
    loads[1].wait()
    for k in range(2):
        a2_o[k] = -LOG2E * jnp.exp(rates[k])
    for copy in row_copies:
        copy.wait()
    for i in range(n_dp):
        mod_o[:, i * columns : (i + 1) * columns] = rows_in[i]
    for copy in flag_copies:
        copy.wait()
    for copy in locals_:
        copy.wait()
    for copy in loads[2:4]:
        copy.wait()

    def project(block):
        at = pl.ds(pl.multiple_of(block * seg, seg), seg)
        tokens = toks[block].astype(F32)
        centred = tokens - jnp.mean(tokens, axis=1, keepdims=True)
        normed = centred * lax.rsqrt(jnp.mean(centred * centred, axis=1, keepdims=True) + epsilon)
        marks = flags[block].T[:, :1]
        hid = normed * (1.0 + mod_o[:, width : 2 * width]) + mod_o[:, :width] + marks * edge[...]
        hid = hid.astype(BF)
        hidden[at, :] = hid
        xin[at, :] = dot(hid, w_x[...]).astype(BF)
        z[at, :] = dot(hid, w_z[...])

    project(s)
    tok_sib.wait()
    project(sib)
    tok_far.wait()
    tok_forward.start()
    project(far)
    tok_forward.wait()
    project(diag)

    stores = [
        (hidden, hidden_o), (xin, xin_o), (act, act_o), (slope, slope_o), (c3.total, proj_o),
        (grad_branch, branch_o), (dy, dy_o), (silu_z, silu_o), (slope_z, slope_z_o),
    ]
    stores = [pltpu.make_async_copy(a, b, store_sems.at[i]) for i, (a, b) in enumerate(stores)]
    stores[0].start()
    stores[1].start()
    pad[:16, :] = jnp.zeros((16, chans), F32)
    pad[total + 16 :, :] = jnp.zeros((16, chans), F32)
    pad[16 : total + 16, :] = xin[...].astype(F32)
    for copy in loads[4:]:
        copy.wait()
    step = 64

    def chunk(c, carry):
        base = pl.multiple_of(c * step, step)
        window = pad[pl.ds(base, step + 32), :]
        here = pl.ds(base, step)
        for k in range(2):
            value = conv_b[k : k + 1, :]
            for tap in range(4):
                first = 13 + tap if k == 0 else 19 - tap
                value = value + conv_w[k, tap : tap + 1, :] * window[first : first + step]
            sig = jax.nn.sigmoid(value)
            acted = (value * sig).astype(BF)
            act[k, here, :] = acted
            slope[k, here, :] = (sig * (1.0 + value * (1.0 - sig))).astype(BF)
            c3.x[k, here, :] = dot(acted, xproj[k])
        return carry

    lax.fori_loop(0, total // step, chunk, 0)
    c3.start()
    stores[2].start()
    stores[3].start()

    def gate_back(block):
        at = pl.ds(pl.multiple_of(block * seg, seg), seg)
        grad = (cots[block].astype(F32) * mod_o[:, 2 * width :]).astype(BF)
        grad_branch[at, :] = grad
        grad_gated = dot_nt(grad, w_out[...])
        value = z[at, :]
        sigma = jax.nn.sigmoid(value)
        silu_z[at, :] = value * sigma
        dy[at, :] = grad_gated * (value * sigma)
        slope_z[at, :] = grad_gated * (sigma * (1.0 + value * (1.0 - sigma)))

    cot_far.wait()
    cot_forward.start()
    gate_back(s)
    c3.cross()
    cot_sib.wait()
    gate_back(sib)
    gate_back(far)
    cot_forward.wait()
    gate_back(diag)
    for copy in stores[5:]:
        copy.start()
    c3.back()
    c3.finish()
    stores[4].start()
    for copy in stores:
        copy.wait()


def first_part(
    tok, cot, flag, emb, ada_b, edge, in_weight, out_weight, conv_weight, conv_bias, xproj_weight,
    ada_w, a_log, collective_id,
):
    seg, width = tok.shape
    total = 4 * seg
    chans = out_weight.shape[0] // 4
    n_dp = emb.shape[0]
    columns = ada_w.shape[0]
    any_spec = pl.BlockSpec(memory_space=pl.ANY)
    shape = jax.ShapeDtypeStruct
    out_shape = [
        shape((total, width), BF),
        shape((total, width), BF),
        shape((total, chans), BF),
        shape((2, total, chans), BF),
        shape((2, total, chans), BF),
        shape((2, total, 128), F32),
        shape((total, chans), F32),
        shape((total, chans), F32),
        shape((total, chans), F32),
        shape((1, 3 * width), F32),
        shape((2, STATE, chans), F32),
    ]
    dma = pltpu.SemaphoreType.DMA
    vmem = pltpu.VMEM
    scratch = [
        vmem((width, chans), BF),
        vmem((width, chans), BF),
        vmem((chans, width), BF),
        vmem((2, 4, chans), F32),
        vmem((2, chans), F32),
        vmem((2, chans, 128), BF),
        vmem(ada_w.shape, BF),
        vmem((2, STATE, chans), F32),
        dma((8,)),
        vmem((4, seg, width), BF),
        vmem((4, seg, width), BF),
        vmem((4, 8, 128), F32),
        vmem((n_dp, 1, columns), F32),
        vmem((n_dp, 1, columns), F32),
        vmem((total, width), BF),
        vmem((total, width), BF),
        vmem((total, chans), BF),
        vmem((total, chans), F32),
        vmem((2, total, chans), BF),
        vmem((2, total, chans), BF),
    ]
    scratch += [vmem((total, chans), F32)] * 3 + [vmem((total + 32, chans), F32)]
    scratch += [dma((2, 3)), dma((2, 3)), dma((2, 3)), dma((2, n_dp)), dma((3,)), dma((9,))]
    scratch += SeqReduce.scratch(total, 128)
    return pl.pallas_call(
        first_kernel,
        in_specs=[VMEM_SPEC] * 6 + [any_spec] * 7,
        out_specs=[any_spec] * 9 + [VMEM_SPEC] * 2,
        out_shape=out_shape,
        scratch_shapes=scratch,
        compiler_params=comm_params(collective_id, 60),
        name="first_part",
    )(
        tok, cot, flag, emb, ada_b, edge, in_weight, out_weight, conv_weight, conv_bias, xproj_weight,
        ada_w, a_log,
    )


def rows_in_eights(x):
    total = x[:8]
    for k in range(1, x.shape[0] // 8):
        total = total + x[8 * k : 8 * k + 8]
    return total


def backward_kernel(*refs):
    refs = list(refs)

    def take(count):
        taken = refs[:count]
        del refs[:count]
        return taken

    (dl, hp, proj, act, coef, a2, dy, dread) = take(8)
    (tok, cot, gate, scale, flags) = take(5)
    far_inputs = take(13)
    dt_weight, conv_weight, skip_all = far_inputs[6:9]
    in_weight, xproj_weight = far_inputs[4:6]
    (result, tokg, in_ref, out_ref, a_ref, x0_ref, x1_ref, cv_ref, table_ref) = take(9)
    g_sc, g_a, g_b, q_a, q_b, r0, r1, r2, red = take(9)
    dpre, dc, dflow, dalog, sums = take(5)
    slope, xpad, hidden, grad_z, w_x, w_z, xproj, dtw, conv_w, skip, hid_in, out_in, xs_in, local_sems = take(14)
    conv_acc, dxin, gate_row = take(3)
    seq1 = SeqScatter(hid_in, *take(4), out=far_inputs[9])
    outs = DpScatter(out_in, *take(4))
    zs = DpScatter(xs_in, *take(4), out=far_inputs[11])
    gates, gate_sems = take(2)
    g_swap = SeqSwap(far_inputs[10], gates, gate_sems)
    z_red, z_got, z_swap_sems = take(3)
    z_swap = SeqSwap(z_red, z_got, z_swap_sems)
    c7 = SeqReduce(*take(6))
    smalls = []
    for _ in range(5):
        source = take(1)[0]
        scatter = DpDirect(source, *take(4))
        buf, sems = take(2)
        smalls.append((source, scatter, buf, Spread(buf, sems)))
    parts_a, parts_x, part_c = smalls[:2], smalls[2:4], smalls[4]
    seq2 = SeqScatter(hid_in, *take(4))
    xs = DpScatter(xs_in, *take(4))
    x_red, x_got, x_swap_sems = take(3)
    x_swap = SeqSwap(x_red, x_got, x_swap_sems)
    row, rows_in, row_sems, table, table_sems, result_sems = take(6)

    j = pl.program_id(0)
    blocks = pl.num_programs(0) // 2
    length = dl.shape[1]
    total = blocks * length
    chans = dl.shape[2]
    width = tok.shape[1]
    n = outs.n
    n_dp = 2 * n
    d_index, s_index = lax.axis_index("dp"), lax.axis_index("seq")
    rows_x = chans // n_dp

    def loads():
        own = pl.ds(pl.multiple_of(s_index * chans, 128), chans)
        own_z = pl.ds(pl.multiple_of((4 + s_index) * chans, 128), chans)
        pairs = [
            (far_inputs[0], slope),
            (far_inputs[1], xpad.at[pl.ds(16, total)]),
            (far_inputs[12], hidden),
            (far_inputs[3], grad_z),
            (in_weight.at[:, own], w_x),
            (in_weight.at[:, own_z], w_z),
            (xproj_weight.at[:, own], xproj),
            (dt_weight.at[:, :, own], dtw.at[:, pl.ds(0, dt_weight.shape[1])]),
            (conv_weight.at[:, :, own], conv_w),
            (far_inputs[9], hid_in),
            (far_inputs[10].at[s_index], gates.at[s_index]),
            (far_inputs[11], xs_in),
            (skip_all.at[:, own], skip),
            (far_inputs[2], hidden),
        ]
        return [pltpu.make_async_copy(a, b, local_sems.at[i]) for i, (a, b) in enumerate(pairs)]

    def results():
        pairs = []
        for d in range(2):
            buf = parts_a[d][2]
            pairs += [(buf.at[q], a_ref.at[d, :, :, :, pl.ds(q * chans, chans)]) for q in range(4)]
        pairs += [(parts_x[0][2], x0_ref), (parts_x[1][2], x1_ref), (part_c[2], cv_ref)]
        return [pltpu.make_async_copy(a, b, result_sems.at[i]) for i, (a, b) in enumerate(pairs)]

    near = [(zs, k) for k in range(n)] + [(outs, k) for k in range(n)]
    pair_at = [2, 4, 5, 7, 8, 8, 8, 8]

    def step_of(i):
        return pair_at[i * 8 // (2 * n)]

    unit = 2 * blocks // 8

    @pl.when(j == 0)
    def _():
        greet_all()
        g_swap.send()
        seq1.start()
        zs.start()
        for copy in loads()[:13]:
            copy.start()
        loads()[12].wait()
        for d in range(2):
            dc[d, :16, :] = jnp.zeros((16, chans), F32)
            dc[d, total + 16 :, :] = jnp.zeros((16, chans), F32)
        xpad[:16, :] = jnp.zeros((16, chans), BF)
        xpad[total + 16 :, :] = jnp.zeros((16, chans), BF)
        dtw[:, dt_weight.shape[1] :, :] = jnp.zeros((2, 128 - dt_weight.shape[1], chans), BF)
        dalog[...] = jnp.zeros_like(dalog)
        sums[...] = jnp.zeros_like(sums)
        conv_acc[...] = jnp.zeros_like(conv_acc)

    @pl.when(j == 2 * unit)
    def _():
        for copy in loads()[9:12]:
            copy.wait()
        seq1.cross()

    @pl.when(j == 3 * unit)
    def _():
        g_swap.finish()
        loads()[2].wait()
        for q in range(4):
            grad = dot_tn(gates[q], hidden[...]).astype(BF)
            for b in range(n_dp // 4):
                out_in[n_dp // 4 * q + b] = grad[b * rows_x : (b + 1) * rows_x]
        outs.start()
        loads()[13].start()

    for i, (scatter, k) in enumerate(near):
        if step_of(i) < 8:
            pl.when(j == unit * step_of(i))(functools.partial(scatter.pair, k))


    @pl.when(j == 5 * unit)
    def _():
        branch = seq1.finish()
        result[...] = (tok[...].astype(F32) + gate[...] * branch).astype(BF)
        gate_row[...] = jnp.sum(cot[...].astype(F32) * branch, axis=0, keepdims=True)

    @pl.when(lax.rem(j, blocks) == 0)
    def _():
        g_sc[...] = jnp.zeros_like(g_sc)

    def run(rev):
        d = int(rev)
        block = j - blocks if rev else blocks - 1 - j
        base = pl.multiple_of(block * length, length)
        here = pl.ds(base, length)
        backward_block(
            rev, dl.at[0], act.at[d, here], coef.at[0], a2.at[d],
            proj.at[d, here], dy.at[here], skip.at[pl.ds(d, 1)], hp.at[0], dpre.at[d, here],
            dc.at[d, pl.ds(pl.multiple_of(base + 16, 16), length)], dflow.at[d, block], dalog.at[d],
            sums.at[d], g_sc, ((g_a, q_a), (g_b, q_b)), (r0, r1, r2), red,
        )

    pl.when(j < blocks)(lambda: run(False))
    pl.when(j >= blocks)(lambda: run(True))

    @pl.when(j == 2 * blocks - 1)
    def _():
        late = [near[i] for i in range(2 * n) if step_of(i) >= 8]

        def pairs():
            for _ in range(len(late) // 4):
                scatter, k = late[pairs.done]
                pairs.done += 1
                scatter.pair(k)

        pairs.done = 0
        for i in (0, 1, 3, 4, 5, 6, 7, 8, 13):
            loads()[i].wait()
        for d in range(2):
            value = dot_nt(dpre[d], dtw[d])
            for b in range(blocks):
                at = slice(b * length, (b + 1) * length)
                square = jnp.concatenate(
                    [jnp.zeros((128 - 2 * STATE, length), F32), dflow[d, b], dread[d, b]], axis=0
                )
                c7.x[d, at] = value[at] + square.T
        c7.start()
        rank = 128 - 2 * STATE
        per_d = 128 // n_dp
        for d in range(2):
            source, scatter, _, _ = parts_a[d]
            lines = dot_tn(proj[d].astype(BF), dpre[d])[:rank]
            extra = [jnp.sum(sums[d, i], axis=0, keepdims=True) for i in range(2)]
            lines = jnp.concatenate(
                [lines, dalog[d] * (a2[d] * LN2)] + extra + [jnp.zeros((STATE - 2, chans), F32)], axis=0
            ).astype(BF)
            for b in range(n_dp):
                source[b] = lines[b * per_d : (b + 1) * per_d]
            scatter.start()
        c7.cross()
        pairs()
        z_red[...] = zs.finish().astype(BF)
        z_swap.start()
        c7.back()
        pairs()
        c7.finish()

        for d in range(2):
            dproj = c7.total[d].astype(BF)
            source, scatter, _, _ = parts_x[d]
            grad = dot_tn(act[d], dproj).astype(BF)
            for b in range(n_dp):
                source[b] = grad[b * rows_x : (b + 1) * rows_x]
            scatter.start()

            def act_rows(c, carry, d=d):
                at = pl.ds(pl.multiple_of(c * 128, 128), 128)
                shifted = pl.ds(pl.multiple_of(c * 128 + 16, 16), 128)
                value = dot_nt(c7.total[d, at].astype(BF), xproj[d]) + dc[d, shifted]
                dc[d, shifted] = value * slope[d, at].astype(F32)
                return carry

            lax.fori_loop(0, total // 128, act_rows, 0)
        pairs()
        step = 32

        def conv_rows(c, carry):
            base = pl.multiple_of(c * step, step)
            window = pl.ds(base, step + 32)
            x_w = xpad[window, :].astype(F32)
            grad = jnp.zeros((step, chans), F32)
            for d in range(2):
                d_w = dc[d, window]
                here = d_w[16 : 16 + step]
                conv_acc[5 * d + 4] += rows_in_eights(here)
                for tap in range(4):
                    off = tap - 3 if d == 0 else 3 - tap
                    conv_acc[5 * d + tap] += rows_in_eights(here * x_w[16 + off : 16 + off + step])
                    grad = grad + conv_w[d, tap : tap + 1] * d_w[16 - off : 16 - off + step]
            dxin[pl.ds(base, step), :] = grad.astype(BF)
            return carry

        lax.fori_loop(0, total // step, conv_rows, 0)
        source, scatter, _, _ = part_c
        conv_lines = [jnp.sum(conv_acc[i], axis=0, keepdims=True) for i in range(10)]
        conv_lines = jnp.concatenate(conv_lines + [jnp.zeros((6, chans), F32)], axis=0)
        for b in range(n_dp):
            source[b, :, :rows_x] = conv_lines[:, b * rows_x : (b + 1) * rows_x].astype(BF)
            source[b, :, rows_x:] = jnp.zeros((16, 128 - rows_x), BF)
        scatter.start()
        pairs()

        rb = width // (4 * n_dp)
        half = n_dp // 2
        for h in range(2):
            cols = slice(h * width // 2, (h + 1) * width // 2)
            grad = dot_tn(hidden[:, cols], dxin[...]).astype(BF)
            for b in range(half):
                for q in range(4):
                    first = (4 * b + q) * rb
                    xs_in[h * half + b, q] = grad[first : first + rb]
        xs.start()
        for _, scatter, _, _ in parts_a:
            for k in range(n):
                scatter.pair(k)
        seg = tok.shape[0]
        for h in range(2):
            cols = slice(h * width // 2, (h + 1) * width // 2)
            grad = (dot_nt(dxin[...], w_x[cols, :]) + dot_nt(grad_z[...], w_z[cols, :])).astype(BF)
            for q in range(4):
                hid_in[q, :, cols] = grad[q * seg : (q + 1) * seg]
        seq2.start()
        for _, scatter, _, _ in parts_x + [part_c]:
            for k in range(n):
                scatter.pair(k)
        seq2.cross()
        for k in range(n // 4):
            xs.pair(k)

        def gathered(parts):
            for _, scatter, buf, spread in parts:
                buf[spread.place] = scatter.finish().astype(BF)
                spread.go_z()

        gathered(parts_a)
        gathered(parts_x + [part_c])
        out_ref[...] = outs.finish().astype(BF)
        for k in range(n // 4, n // 2):
            xs.pair(k)

        grad = seq2.finish()
        tokens = tok[...].astype(F32)
        centred = tokens - jnp.mean(tokens, axis=1, keepdims=True)
        inv_std = lax.rsqrt(jnp.mean(centred * centred, axis=1, keepdims=True) + epsilon)
        normed = centred * inv_std
        row[:, :width] = jnp.sum(grad, axis=0, keepdims=True)
        row[:, width : 2 * width] = jnp.sum(grad * normed, axis=0, keepdims=True)
        row[:, 2 * width : 3 * width] = gate_row[...]
        row[:, 3 * width :] = jnp.sum(grad * flags[...], axis=0, keepdims=True)
        pair = (row_sems.at[0], row_sems.at[1])
        row_copies = [
            remote(row, rows_in.at[k], pair, k, {"seq": other})
            for k, other in enumerate(seq_others())
        ]
        for copy in row_copies:
            copy.start()
        grad_normed = grad * (1.0 + scale[...])
        inner_product = jnp.mean(grad_normed * normed, axis=1, keepdims=True)
        tokg[...] = (
            cot[...].astype(F32)
            + inv_std
            * (grad_normed - jnp.mean(grad_normed, axis=1, keepdims=True) - normed * inner_product)
        ).astype(BF)
        spreads = [item[3] for item in parts_a + parts_x + [part_c]]
        for spread in spreads:
            spread.go_y()
        for k in range(n // 2, 3 * n // 4):
            xs.pair(k)
        for copy in row_copies:
            copy.wait()
        table[d_index] = row[...] + rows_in[1] + (rows_in[0] + rows_in[2])
        pair = (table_sems.at[0], table_sems.at[1])
        table_copies = [
            remote(table.at[d_index], table.at[d_index], pair, k, {"dp": other})
            for k, other in enumerate(dp_others())
        ]
        for copy in table_copies:
            copy.start()
        for k in range(3 * n // 4, n):
            xs.pair(k)
        for spread in spreads:
            spread.go_x()
        x_red[...] = xs.finish().astype(BF)
        x_swap.start()
        z_swap.finish()
        for q in range(4):
            in_ref[:, (4 + q) * chans : (5 + q) * chans] = z_got[q]
        for copy in table_copies:
            copy.wait()
        table_ref[...] = table[...]
        for spread in spreads:
            spread.go_sib()
        x_swap.finish()
        for q in range(4):
            in_ref[:, q * chans : (q + 1) * chans] = x_got[q]
        for spread in spreads:
            spread.finish()
        for copy in results():
            copy.start()
        for copy in results():
            copy.wait()


def scan_backward(
    dl, hp, proj, act, coef, a2, dy, dread, branch, sorted_gated, grad_branch, z_part,
    tok, cot, gate, scale, flags, slope, xin, hidden, grad_z, in_weight, xproj_weight, dt_weight, conv_weight, skip,
    collective_id, tile,
):
    total, chans = dy.shape
    blocks = total // tile
    n_dp = z_part.shape[0]
    n = n_dp // 2
    rows, width = tok.shape
    rb = width // (4 * n_dp)
    rows_x = chans // n_dp
    per_d = 128 // n_dp
    out_block = (rows_x, width)

    def place(j):
        d = j // blocks
        b = lax.rem(j, blocks)
        return d, blocks - 1 - b + d * (2 * b - blocks + 1)

    def tokens_of(j):
        d, b = place(j)
        return d, b, 0

    def cells(j):
        d, b = place(j)
        return d, b, 0, 0

    any_spec = pl.BlockSpec(memory_space=pl.ANY)
    in_specs = (
        [
            pl.BlockSpec((1, tile, chans), tokens_of),
            pl.BlockSpec((1, tile * STATE, chans), tokens_of),
        ]
        + [VMEM_SPEC] * 2
        + [pl.BlockSpec((1, tile // U, 2 * STATE, U), cells)]
        + [VMEM_SPEC] * 8
        + [any_spec] * 13
    )
    shape = jax.ShapeDtypeStruct
    in_out = (4, n, 2)
    out_shape = [
        shape((rows, width), BF),
        shape((rows, width), BF),
        shape((rb, 8 * chans), BF),
        shape(out_block, BF),
        shape((2, n, 2, per_d, 4 * chans), BF),
        shape(in_out + (rows_x, 128), BF),
        shape(in_out + (rows_x, 128), BF),
        shape(in_out + (16, 128), BF),
        shape((n_dp, 1, 4 * width), F32),
    ]
    dma = pltpu.SemaphoreType.DMA
    vmem = pltpu.VMEM
    scratch = [
        vmem((STATE, chans), F32),
        vmem((U * STATE, chans), BF),
        vmem((U * STATE, chans), BF),
        vmem((U * 8, chans), BF),
        vmem((U * 8, chans), BF),
    ]
    scratch += [vmem((U, chans), F32)] * 3 + [vmem((U, STATE, 128), F32)]
    scratch += [
        vmem((2, total, chans), BF),
        vmem((2, total + 32, chans), F32),
        vmem((2, blocks, STATE, tile), F32),
        vmem((2, STATE, chans), F32),
        vmem((2, 2, U, chans), F32),
    ]
    scratch += [
        vmem(slope.shape, BF),
        vmem((total + 32, chans), BF),
        vmem(hidden.shape, BF),
        vmem(grad_z.shape, BF),
        vmem((width, chans), BF),
        vmem((width, chans), BF),
        vmem((2, chans, 128), BF),
        vmem((2, 128, chans), BF),
        vmem((2, 4, chans), F32),
        vmem((2, chans), F32),
        vmem((4, rows, width), BF),
        vmem((n_dp,) + out_block, BF),
        vmem(z_part.shape, BF),
        dma((14,)),
    ]
    scratch += [
        vmem((10, 8, chans), F32),
        vmem((total, chans), BF),
        vmem((1, width), F32),
    ]
    scratch += SeqScatter.scratch(rows, width)
    scratch += DpScatter.scratch(n_dp, out_block) + DpScatter.scratch(n_dp, z_part.shape[1:])
    scratch += [vmem(sorted_gated.shape, BF), dma((2, 3))]
    scratch += [vmem(z_part.shape[1:], BF)] * 2 + [dma((2, 3))]
    scratch += SeqReduce.scratch(total, 128)
    for block in [(per_d, chans)] * 2 + [(rows_x, 128)] * 2 + [(16, 128)]:
        scratch += [vmem((n_dp,) + block, BF)] + DpScatter.scratch(n_dp, block)
        scratch += Spread.scratch(n_dp, block)
    scratch += SeqScatter.scratch(rows, width)
    scratch += DpScatter.scratch(n_dp, z_part.shape[1:])
    scratch += [vmem(z_part.shape[1:], BF)] * 2 + [dma((2, 3))]
    scratch += [
        vmem((1, 4 * width), F32),
        vmem((3, 1, 4 * width), F32),
        dma((2, 3)),
        vmem((n_dp, 1, 4 * width), F32),
        dma((2, n_dp)),
        dma((11,)),
    ]
    return pl.pallas_call(
        backward_kernel,
        grid=(2 * blocks,),
        in_specs=in_specs,
        out_specs=[VMEM_SPEC] * 4 + [any_spec] * 4 + [VMEM_SPEC],
        out_shape=out_shape,
        scratch_shapes=scratch,
        compiler_params=comm_params(collective_id, 62),
        name="scan_backward",
    )(
        dl, hp, proj, act, coef, a2, dy, dread, tok, cot, gate, scale, flags, slope, xin, hidden,
        grad_z, in_weight, xproj_weight, dt_weight, conv_weight, skip, branch,
        sorted_gated, z_part, grad_branch,
    )


def time_embedding(step_ids, model_width):
    halfway = model_width // 2
    frequency = jnp.exp(-math.log(10000.0) * jnp.arange(halfway, dtype=jnp.float32) / halfway)
    angles = step_ids.astype(jnp.float32)[:, None] * frequency[None, :]
    return jnp.concatenate([jnp.cos(angles), jnp.sin(angles)], axis=1)


def silu_slope(values):
    sigma = jax.nn.sigmoid(values)
    return sigma * (1.0 + values * (1.0 - sigma))


def shards(
    tokens,
    cotangent,
    timesteps,
    grid_widths,
    scan_path,
    ada_weight,
    ada_bias,
    edge,
    in_weight,
    conv_weight,
    conv_bias,
    xproj_weight,
    dt_weight,
    dt_bias,
    a_log,
    skip,
    out_weight,
):
    seg_len, width = tokens.shape[1:]
    inner = in_weight.shape[1] // 2
    rank = dt_weight.shape[1]
    taps = conv_weight.shape[1]
    rim = taps - 1
    columns = ada_weight.shape[1]
    n_seq = lax.axis_size("seq")
    n_dp = lax.axis_size("dp")
    dp_index = lax.axis_index("dp")
    seq_index = lax.axis_index("seq")
    length = seg_len * n_seq
    chans = inner // n_seq

    def flags_of(item):
        return (jnp.remainder(item, grid_widths[0]) == grid_widths[0] - 1).astype(F32)

    embedded = jax.nn.silu(time_embedding(timesteps, width)).astype(BF)
    own_flags = flags_of(scan_path)
    hidden, grad_branch, xin, act, slope, proj, dy, silu_z, slope_z, modulation, decay2 = first_part(
        tokens[0], cotangent[0], jnp.broadcast_to(own_flags, (8, seg_len)), embedded, ada_bias[None],
        edge[None], in_weight, out_weight, conv_weight, conv_bias, xproj_weight, ada_weight.T,
        jnp.swapaxes(a_log, 1, 2), 0,
    )
    scale_term = modulation[:, width : 2 * width]
    gate_term = modulation[:, 2 * width :]
    tile = 128 if n_dp <= 8 else 32
    coef = jnp.swapaxes(proj[:, :, 128 - 2 * STATE :].reshape(2, length // U, U, 2 * STATE), 2, 3)
    held, delta, dread, branch, sorted_gated, z_part, grad_z = scan_forward(
        seq_index.astype(jnp.int32)[None], proj, act, coef, dt_weight, dt_bias, decay2,
        skip, dy, silu_z, slope_z, hidden, out_weight, tile,
    )
    total = n_dp * n_seq

    def in_blocks(grad):
        return grad.reshape(n_dp, n_seq, width // total, chans)

    result, grad_tok, in_rows, out_rows, lines, x0, x1, conv_lines, table = scan_backward(
        delta, held, proj, act, coef, decay2, dy, dread,
        branch.reshape(n_seq, seg_len, width),
        sorted_gated,
        grad_branch,
        in_blocks(z_part),
        tokens[0], cotangent[0], gate_term, scale_term, own_flags[0][:, None],
        slope, xin, hidden, grad_z, in_weight, xproj_weight, dt_weight, conv_weight, skip,
        2, tile,
    )
    table = table.reshape(n_dp, -1)
    edge_grad = jnp.sum(table[:, 3 * width :], axis=0)
    mod_columns = lax.dynamic_slice_in_dim(table[:, : 3 * width], dp_index * columns, columns, 1)
    ada_b_grad = jnp.sum(mod_columns, axis=0)
    ada_w_grad = jnp.dot(embedded.astype(F32).T, mod_columns, precision=highest)
    lines = lines.reshape(2, 128, inner).astype(F32)
    alog_grad = jnp.swapaxes(lines[:, rank : rank + STATE], 1, 2)
    xproj_grad = jnp.stack([item.reshape(inner, 128) for item in (x0, x1)]).astype(F32)
    conv_lines = jnp.moveaxis(conv_lines[..., : chans // n_dp], 3, 0).reshape(16, inner).astype(F32)
    conv_lines = conv_lines[: 2 * (taps + 1)].reshape(2, taps + 1, inner)
    return (
        result[None],
        grad_tok[None],
        ada_w_grad,
        ada_b_grad,
        edge_grad,
        in_rows.astype(F32),
        conv_lines[:, :taps],
        conv_lines[:, taps],
        xproj_grad,
        lines[:, :rank],
        lines[:, rank + STATE],
        alog_grad,
        lines[:, rank + STATE + 1],
        out_rows.astype(F32),
    )


def solution(mesh):
    in_specs = (
        P("dp", "seq", None),
        P("dp", "seq", None),
        P(),
        P("dp"),
        P("dp", "seq"),
        P(None, "dp"),
        P("dp"),
        P(),
        P(),
        P(),
        P(),
        P(),
        P(),
        P(),
        P(),
        P(),
        P(),
    )
    out_specs = (
        P("dp", "seq", None),
        P("dp", "seq", None),
        P(None, "dp"),
        P("dp"),
        P(),
        P(("dp", "seq"), None),
        P(),
        P(),
        P(),
        P(),
        P(),
        P(),
        P(),
        P(("dp", "seq"), None),
    )
    return jax.shard_map(shards, mesh=mesh, in_specs=in_specs, out_specs=out_specs, check_vma=False)
```

```python
import functools
import math

import jax
import jax.numpy as jnp
from jax import lax
from jax.experimental import pallas as pl
from jax.experimental.pallas import tpu as pltpu
from jax.sharding import PartitionSpec as P

STATE = 16
U = 16
PARTS = 3
LOG2E = 1.4426950408889634
LN2 = 0.6931471805599453
F32 = jnp.float32
BF = jnp.bfloat16
epsilon = 1e-06
highest = lax.Precision.HIGHEST
MESH = pl.DeviceIdType.MESH
VMEM_SPEC = pl.BlockSpec(memory_space=pltpu.VMEM)


def iota(shape, dim):
    return lax.broadcasted_iota(jnp.int32, shape, dim)


def dot(a, b):
    return lax.dot_general(a, b, (((1,), (0,)), ((), ())), preferred_element_type=F32)


def dot_nt(a, b):
    return lax.dot_general(a, b, (((1,), (1,)), ((), ())), preferred_element_type=F32)


def dot_tn(a, b):
    return lax.dot_general(a, b, (((0,), (0,)), ((), ())), preferred_element_type=F32)


def softplus(x):
    return jnp.maximum(x, 0.0) + jnp.log1p(jnp.exp(-jnp.abs(x)))


def diag_of(rows, first):
    k = U * STATE
    pick = (iota((128, k), 0) - first == lax.rem(iota((128, k), 1), STATE)).astype(F32).astype(BF)
    keep = (iota((U, k), 1) // STATE == iota((U, k), 0)).astype(F32)
    return (dot(rows.astype(BF), pick) * keep).astype(BF)


def over_lanes(x, t):
    return jnp.broadcast_to(x[:, t : t + 1], (x.shape[0], 128))


def wide(x, n):
    return jnp.concatenate([x] * n, axis=1)


def lane_fold(x):
    acc = x[:, :128]
    for j in range(1, x.shape[1] // 128):
        acc = acc + x[:, 128 * j : 128 * (j + 1)]
    return acc


def interleave(steps, pieces):
    done = 0
    for i, step in enumerate(steps):
        step()
        while done < (i + 1) * len(pieces) // len(steps):
            pieces[done]()
            done += 1


def pipeline(groups, work, drain):
    interleave(work(0, 0), [])

    def two(p, carry):
        interleave(work(2 * p + 1, 1), drain(2 * p, 0))
        interleave(work(2 * p + 2, 0), drain(2 * p + 1, 1))
        return carry

    lax.fori_loop(0, groups // 2 - 1, two, 0)
    interleave(work(groups - 1, 1), drain(groups - 2, 0))
    interleave([lambda: None], drain(groups - 1, 1))


def forward_block(rev, dl, act, coef, a2, proj, dy, hp, put_y, dread, h_sc, hb_sc, slots, rows, red):
    length, chans = dl.shape
    groups = length // U
    part_width = chans // PARTS
    dlu, duu, dyu = rows
    dread[...] = jnp.zeros_like(dread)

    def place(k):
        return (groups - 1 - k) if rev else k

    def work(k, slot):
        g = place(k)
        t0 = pl.multiple_of(g * U, U)
        at = pl.ds(t0, U)
        dlu[...] = dl[at, :]
        duu[...] = dl[at, :] * act[at, :].astype(F32)
        dyu[...] = dy[at, :]
        inflow = coef[g][:STATE]
        spread = [over_lanes(inflow, t) for t in range(U)]
        hbuf = slots[slot]
        v = {}

        def token(part, i):
            col = pl.ds(part * part_width, part_width)
            if i == 0:
                v["a"], v["h"], v["hb"] = a2[:, col], h_sc[:, col], hb_sc[:, col]
            loc = (U - 1 - i) if rev else i
            one = pl.ds(loc, 1)
            h = jnp.exp2(dlu[one, col] * v["a"]) * v["h"] + duu[one, col] * wide(
                spread[loc], part_width // 128
            )
            hp[pl.ds(pl.multiple_of((t0 + loc) * STATE, STATE), STATE), col] = v["hb"]
            hb = h.astype(BF)
            hbuf[pl.ds(loc * STATE, STATE), col] = hb
            v["h"], v["hb"] = h, hb
            total = lane_fold(dyu[one, col] * h)
            if part:
                total = red[loc] + total
            if part < PARTS - 1:
                red[loc] = total
            else:
                here = iota(dread.shape, 1) == g * U + loc
                v["sum"] = jnp.where(here, jnp.sum(total, axis=1, keepdims=True), v.get("sum", 0.0))
                if i == U - 1:
                    dread[...] += v["sum"]
            if i == U - 1:
                h_sc[:, col] = h
                hb_sc[:, col] = hb

        return [functools.partial(token, part, i) for part in range(PARTS) for i in range(U)]

    def drain(k, slot):
        at = pl.ds(pl.multiple_of(place(k) * U, U), U)
        hbuf = slots[slot]
        v = {}

        def first():
            v["c"] = diag_of(proj[at, :], 128 - STATE)

        def out(c):
            col = pl.ds(256 * c, 256)
            put_y(at, col, dot(v["c"], hbuf[:, col]))

        return [first] + [functools.partial(out, c) for c in range(chans // 256)]

    pipeline(groups, work, drain)


def backward_block(
    rev, dl, act, coef, a2, proj, dy, skip, hp, dpre, dact, dflow, dalog, sums, g_sc, slots, rows, red
):
    length, chans = dl.shape
    groups = length // U
    part_width = chans // PARTS
    dlu, duu, dyu = rows
    dflow[...] = jnp.zeros_like(dflow)

    def place(k):
        return k if rev else (groups - 1 - k)

    def work(k, slot):
        g = place(k)
        t0 = pl.multiple_of(g * U, U)
        at = pl.ds(t0, U)
        dlu[...] = dl[at, :]
        duu[...] = dl[at, :] * act[at, :].astype(F32)
        dyu[...] = dy[at, :]
        readout = coef[g][STATE:]
        spread = [over_lanes(readout, t) for t in range(U)]
        gbuf, qbuf = slots[slot]
        v = {}

        def token(part, i):
            col = pl.ds(part * part_width, part_width)
            if i == 0:
                v["a"], v["car"], v["acc"] = a2[:, col], g_sc[:, col], dalog[:, col]
            loc = i if rev else (U - 1 - i)
            one = pl.ds(loc, 1)
            step = dlu[one, col]
            g_t = dyu[one, col] * wide(spread[loc], part_width // 128) + v["car"]
            car = jnp.exp2(step * v["a"]) * g_t
            before = hp[pl.ds(pl.multiple_of((t0 + loc) * STATE, STATE), STATE), col].astype(F32)
            q = car * before
            v["acc"] = v["acc"] + q * step
            v["car"] = car
            gbuf[pl.ds(loc * STATE, STATE), col] = g_t.astype(BF)
            total = lane_fold(duu[one, col] * g_t)
            if part:
                total = red[loc] + total
            if part < PARTS - 1:
                red[loc] = total
            else:
                here = iota(dflow.shape, 1) == g * U + loc
                v["sum"] = jnp.where(here, jnp.sum(total, axis=1, keepdims=True), v.get("sum", 0.0))
                if i == U - 1:
                    dflow[...] += v["sum"]
            qa = q * v["a"]
            qa = qa[:8] + qa[8:]
            if i % 2 == 0:
                v["held"] = qa
            else:
                pair = [v["held"], qa] if rev else [qa, v["held"]]
                qbuf[pl.ds((loc // 2) * STATE, STATE), col] = jnp.concatenate(pair, 0).astype(BF)
            if i == U - 1:
                g_sc[:, col] = v["car"]
                dalog[:, col] = v["acc"]

        return [functools.partial(token, part, i) for part in range(PARTS) for i in range(U)]

    def drain(k, slot):
        at = pl.ds(pl.multiple_of(place(k) * U, U), U)
        gbuf, qbuf = slots[slot]
        v = {}

        def first():
            v["b"] = diag_of(proj[at, :], 128 - 2 * STATE)
            v["ones"] = (iota((U, U * 8), 1) // 8 == iota((U, U * 8), 0)).astype(F32).astype(BF)

        def cols(c):
            col = pl.ds(256 * c, 256)
            s = dot(v["b"], gbuf[:, col])
            q = dot(v["ones"], qbuf[:, col]) * LN2
            a = act[at, col].astype(F32)
            step = dl[at, col]
            grad = dy[at, col]
            pre = ((q + a * s) * (1.0 - jnp.exp(-step))).astype(BF)
            dpre[at, col] = pre
            dact[at, col] = step * s + skip[:, col] * grad
            sums[0, :, col] += pre.astype(F32)
            sums[1, :, col] += grad * a

        return [first] + [functools.partial(cols, c) for c in range(chans // 256)]

    pipeline(groups, work, drain)


def forward_kernel(
    s_ref, proj, act, coef, dtw, dtb, a2, skip, dy, silu_all, slope_all, hidden_all, out_weight,
    hp, dl, dread, branch, sorted_gated, z_part, grad_z,
    y, h_sc, hb_sc, h_a, h_b, r0, r1, r2, red, gated, silu_z, slope_z, hidden, w_out, sems,
):
    j = pl.program_id(0)
    blocks = pl.num_programs(0) // 2
    length, chans = dl.shape[1:]
    n_dp = lax.axis_size("dp")
    own_rows = pl.ds(pl.multiple_of(s_ref[0] * chans, 128), chans)
    late = [(silu_all, silu_z), (slope_all, slope_z), (hidden_all, hidden), (out_weight.at[own_rows], w_out)]
    late = [pltpu.make_async_copy(a, b, sems.at[i]) for i, (a, b) in enumerate(late)]

    @pl.when(j == 0)
    def _():
        for copy in late:
            copy.start()

    @pl.when(lax.rem(j, blocks) == 0)
    def _():
        h_sc[...] = jnp.zeros_like(h_sc)
        hb_sc[...] = jnp.zeros_like(hb_sc)

    def run(rev):
        own = slice(int(rev), int(rev) + 1)
        pre = dot(proj[0][:, : dtw.shape[1]].astype(BF), dtw[0]) + dtb[own]
        dl[0] = softplus(pre)
        base = (2 * blocks - 1 - j if rev else j) * length
        dy_block = dy.at[pl.ds(pl.multiple_of(base, length), length)]

        def put_y(at, col, value):
            value = value + skip[own, col] * act[0, at, col].astype(F32)
            rows = pl.ds(pl.multiple_of(base + at.start, U), U)
            if rev:
                value = value + y[rows, col]
            y[rows, col] = value

        forward_block(
            rev, dl.at[0], act.at[0], coef.at[0], a2.at[0], proj.at[0], dy_block, hp.at[0], put_y,
            dread.at[0, 0], h_sc, hb_sc, (h_a, h_b), (r0, r1, r2), red,
        )

    pl.when(j < blocks)(lambda: run(False))
    pl.when(j >= blocks)(lambda: run(True))

    @pl.when(j == 2 * blocks - 1)
    def _():
        total = y.shape[0]
        for copy in late:
            copy.wait()

        def rows_of(c, carry):
            at = pl.ds(pl.multiple_of(c * 64, 64), 64)
            value = y[at, :]
            opened = value * silu_z[at, :]
            gated[at, :] = opened.astype(BF)
            piece = 4 * sorted_gated.shape[2] // n_dp
            for q in range(4):
                pieces = [opened[:, b * piece : (b + 1) * piece] for b in range(q, n_dp, 4)]
                sorted_gated[q, at, :] = jnp.concatenate(pieces, axis=1).astype(BF)
            grad_z[at, :] = (value * slope_z[at, :]).astype(BF)
            return carry

        lax.fori_loop(0, total // 64, rows_of, 0)
        width = w_out.shape[1]

        for c in range(2):
            at = slice(c * total // 2, (c + 1) * total // 2)
            branch[at, :] = dot(gated[at, :], w_out[...]).astype(BF)

        for c in range(2):
            at = slice(c * width // 2, (c + 1) * width // 2)
            z_part[at, :] = dot_tn(hidden[:, at], grad_z[...]).astype(BF)


def scan_forward(
    seq_index, proj, act, coef, dtw, dtb, a2, skip, dy, silu_z, slope_z, hidden, w_out, tile
):
    total, chans = dy.shape
    width = w_out.shape[1]
    blocks = total // tile

    def place(j):
        d = j // blocks
        b = lax.rem(j, blocks)
        return d, b + d * (blocks - 1 - 2 * b)

    def tokens_of(j, s):
        d, b = place(j)
        return d, b, 0

    def direction_of(j, s):
        return j // blocks, 0, 0

    def channels_of(j, s):
        return j // blocks, 0, s[0]

    def cells(j, s):
        d, b = place(j)
        return d, b, 0, 0

    whole = VMEM_SPEC
    in_specs = [
        pl.BlockSpec((1, tile, 128), tokens_of),
        pl.BlockSpec((1, tile, chans), tokens_of),
        pl.BlockSpec((1, tile // U, 2 * STATE, U), cells),
        pl.BlockSpec((1, dtw.shape[1], chans), channels_of),
        pl.BlockSpec((2, chans), lambda j, s: (0, s[0])),
        pl.BlockSpec((1, STATE, chans), direction_of),
        pl.BlockSpec((2, chans), lambda j, s: (0, s[0])),
    ] + [whole] + [pl.BlockSpec(memory_space=pl.ANY)] * 4
    out_specs = [
        pl.BlockSpec((1, tile * STATE, chans), tokens_of),
        pl.BlockSpec((1, tile, chans), tokens_of),
        pl.BlockSpec((1, 1, STATE, tile), cells),
    ] + [whole] * 4
    out_shape = [
        jax.ShapeDtypeStruct((2, total * STATE, chans), BF),
        jax.ShapeDtypeStruct((2, total, chans), F32),
        jax.ShapeDtypeStruct((2, blocks, STATE, tile), F32),
        jax.ShapeDtypeStruct((total, width), BF),
        jax.ShapeDtypeStruct((4, total, chans // 4), BF),
        jax.ShapeDtypeStruct((width, chans), BF),
        jax.ShapeDtypeStruct((total, chans), BF),
    ]
    return pl.pallas_call(
        forward_kernel,
        grid_spec=pltpu.PrefetchScalarGridSpec(
            num_scalar_prefetch=1,
            grid=(2 * blocks,),
            in_specs=in_specs,
            out_specs=out_specs,
            scratch_shapes=[
                pltpu.VMEM((total, chans), F32),
                pltpu.VMEM((STATE, chans), F32),
                pltpu.VMEM((STATE, chans), BF),
                pltpu.VMEM((U * STATE, chans), BF),
                pltpu.VMEM((U * STATE, chans), BF),
            ]
            + [pltpu.VMEM((U, chans), F32)] * 3
            + [pltpu.VMEM((U, STATE, 128), F32), pltpu.VMEM((total, chans), BF)]
            + [pltpu.VMEM((total, chans), F32)] * 2
            + [pltpu.VMEM((total, width), BF), pltpu.VMEM((chans, width), BF)]
            + [pltpu.SemaphoreType.DMA((4,))],
        ),
        out_shape=out_shape,
        compiler_params=pltpu.CompilerParams(vmem_limit_bytes=60 << 20),
        name="scan_forward",
    )(seq_index, proj, act, coef, dtw, dtb, a2, skip, dy, silu_z, slope_z, hidden, w_out)


def sibling_of(s):
    return s + 1 - 2 * lax.rem(s, 2)


def across_of(s):
    return lax.rem(s + 2, 4)


def remote(src, dst, sems, slot, peer):
    return pltpu.make_async_remote_copy(
        src_ref=src,
        dst_ref=dst,
        send_sem=sems[0].at[slot],
        recv_sem=sems[1].at[slot],
        device_id=peer,
        device_id_type=MESH,
    )


def greet(peers):
    barrier = pltpu.get_barrier_semaphore()
    for peer in peers:
        pl.semaphore_signal(barrier, inc=1, device_id=peer, device_id_type=MESH)
    pl.semaphore_wait(barrier, len(peers))


def comm_params(collective_id, mib=48):
    return pltpu.CompilerParams(
        collective_id=collective_id, has_side_effects=True, vmem_limit_bytes=mib << 20
    )


class DpScatter:
    def __init__(self, x, got, acc, far, sems, out=None):
        self.x, self.got, self.acc, self.far = x, got, acc, far
        self.out = x if out is None else out
        self.sems = sems
        d = lax.axis_index("dp")
        n = lax.axis_size("dp") // 2
        self.n = n
        self.y = lax.rem(d, 2)
        self.z = d // 2
        self.order = sorted(range(n), key=lambda m: (m & -m or n, -m))

    def flipped(self, mask):
        z = self.z
        for bit in range(mask.bit_length()):
            if mask >> bit & 1:
                z = z + 2**bit * (1 - 2 * lax.rem(self.z // 2**bit, 2))
        return z

    @staticmethod
    def scratch(n_dp, block):
        n = n_dp // 2
        dma = pltpu.SemaphoreType.DMA
        return [pltpu.VMEM((n,) + block, BF)] * 3 + [dma((4, n))]

    def near_copy(self, k):
        z = self.flipped(self.order[k])
        return pltpu.make_async_remote_copy(
            src_ref=self.out.at[2 * z + 1 - self.y],
            dst_ref=self.got.at[k],
            send_sem=self.sems.at[0, k],
            recv_sem=self.sems.at[1, k],
            device_id={"dp": 2 * self.z + 1 - self.y},
            device_id_type=MESH,
        )

    def far_copy(self, k):
        mask = self.order[k]
        return pltpu.make_async_remote_copy(
            src_ref=self.acc.at[k],
            dst_ref=self.far.at[k],
            send_sem=self.sems.at[2, k],
            recv_sem=self.sems.at[3, k],
            device_id={"dp": 2 * self.flipped(mask & -mask) + self.y},
            device_id_type=MESH,
        )

    def start(self):
        for k in range(self.n):
            self.near_copy(k).start()

    def pair(self, k):
        mask = self.order[k]
        self.near_copy(k).wait()
        z = self.flipped(mask)
        total = self.x[2 * z + self.y].astype(F32) + self.got[k].astype(F32)
        bit = 1
        while mask and bit < mask & -mask:
            other = self.order.index(mask + bit)
            self.far_copy(other).wait()
            total = total + self.far[other].astype(F32)
            bit *= 2
        self.acc[k] = total.astype(BF)
        if mask:
            self.far_copy(k).start()

    def finish(self):
        total = self.acc[self.n - 1].astype(F32)
        bit = 1
        while bit < self.n:
            other = self.order.index(bit)
            self.far_copy(other).wait()
            total = total + self.far[other].astype(F32)
            bit *= 2
        return total


class DpDirect:
    def __init__(self, x, got, acc, far, sems, out=None):
        self.x, self.got, self.acc, self.far = x, got, acc, far
        self.out = x if out is None else out
        self.sems = sems
        d = lax.axis_index("dp")
        n = lax.axis_size("dp") // 2
        self.n = n
        self.y = lax.rem(d, 2)
        self.z = d // 2
        self.order = [lax.rem(self.z + k, n) for k in range(1, n + 1)]

    @staticmethod
    def scratch(n_dp, block):
        n = n_dp // 2
        dma = pltpu.SemaphoreType.DMA
        return [pltpu.VMEM((n,) + block, BF)] * 3 + [dma((4, n))]

    def near_copy(self, k):
        z = self.order[k]
        peer = 2 * self.z + 1 - self.y
        return pltpu.make_async_remote_copy(
            src_ref=self.out.at[2 * z + 1 - self.y],
            dst_ref=self.got.at[z],
            send_sem=self.sems.at[0, k],
            recv_sem=self.sems.at[1, k],
            device_id={"dp": peer},
            device_id_type=MESH,
        )

    def near_arrival(self, k):
        return self.near_copy(k)

    def far_copy(self, k):
        z = self.order[k]
        return pltpu.make_async_remote_copy(
            src_ref=self.acc.at[z],
            dst_ref=self.far.at[k],
            send_sem=self.sems.at[2, k],
            recv_sem=self.sems.at[3, k],
            device_id={"dp": 2 * z + self.y},
            device_id_type=MESH,
        )

    def start(self):
        for k in range(self.n):
            self.near_copy(k).start()

    def pair(self, k):
        z = self.order[k]
        self.near_copy(k).wait()
        self.acc[z] = (self.x[2 * z + self.y].astype(F32) + self.got[z].astype(F32)).astype(BF)
        if k < self.n - 1:
            self.far_copy(k).start()

    def finish(self):
        for k in range(self.n - 1):
            self.far_copy(k).wait()
        total = self.acc[self.z].astype(F32)
        for k in range(self.n - 1):
            total = total + self.far[k].astype(F32)
        return total


class SeqScatter:
    def __init__(self, x, from_sib, to_x, from_x, sems, out=None):
        out = x if out is None else out
        s = lax.axis_index("seq")
        self.s, self.far = s, across_of(s)
        sib = sibling_of(s)
        self.x, self.from_sib, self.to_x, self.from_x = x, from_sib, to_x, from_x
        pair = (sems.at[0], sems.at[1])
        self.first = remote(out.at[across_of(sib)], from_sib.at[0], pair, 0, {"seq": sib})
        self.second = remote(out.at[sib], from_sib.at[1], pair, 1, {"seq": sib})
        self.third = remote(to_x, from_x, pair, 2, {"seq": self.far})

    @staticmethod
    def scratch(rows, width):
        return [
            pltpu.VMEM((2, rows, width), BF),
            pltpu.VMEM((rows, width), BF),
            pltpu.VMEM((rows, width), BF),
            pltpu.SemaphoreType.DMA((2, 3)),
        ]

    def start(self):
        self.first.start()
        self.second.start()

    def cross(self):
        self.first.wait()
        self.to_x[...] = (self.x[self.far].astype(F32) + self.from_sib[0].astype(F32)).astype(BF)
        self.third.start()

    def finish(self):
        self.second.wait()
        self.third.wait()
        return (
            self.x[self.s].astype(F32) + self.from_sib[1].astype(F32) + self.from_x[...].astype(F32)
        )


class SeqSwap:
    def __init__(self, src, dst, sems):
        s = lax.axis_index("seq")
        self.s, self.src, self.dst = s, src, dst
        pair = (sems.at[0], sems.at[1])
        self.copies = [
            remote(src.at[lax.rem(s + k, 4)], dst.at[s], pair, k - 1, {"seq": lax.rem(s + k, 4)})
            for k in (2, 1, 3)
        ]

    def send(self):
        for copy in self.copies:
            copy.start()

    def start(self):
        self.send()
        self.dst[self.s] = self.src[self.s]

    def finish(self):
        for copy in self.copies:
            copy.wait()


def dp_others():
    n = lax.axis_size("dp")
    d = lax.axis_index("dp")
    return [lax.rem(d + k, n) for k in range(1, n)]


def seq_others():
    s = lax.axis_index("seq")
    return [lax.rem(s + k, 4) for k in (1, 2, 3)]


def greet_all():
    greet([{"seq": other} for other in seq_others()] + [{"dp": other} for other in dp_others()])


class Spread:
    def __init__(self, buf, sems):
        d, s = lax.axis_index("dp"), lax.axis_index("seq")
        n = lax.axis_size("dp") // 2
        y, z = lax.rem(d, 2), d // 2
        sib, far = sibling_of(s), across_of(s)
        pair = (sems.at[0], sems.at[1])
        block, column, mine, other = buf.at[s, z, y], buf.at[s, :, y], buf.at[s], buf.at[far]
        self.along_z = [
            remote(block, block, pair, k, {"dp": 2 * lax.rem(z + k + 1, n) + y})
            for k in range(n - 1)
        ]
        self.along_y = remote(column, column, pair, n - 1, {"dp": 2 * z + 1 - y})
        self.along_x = remote(mine, mine, pair, n, {"seq": far})
        self.to_sib = remote(mine, mine, pair, n + 1, {"seq": sib})
        self.forward = remote(other, other, pair, n + 2, {"seq": sib})
        self.place = (s, z, y)

    @staticmethod
    def scratch(n_dp, block):
        n = n_dp // 2
        return [pltpu.VMEM((4, n, 2) + block, BF), pltpu.SemaphoreType.DMA((2, n + 3))]

    def go_z(self):
        for copy in self.along_z:
            copy.start()

    def go_y(self):
        for copy in self.along_z:
            copy.wait()
        self.along_y.start()

    def go_x(self):
        self.along_y.wait()
        self.along_x.start()
        self.to_sib.start()

    def go_sib(self):
        self.along_x.wait()
        self.forward.start()

    def finish(self):
        self.to_sib.wait()
        self.forward.wait()


class SeqReduce:
    def __init__(self, x, total, from_sib, half, from_x, sems):
        s = lax.axis_index("seq")
        self.c = c = lax.rem(s, 2)
        sib, far = sibling_of(s), across_of(s)
        pair = (sems.at[0], sems.at[1])
        self.x, self.total, self.from_sib, self.half, self.from_x = x, total, from_sib, half, from_x
        self.first = remote(x.at[1 - c], from_sib, pair, 0, {"seq": sib})
        self.second = remote(half, from_x, pair, 1, {"seq": far})
        self.third = remote(total.at[c], total.at[c], pair, 2, {"seq": sib})

    @staticmethod
    def scratch(rows, width):
        return (
            [pltpu.VMEM((2, rows, width), F32)] * 2
            + [pltpu.VMEM((rows, width), F32)]
            + [pltpu.VMEM((rows, width), BF)] * 2
            + [pltpu.SemaphoreType.DMA((2, 3))]
        )

    def start(self):
        self.first.start()

    def cross(self):
        self.first.wait()
        self.half[...] = (self.x[self.c] + self.from_sib[...]).astype(BF)
        self.second.start()

    def back(self):
        self.second.wait()
        self.total[self.c] = self.half[...].astype(F32) + self.from_x[...].astype(F32)
        self.third.start()

    def finish(self):
        self.third.wait()


def first_kernel(*refs):
    refs = list(refs)

    def take(count):
        taken = refs[:count]
        del refs[:count]
        return taken

    tok, cot, flag, emb, ada_b, edge = take(6)
    in_weight, out_weight, conv_weight, conv_bias, xproj_weight, ada_weight, a_log = take(7)
    hidden_o, branch_o, xin_o, act_o, slope_o, proj_o, dy_o, silu_o, slope_z_o, mod_o, a2_o, coef_o = take(12)
    w_x, w_z, w_out, conv_w, conv_b, xproj, ada_w, rates, load_sems = take(9)
    toks, cots, flags, rows_out, rows_in = take(5)
    hidden, grad_branch, xin, z, act, slope, dy, silu_z, slope_z, pad = take(10)
    tok_sems, cot_sems, flag_sems, row_sems, own_sems, store_sems = take(6)
    c3 = SeqReduce(*take(6))
    d, s = lax.axis_index("dp"), lax.axis_index("seq")
    sib, far = sibling_of(s), across_of(s)
    diag = across_of(sib)
    n_dp = lax.axis_size("dp")
    seg, width = tok.shape
    total, chans = xin.shape

    own = pl.ds(pl.multiple_of(s * chans, 128), chans)
    own_z = pl.ds(pl.multiple_of((4 + s) * chans, 128), chans)
    loads = [
        (ada_weight, ada_w),
        (a_log.at[:, :, own], rates),
        (in_weight.at[:, own], w_x),
        (in_weight.at[:, own_z], w_z),
        (conv_weight.at[:, :, own], conv_w),
        (conv_bias.at[:, own], conv_b),
        (xproj_weight.at[:, own], xproj),
        (out_weight.at[own], w_out),
    ]
    loads = [pltpu.make_async_copy(a, b, load_sems.at[i]) for i, (a, b) in enumerate(loads)]
    for copy in loads:
        copy.start()
    greet_all()

    def spread_out(src, dst, sems):
        pair = (sems.at[0], sems.at[1])
        to_far = remote(src, dst.at[s], pair, 0, {"seq": far})
        to_sib = remote(src, dst.at[s], pair, 1, {"seq": sib})
        forward = remote(dst.at[far], dst.at[far], pair, 2, {"seq": sib})
        return to_far, to_sib, forward

    tok_far, tok_sib, tok_forward = spread_out(tok, toks, tok_sems)
    cot_far, cot_sib, cot_forward = spread_out(cot, cots, cot_sems)
    tok_far.start()
    tok_sib.start()
    pair = (flag_sems.at[0], flag_sems.at[1])
    flag_copies = [
        remote(flag, flags.at[s], pair, k, {"seq": other}) for k, other in enumerate(seq_others())
    ]
    for copy in flag_copies:
        copy.start()
    locals_ = [(tok, toks.at[s]), (cot, cots.at[s]), (flag, flags.at[s])]
    locals_ = [pltpu.make_async_copy(a, b, own_sems.at[i]) for i, (a, b) in enumerate(locals_)]
    for copy in locals_:
        copy.start()

    loads[0].wait()
    part = dot_nt(emb[...], ada_w[...]) + ada_b[...]
    columns = part.shape[1]
    for i in range(n_dp):
        rows_out[i] = part[i : i + 1]
    pair = (row_sems.at[0], row_sems.at[1])
    row_copies = [
        remote(rows_out.at[other], rows_in.at[d], pair, k, {"dp": other})
        for k, other in enumerate(dp_others())
    ]
    for copy in row_copies:
        copy.start()
    cot_far.start()
    cot_sib.start()
    rows_in[d] = rows_out[d]
    loads[1].wait()
    for k in range(2):
        a2_o[k] = -LOG2E * jnp.exp(rates[k])
    for copy in row_copies:
        copy.wait()
    for i in range(n_dp):
        mod_o[:, i * columns : (i + 1) * columns] = rows_in[i]
    for copy in flag_copies:
        copy.wait()
    for copy in locals_:
        copy.wait()
    for copy in loads[2:4]:
        copy.wait()

    def project(block):
        at = pl.ds(pl.multiple_of(block * seg, seg), seg)
        tokens = toks[block].astype(F32)
        centred = tokens - jnp.mean(tokens, axis=1, keepdims=True)
        normed = centred * lax.rsqrt(jnp.mean(centred * centred, axis=1, keepdims=True) + epsilon)
        marks = flags[block].T[:, :1]
        hid = normed * (1.0 + mod_o[:, width : 2 * width]) + mod_o[:, :width] + marks * edge[...]
        hid = hid.astype(BF)
        hidden[at, :] = hid
        xin[at, :] = dot(hid, w_x[...]).astype(BF)
        z[at, :] = dot(hid, w_z[...])

    project(s)
    tok_sib.wait()
    project(sib)
    tok_far.wait()
    tok_forward.start()
    project(far)
    tok_forward.wait()
    project(diag)

    stores = [
        (hidden, hidden_o), (xin, xin_o), (act, act_o), (slope, slope_o), (c3.total, proj_o),
        (grad_branch, branch_o), (dy, dy_o), (silu_z, silu_o), (slope_z, slope_z_o),
    ]
    stores = [pltpu.make_async_copy(a, b, store_sems.at[i]) for i, (a, b) in enumerate(stores)]
    stores[0].start()
    stores[1].start()
    pad[:16, :] = jnp.zeros((16, chans), F32)
    pad[total + 16 :, :] = jnp.zeros((16, chans), F32)
    pad[16 : total + 16, :] = xin[...].astype(F32)
    for copy in loads[4:]:
        copy.wait()
    step = 64

    def chunk(c, carry):
        base = pl.multiple_of(c * step, step)
        window = pad[pl.ds(base, step + 32), :]
        here = pl.ds(base, step)
        for k in range(2):
            value = conv_b[k : k + 1, :]
            for tap in range(4):
                first = 13 + tap if k == 0 else 19 - tap
                value = value + conv_w[k, tap : tap + 1, :] * window[first : first + step]
            sig = jax.nn.sigmoid(value)
            acted = (value * sig).astype(BF)
            act[k, here, :] = acted
            slope[k, here, :] = (sig * (1.0 + value * (1.0 - sig))).astype(BF)
            c3.x[k, here, :] = dot(acted, xproj[k])
        return carry

    lax.fori_loop(0, total // step, chunk, 0)
    c3.start()
    stores[2].start()
    stores[3].start()

    def gate_back(block):
        at = pl.ds(pl.multiple_of(block * seg, seg), seg)
        grad = (cots[block].astype(F32) * mod_o[:, 2 * width :]).astype(BF)
        grad_branch[at, :] = grad
        grad_gated = dot_nt(grad, w_out[...])
        value = z[at, :]
        sigma = jax.nn.sigmoid(value)
        silu_z[at, :] = value * sigma
        dy[at, :] = grad_gated * (value * sigma)
        slope_z[at, :] = grad_gated * (sigma * (1.0 + value * (1.0 - sigma)))

    cot_far.wait()
    cot_forward.start()
    gate_back(s)
    c3.cross()
    cot_sib.wait()
    gate_back(sib)
    gate_back(far)
    cot_forward.wait()
    gate_back(diag)
    for copy in stores[5:]:
        copy.start()
    c3.back()
    c3.finish()
    stores[4].start()
    for k in range(2):
        for t in range(total // 128):
            square = c3.total[k, t * 128 : (t + 1) * 128].T
            for g in range(128 // U):
                coef_o[k, t * (128 // U) + g] = square[128 - 2 * STATE :, g * U : (g + 1) * U]
    for copy in stores:
        copy.wait()


def first_part(
    tok, cot, flag, emb, ada_b, edge, in_weight, out_weight, conv_weight, conv_bias, xproj_weight,
    ada_w, a_log, collective_id,
):
    seg, width = tok.shape
    total = 4 * seg
    chans = out_weight.shape[0] // 4
    n_dp = emb.shape[0]
    columns = ada_w.shape[0]
    any_spec = pl.BlockSpec(memory_space=pl.ANY)
    shape = jax.ShapeDtypeStruct
    out_shape = [
        shape((total, width), BF),
        shape((total, width), BF),
        shape((total, chans), BF),
        shape((2, total, chans), BF),
        shape((2, total, chans), BF),
        shape((2, total, 128), F32),
        shape((total, chans), F32),
        shape((total, chans), F32),
        shape((total, chans), F32),
        shape((1, 3 * width), F32),
        shape((2, STATE, chans), F32),
        shape((2, total // U, 2 * STATE, U), F32),
    ]
    dma = pltpu.SemaphoreType.DMA
    vmem = pltpu.VMEM
    scratch = [
        vmem((width, chans), BF),
        vmem((width, chans), BF),
        vmem((chans, width), BF),
        vmem((2, 4, chans), F32),
        vmem((2, chans), F32),
        vmem((2, chans, 128), BF),
        vmem(ada_w.shape, BF),
        vmem((2, STATE, chans), F32),
        dma((8,)),
        vmem((4, seg, width), BF),
        vmem((4, seg, width), BF),
        vmem((4, 8, 128), F32),
        vmem((n_dp, 1, columns), F32),
        vmem((n_dp, 1, columns), F32),
        vmem((total, width), BF),
        vmem((total, width), BF),
        vmem((total, chans), BF),
        vmem((total, chans), F32),
        vmem((2, total, chans), BF),
        vmem((2, total, chans), BF),
    ]
    scratch += [vmem((total, chans), F32)] * 3 + [vmem((total + 32, chans), F32)]
    scratch += [dma((2, 3)), dma((2, 3)), dma((2, 3)), dma((2, n_dp)), dma((3,)), dma((9,))]
    scratch += SeqReduce.scratch(total, 128)
    return pl.pallas_call(
        first_kernel,
        in_specs=[VMEM_SPEC] * 6 + [any_spec] * 7,
        out_specs=[any_spec] * 9 + [VMEM_SPEC] * 3,
        out_shape=out_shape,
        scratch_shapes=scratch,
        compiler_params=comm_params(collective_id, 60),
        name="first_part",
    )(
        tok, cot, flag, emb, ada_b, edge, in_weight, out_weight, conv_weight, conv_bias, xproj_weight,
        ada_w, a_log,
    )


def rows_in_eights(x):
    total = x[:8]
    for k in range(1, x.shape[0] // 8):
        total = total + x[8 * k : 8 * k + 8]
    return total


def backward_kernel(*refs):
    refs = list(refs)

    def take(count):
        taken = refs[:count]
        del refs[:count]
        return taken

    (dl, hp, proj, act, coef, a2, dy, dread) = take(8)
    (tok, cot, gate, scale, flags) = take(5)
    far_inputs = take(13)
    dt_weight, conv_weight, skip_all = far_inputs[6:9]
    in_weight, xproj_weight = far_inputs[4:6]
    (result, tokg, in_ref, out_ref, a_ref, x0_ref, x1_ref, convw_ref, convb_ref, table_ref) = take(10)
    g_sc, g_a, g_b, q_a, q_b, r0, r1, r2, red = take(9)
    dpre, dc, dflow, dalog, sums = take(5)
    slope, xpad, hidden, grad_z, w_x, w_z, xproj, dtw, conv_w, skip, hid_in, out_in, xs_in, local_sems = take(14)
    conv_acc, dxin, gate_row = take(3)
    seq1 = SeqScatter(hid_in, *take(4), out=far_inputs[9])
    outs = DpScatter(out_in, *take(4))
    zs = DpScatter(xs_in, *take(4), out=far_inputs[11])
    gates, gate_sems = take(2)
    g_swap = SeqSwap(far_inputs[10], gates, gate_sems)
    z_red, z_got, z_swap_sems = take(3)
    z_swap = SeqSwap(z_red, z_got, z_swap_sems)
    c7 = SeqReduce(*take(6))
    smalls = []
    for _ in range(5):
        source = take(1)[0]
        scatter = DpDirect(source, *take(4))
        buf, sems = take(2)
        smalls.append((source, scatter, buf, Spread(buf, sems)))
    parts_a, parts_x, part_c = smalls[:2], smalls[2:4], smalls[4]
    seq2 = SeqScatter(hid_in, *take(4))
    xs = DpScatter(xs_in, *take(4))
    x_red, x_got, x_swap_sems = take(3)
    x_swap = SeqSwap(x_red, x_got, x_swap_sems)
    row, rows_in, row_sems, table, table_sems, result_sems, conv_all = take(7)

    j = pl.program_id(0)
    blocks = pl.num_programs(0) // 2
    length = dl.shape[1]
    total = blocks * length
    chans = dl.shape[2]
    width = tok.shape[1]
    n = outs.n
    n_dp = 2 * n
    d_index, s_index = lax.axis_index("dp"), lax.axis_index("seq")
    rows_x = chans // n_dp

    def loads():
        own = pl.ds(pl.multiple_of(s_index * chans, 128), chans)
        own_z = pl.ds(pl.multiple_of((4 + s_index) * chans, 128), chans)
        pairs = [
            (far_inputs[0], slope),
            (far_inputs[1], xpad.at[pl.ds(16, total)]),
            (far_inputs[12], hidden),
            (far_inputs[3], grad_z),
            (in_weight.at[:, own], w_x),
            (in_weight.at[:, own_z], w_z),
            (xproj_weight.at[:, own], xproj),
            (dt_weight.at[:, :, own], dtw.at[:, pl.ds(0, dt_weight.shape[1])]),
            (conv_weight.at[:, :, own], conv_w),
            (far_inputs[9], hid_in),
            (far_inputs[10].at[s_index], gates.at[s_index]),
            (far_inputs[11], xs_in),
            (skip_all.at[:, own], skip),
            (far_inputs[2], hidden),
        ]
        return [pltpu.make_async_copy(a, b, local_sems.at[i]) for i, (a, b) in enumerate(pairs)]

    def results():
        pairs = []
        for d in range(2):
            buf = parts_a[d][2]
            pairs += [(buf.at[q], a_ref.at[d, :, :, :, pl.ds(q * chans, chans)]) for q in range(4)]
        pairs += [(parts_x[0][2], x0_ref), (parts_x[1][2], x1_ref)]
        return [pltpu.make_async_copy(a, b, result_sems.at[i]) for i, (a, b) in enumerate(pairs)]

    near = [(zs, k) for k in range(n)] + [(outs, k) for k in range(n)]
    pair_at = [2, 4, 5, 7, 8, 8, 8, 8]

    def step_of(i):
        return pair_at[i * 8 // (2 * n)]

    unit = 2 * blocks // 8

    @pl.when(j == 0)
    def _():
        greet_all()
        g_swap.send()
        seq1.start()
        zs.start()
        for copy in loads()[:13]:
            copy.start()
        loads()[12].wait()
        for d in range(2):
            dc[d, :16, :] = jnp.zeros((16, chans), F32)
            dc[d, total + 16 :, :] = jnp.zeros((16, chans), F32)
        xpad[:16, :] = jnp.zeros((16, chans), BF)
        xpad[total + 16 :, :] = jnp.zeros((16, chans), BF)
        dtw[:, dt_weight.shape[1] :, :] = jnp.zeros((2, 128 - dt_weight.shape[1], chans), BF)
        dalog[...] = jnp.zeros_like(dalog)
        sums[...] = jnp.zeros_like(sums)
        conv_acc[...] = jnp.zeros_like(conv_acc)

    @pl.when(j == 2 * unit)
    def _():
        for copy in loads()[9:12]:
            copy.wait()
        seq1.cross()

    @pl.when(j == 3 * unit)
    def _():
        g_swap.finish()
        loads()[2].wait()
        for q in range(4):
            grad = dot_tn(gates[q], hidden[...]).astype(BF)
            for b in range(n_dp // 4):
                out_in[n_dp // 4 * q + b] = grad[b * rows_x : (b + 1) * rows_x]
        outs.start()
        loads()[13].start()

    for i, (scatter, k) in enumerate(near):
        if step_of(i) < 8:
            pl.when(j == unit * step_of(i))(functools.partial(scatter.pair, k))


    @pl.when(j == 5 * unit)
    def _():
        branch = seq1.finish()
        result[...] = (tok[...].astype(F32) + gate[...] * branch).astype(BF)
        gate_row[...] = jnp.sum(cot[...].astype(F32) * branch, axis=0, keepdims=True)

    @pl.when(lax.rem(j, blocks) == 0)
    def _():
        g_sc[...] = jnp.zeros_like(g_sc)

    def run(rev):
        d = int(rev)
        block = j - blocks if rev else blocks - 1 - j
        base = pl.multiple_of(block * length, length)
        here = pl.ds(base, length)
        backward_block(
            rev, dl.at[0], act.at[d, here], coef.at[0], a2.at[d],
            proj.at[d, here], dy.at[here], skip.at[pl.ds(d, 1)], hp.at[0], dpre.at[d, here],
            dc.at[d, pl.ds(pl.multiple_of(base + 16, 16), length)], dflow.at[d, block], dalog.at[d],
            sums.at[d], g_sc, ((g_a, q_a), (g_b, q_b)), (r0, r1, r2), red,
        )

    pl.when(j < blocks)(lambda: run(False))
    pl.when(j >= blocks)(lambda: run(True))

    @pl.when(j == 2 * blocks - 1)
    def _():
        late = [near[i] for i in range(2 * n) if step_of(i) >= 8]

        def pairs():
            for _ in range(len(late) // 4):
                scatter, k = late[pairs.done]
                pairs.done += 1
                scatter.pair(k)

        pairs.done = 0
        for i in (0, 1, 3, 4, 5, 6, 7, 8, 13):
            loads()[i].wait()
        for d in range(2):
            value = dot_nt(dpre[d], dtw[d])
            for b in range(blocks):
                at = slice(b * length, (b + 1) * length)
                square = jnp.concatenate(
                    [jnp.zeros((128 - 2 * STATE, length), F32), dflow[d, b], dread[d, b]], axis=0
                )
                c7.x[d, at] = value[at] + square.T
        c7.start()
        rank = 128 - 2 * STATE
        per_d = 128 // n_dp
        for d in range(2):
            source, scatter, _, _ = parts_a[d]
            lines = dot_tn(proj[d].astype(BF), dpre[d])[:rank]
            extra = [jnp.sum(sums[d, i], axis=0, keepdims=True) for i in range(2)]
            lines = jnp.concatenate(
                [lines, dalog[d] * (a2[d] * LN2)] + extra + [jnp.zeros((STATE - 2, chans), F32)], axis=0
            ).astype(BF)
            for b in range(n_dp):
                source[b] = lines[b * per_d : (b + 1) * per_d]
            scatter.start()
        c7.cross()
        pairs()
        z_red[...] = zs.finish().astype(BF)
        z_swap.start()
        c7.back()
        pairs()
        c7.finish()

        for d in range(2):
            dproj = c7.total[d].astype(BF)
            source, scatter, _, _ = parts_x[d]
            grad = dot_tn(act[d], dproj).astype(BF)
            for b in range(n_dp):
                source[b] = grad[b * rows_x : (b + 1) * rows_x]
            scatter.start()

            def act_rows(c, carry, d=d):
                at = pl.ds(pl.multiple_of(c * 128, 128), 128)
                shifted = pl.ds(pl.multiple_of(c * 128 + 16, 16), 128)
                value = dot_nt(c7.total[d, at].astype(BF), xproj[d]) + dc[d, shifted]
                dc[d, shifted] = value * slope[d, at].astype(F32)
                return carry

            lax.fori_loop(0, total // 128, act_rows, 0)
        pairs()
        step = 32

        def conv_rows(c, carry):
            base = pl.multiple_of(c * step, step)
            window = pl.ds(base, step + 32)
            x_w = xpad[window, :].astype(F32)
            grad = jnp.zeros((step, chans), F32)
            for d in range(2):
                d_w = dc[d, window]
                here = d_w[16 : 16 + step]
                conv_acc[5 * d + 4] += rows_in_eights(here)
                for tap in range(4):
                    off = tap - 3 if d == 0 else 3 - tap
                    conv_acc[5 * d + tap] += rows_in_eights(here * x_w[16 + off : 16 + off + step])
                    grad = grad + conv_w[d, tap : tap + 1] * d_w[16 - off : 16 - off + step]
            dxin[pl.ds(base, step), :] = grad.astype(BF)
            return carry

        lax.fori_loop(0, total // step, conv_rows, 0)
        source, scatter, _, _ = part_c
        conv_lines = [jnp.sum(conv_acc[i], axis=0, keepdims=True) for i in range(10)]
        conv_lines = jnp.concatenate(conv_lines + [jnp.zeros((6, chans), F32)], axis=0)
        for b in range(n_dp):
            source[b, :, :rows_x] = conv_lines[:, b * rows_x : (b + 1) * rows_x].astype(BF)
            source[b, :, rows_x:] = jnp.zeros((16, 128 - rows_x), BF)
        scatter.start()
        pairs()

        rb = width // (4 * n_dp)
        half = n_dp // 2
        for h in range(2):
            cols = slice(h * width // 2, (h + 1) * width // 2)
            grad = dot_tn(hidden[:, cols], dxin[...]).astype(BF)
            for b in range(half):
                for q in range(4):
                    first = (4 * b + q) * rb
                    xs_in[h * half + b, q] = grad[first : first + rb]
        xs.start()
        for _, scatter, _, _ in parts_a:
            for k in range(n):
                scatter.pair(k)
        seg = tok.shape[0]
        for h in range(2):
            cols = slice(h * width // 2, (h + 1) * width // 2)
            grad = (dot_nt(dxin[...], w_x[cols, :]) + dot_nt(grad_z[...], w_z[cols, :])).astype(BF)
            for q in range(4):
                hid_in[q, :, cols] = grad[q * seg : (q + 1) * seg]
        seq2.start()
        for _, scatter, _, _ in parts_x + [part_c]:
            for k in range(n):
                scatter.pair(k)
        seq2.cross()
        for k in range(n // 4):
            xs.pair(k)

        def gathered(parts):
            for _, scatter, buf, spread in parts:
                buf[spread.place] = scatter.finish().astype(BF)
                spread.go_z()

        gathered(parts_a)
        gathered(parts_x + [part_c])
        out_ref[...] = outs.finish().astype(BF)
        for k in range(n // 4, n // 2):
            xs.pair(k)

        grad = seq2.finish()
        tokens = tok[...].astype(F32)
        centred = tokens - jnp.mean(tokens, axis=1, keepdims=True)
        inv_std = lax.rsqrt(jnp.mean(centred * centred, axis=1, keepdims=True) + epsilon)
        normed = centred * inv_std
        row[:, :width] = jnp.sum(grad, axis=0, keepdims=True)
        row[:, width : 2 * width] = jnp.sum(grad * normed, axis=0, keepdims=True)
        row[:, 2 * width : 3 * width] = gate_row[...]
        row[:, 3 * width :] = jnp.sum(grad * flags[...], axis=0, keepdims=True)
        pair = (row_sems.at[0], row_sems.at[1])
        row_copies = [
            remote(row, rows_in.at[k], pair, k, {"seq": other})
            for k, other in enumerate(seq_others())
        ]
        for copy in row_copies:
            copy.start()
        grad_normed = grad * (1.0 + scale[...])
        inner_product = jnp.mean(grad_normed * normed, axis=1, keepdims=True)
        tokg[...] = (
            cot[...].astype(F32)
            + inv_std
            * (grad_normed - jnp.mean(grad_normed, axis=1, keepdims=True) - normed * inner_product)
        ).astype(BF)
        spreads = [item[3] for item in parts_a + parts_x + [part_c]]
        for spread in spreads:
            spread.go_y()
        for k in range(n // 2, 3 * n // 4):
            xs.pair(k)
        for copy in row_copies:
            copy.wait()
        table[d_index] = row[...] + rows_in[1] + (rows_in[0] + rows_in[2])
        pair = (table_sems.at[0], table_sems.at[1])
        table_copies = [
            remote(table.at[d_index], table.at[d_index], pair, k, {"dp": other})
            for k, other in enumerate(dp_others())
        ]
        for copy in table_copies:
            copy.start()
        for k in range(3 * n // 4, n):
            xs.pair(k)
        for spread in spreads:
            spread.go_x()
        x_red[...] = xs.finish().astype(BF)
        x_swap.start()
        z_swap.finish()
        for q in range(4):
            in_ref[:, (4 + q) * chans : (5 + q) * chans] = z_got[q]
        for copy in table_copies:
            copy.wait()
        table_ref[...] = table[...]
        for spread in spreads:
            spread.go_sib()
        x_swap.finish()
        for q in range(4):
            in_ref[:, q * chans : (q + 1) * chans] = x_got[q]
        for spread in spreads:
            spread.finish()
        for copy in results():
            copy.start()
        for b in range(4 * n_dp):
            q, place = b // n_dp, b % n_dp
            piece = part_c[2][q, place // 2, place % 2][:, :rows_x].astype(F32)
            conv_all[:, b * rows_x : (b + 1) * rows_x] = piece
        for d in range(2):
            convw_ref[d] = conv_all[5 * d : 5 * d + 4]
            convb_ref[d : d + 1] = conv_all[5 * d + 4 : 5 * d + 5]
        for copy in results():
            copy.wait()


def scan_backward(
    dl, hp, proj, act, coef, a2, dy, dread, branch, sorted_gated, grad_branch, z_part,
    tok, cot, gate, scale, flags, slope, xin, hidden, grad_z, in_weight, xproj_weight, dt_weight, conv_weight, skip,
    collective_id, tile,
):
    total, chans = dy.shape
    blocks = total // tile
    n_dp = z_part.shape[0]
    n = n_dp // 2
    rows, width = tok.shape
    rb = width // (4 * n_dp)
    rows_x = chans // n_dp
    per_d = 128 // n_dp
    out_block = (rows_x, width)

    def place(j):
        d = j // blocks
        b = lax.rem(j, blocks)
        return d, blocks - 1 - b + d * (2 * b - blocks + 1)

    def tokens_of(j):
        d, b = place(j)
        return d, b, 0

    def cells(j):
        d, b = place(j)
        return d, b, 0, 0

    any_spec = pl.BlockSpec(memory_space=pl.ANY)
    in_specs = (
        [
            pl.BlockSpec((1, tile, chans), tokens_of),
            pl.BlockSpec((1, tile * STATE, chans), tokens_of),
        ]
        + [VMEM_SPEC] * 2
        + [pl.BlockSpec((1, tile // U, 2 * STATE, U), cells)]
        + [VMEM_SPEC] * 8
        + [any_spec] * 13
    )
    shape = jax.ShapeDtypeStruct
    in_out = (4, n, 2)
    out_shape = [
        shape((rows, width), BF),
        shape((rows, width), BF),
        shape((rb, 8 * chans), BF),
        shape(out_block, BF),
        shape((2, n, 2, per_d, 4 * chans), BF),
        shape(in_out + (rows_x, 128), BF),
        shape(in_out + (rows_x, 128), BF),
        shape((2, 4, 4 * chans), F32),
        shape((2, 4 * chans), F32),
        shape((n_dp, 1, 4 * width), F32),
    ]
    dma = pltpu.SemaphoreType.DMA
    vmem = pltpu.VMEM
    scratch = [
        vmem((STATE, chans), F32),
        vmem((U * STATE, chans), BF),
        vmem((U * STATE, chans), BF),
        vmem((U * 8, chans), BF),
        vmem((U * 8, chans), BF),
    ]
    scratch += [vmem((U, chans), F32)] * 3 + [vmem((U, STATE, 128), F32)]
    scratch += [
        vmem((2, total, chans), BF),
        vmem((2, total + 32, chans), F32),
        vmem((2, blocks, STATE, tile), F32),
        vmem((2, STATE, chans), F32),
        vmem((2, 2, U, chans), F32),
    ]
    scratch += [
        vmem(slope.shape, BF),
        vmem((total + 32, chans), BF),
        vmem(hidden.shape, BF),
        vmem(grad_z.shape, BF),
        vmem((width, chans), BF),
        vmem((width, chans), BF),
        vmem((2, chans, 128), BF),
        vmem((2, 128, chans), BF),
        vmem((2, 4, chans), F32),
        vmem((2, chans), F32),
        vmem((4, rows, width), BF),
        vmem((n_dp,) + out_block, BF),
        vmem(z_part.shape, BF),
        dma((14,)),
    ]
    scratch += [
        vmem((10, 8, chans), F32),
        vmem((total, chans), BF),
        vmem((1, width), F32),
    ]
    scratch += SeqScatter.scratch(rows, width)
    scratch += DpScatter.scratch(n_dp, out_block) + DpScatter.scratch(n_dp, z_part.shape[1:])
    scratch += [vmem(sorted_gated.shape, BF), dma((2, 3))]
    scratch += [vmem(z_part.shape[1:], BF)] * 2 + [dma((2, 3))]
    scratch += SeqReduce.scratch(total, 128)
    for block in [(per_d, chans)] * 2 + [(rows_x, 128)] * 2 + [(16, 128)]:
        scratch += [vmem((n_dp,) + block, BF)] + DpScatter.scratch(n_dp, block)
        scratch += Spread.scratch(n_dp, block)
    scratch += SeqScatter.scratch(rows, width)
    scratch += DpScatter.scratch(n_dp, z_part.shape[1:])
    scratch += [vmem(z_part.shape[1:], BF)] * 2 + [dma((2, 3))]
    scratch += [
        vmem((1, 4 * width), F32),
        vmem((3, 1, 4 * width), F32),
        dma((2, 3)),
        vmem((n_dp, 1, 4 * width), F32),
        dma((2, n_dp)),
        dma((10,)),
        vmem((16, 4 * chans), F32),
    ]
    return pl.pallas_call(
        backward_kernel,
        grid=(2 * blocks,),
        in_specs=in_specs,
        out_specs=[VMEM_SPEC] * 4 + [any_spec] * 3 + [VMEM_SPEC] * 3,
        out_shape=out_shape,
        scratch_shapes=scratch,
        compiler_params=comm_params(collective_id, 62),
        name="scan_backward",
    )(
        dl, hp, proj, act, coef, a2, dy, dread, tok, cot, gate, scale, flags, slope, xin, hidden,
        grad_z, in_weight, xproj_weight, dt_weight, conv_weight, skip, branch,
        sorted_gated, z_part, grad_branch,
    )


def time_embedding(step_ids, model_width):
    halfway = model_width // 2
    frequency = jnp.exp(-math.log(10000.0) * jnp.arange(halfway, dtype=jnp.float32) / halfway)
    angles = step_ids.astype(jnp.float32)[:, None] * frequency[None, :]
    return jnp.concatenate([jnp.cos(angles), jnp.sin(angles)], axis=1)


def silu_slope(values):
    sigma = jax.nn.sigmoid(values)
    return sigma * (1.0 + values * (1.0 - sigma))


def shards(
    tokens,
    cotangent,
    timesteps,
    grid_widths,
    scan_path,
    ada_weight,
    ada_bias,
    edge,
    in_weight,
    conv_weight,
    conv_bias,
    xproj_weight,
    dt_weight,
    dt_bias,
    a_log,
    skip,
    out_weight,
):
    seg_len, width = tokens.shape[1:]
    inner = in_weight.shape[1] // 2
    rank = dt_weight.shape[1]
    taps = conv_weight.shape[1]
    rim = taps - 1
    columns = ada_weight.shape[1]
    n_seq = lax.axis_size("seq")
    n_dp = lax.axis_size("dp")
    dp_index = lax.axis_index("dp")
    seq_index = lax.axis_index("seq")
    length = seg_len * n_seq
    chans = inner // n_seq

    def flags_of(item):
        return (jnp.remainder(item, grid_widths[0]) == grid_widths[0] - 1).astype(F32)

    embedded = jax.nn.silu(time_embedding(timesteps, width)).astype(BF)
    own_flags = flags_of(scan_path)
    hidden, grad_branch, xin, act, slope, proj, dy, silu_z, slope_z, modulation, decay2, coef = first_part(
        tokens[0], cotangent[0], jnp.broadcast_to(own_flags, (8, seg_len)), embedded, ada_bias[None],
        edge[None], in_weight, out_weight, conv_weight, conv_bias, xproj_weight, ada_weight.T,
        jnp.swapaxes(a_log, 1, 2), 0,
    )
    scale_term = modulation[:, width : 2 * width]
    gate_term = modulation[:, 2 * width :]
    tile = 128 if n_dp <= 8 else 32
    held, delta, dread, branch, sorted_gated, z_part, grad_z = scan_forward(
        seq_index.astype(jnp.int32)[None], proj, act, coef, dt_weight, dt_bias, decay2,
        skip, dy, silu_z, slope_z, hidden, out_weight, tile,
    )
    total = n_dp * n_seq

    def in_blocks(grad):
        return grad.reshape(n_dp, n_seq, width // total, chans)

    result, grad_tok, in_rows, out_rows, lines, x0, x1, convw_grad, convb_grad, table = scan_backward(
        delta, held, proj, act, coef, decay2, dy, dread,
        branch.reshape(n_seq, seg_len, width),
        sorted_gated,
        grad_branch,
        in_blocks(z_part),
        tokens[0], cotangent[0], gate_term, scale_term, own_flags[0][:, None],
        slope, xin, hidden, grad_z, in_weight, xproj_weight, dt_weight, conv_weight, skip,
        2, tile,
    )
    table = table.reshape(n_dp, -1)
    edge_grad = jnp.sum(table[:, 3 * width :], axis=0)
    mod_columns = lax.dynamic_slice_in_dim(table[:, : 3 * width], dp_index * columns, columns, 1)
    ada_b_grad = jnp.sum(mod_columns, axis=0)
    ada_w_grad = jnp.dot(embedded.astype(F32).T, mod_columns, precision=highest)
    lines = lines.reshape(2, 128, inner).astype(F32)
    alog_grad = jnp.swapaxes(lines[:, rank : rank + STATE], 1, 2)
    xproj_grad = jnp.stack([item.reshape(inner, 128) for item in (x0, x1)]).astype(F32)
    return (
        result[None],
        grad_tok[None],
        ada_w_grad,
        ada_b_grad,
        edge_grad,
        in_rows.astype(F32),
        convw_grad,
        convb_grad,
        xproj_grad,
        lines[:, :rank],
        lines[:, rank + STATE],
        alog_grad,
        lines[:, rank + STATE + 1],
        out_rows.astype(F32),
    )


def solution(mesh):
    in_specs = (
        P("dp", "seq", None),
        P("dp", "seq", None),
        P(),
        P("dp"),
        P("dp", "seq"),
        P(None, "dp"),
        P("dp"),
        P(),
        P(),
        P(),
        P(),
        P(),
        P(),
        P(),
        P(),
        P(),
        P(),
    )
    out_specs = (
        P("dp", "seq", None),
        P("dp", "seq", None),
        P(None, "dp"),
        P("dp"),
        P(),
        P(("dp", "seq"), None),
        P(),
        P(),
        P(),
        P(),
        P(),
        P(),
        P(),
        P(("dp", "seq"), None),
    )
    return jax.shard_map(shards, mesh=mesh, in_specs=in_specs, out_specs=out_specs, check_vma=False)
```
